32 devices in a mesh: queue: 8 (over z, core), tensor: 4 (over y, x).
Axes of the slice: x: 2, y: 2, z: 4, core: 2. Of those that a mesh axis runs over, the one named last changes fastest.
Arguments:
- latents: bfloat16 [8, 768, 3072], P('queue'), may hold values from -6 to 6
- levels: int32 [8], P('queue'), may hold values from 0 to 49
- mod_table: bfloat16 [50, 9216], replicated, may hold values from -3 to 3
- step_size: float32 [50], replicated, may hold values from 0.2 to 1
- qkv_weight: bfloat16 [3, 3072, 3072], P(None, None, 'tensor'), may hold values from -0.109375 to 0.109375
- q_gain: float32 [128], replicated, may hold values from 0.8 to 4, as said below
- k_gain: float32 [128], replicated, may hold values from 0.8 to 4, as said below
- out_weight: bfloat16 [3072, 3072], P('tensor'), may hold values from -0.109375 to 0.109375
- fresh_noise: bfloat16 [2, 768, 3072], P(None, 'tensor'), may hold values from -6 to 6
Outputs:
- queue_out: bfloat16 [8, 768, 3072], P('queue')
The draws below stay inside these ranges and needn't reach their ends.
Inputs may be any that keep to these rules, and one draw needn't show every extreme that they name: `q_gain`: positive gains. `k_gain`: positive gains.
All inputs are finite; a program needn't handle non-finite values.
Results may differ from the reference program's by a relative error of at most 0.03.
Values may be sent and summed in bfloat16 or wider, within the bound.
No kernel may reach another device: no remote copies, remote signals or barrier semaphores. Data moves between devices by JAX's collectives and lax.ppermute only.
A program may use at most 128 MiB of HBM per device.

```python
import math
import jax
import jax.numpy as jnp
from jax import lax

D = 3072
HEADS = 24
HD = 128
FT = 768
LEVELS = 50
STEPS = 2
FRAMES = 8
N_TENSOR = 4


def draw_q_gain(key, part):
    key = jax.random.fold_in(key, 11)
    return jax.random.uniform(key, (HD,), jnp.float32, 0.8, 2.0)


def draw_k_gain(key, part):
    key = jax.random.fold_in(key, 23)
    return jax.random.uniform(key, (HD,), jnp.float32, 0.8, 2.0)


def plant(array, key, smallest, top_value):
    index_at = [jax.random.randint(jax.random.fold_in(key, axis), (), 0, length) for axis, length in enumerate(array.shape)]
    widest = array.shape.index(max(array.shape))
    beside = index_at[:widest] + [(index_at[widest] + 1) % array.shape[widest]] + index_at[widest + 1:]
    return array.at[tuple(index_at)].set(smallest).at[tuple(beside)].set(top_value)


def block_scale(own_key, shape, split, smallest, high):
    gain = 1.0
    for position, parts in split:
        steps = jax.random.uniform(jax.random.fold_in(jax.random.fold_in(own_key, 6), position), (parts,), jnp.float32, smallest / len(split), high / len(split))
        gain = gain * jnp.repeat(jnp.exp(steps), shape[position] // parts).reshape((-1,) + (1,) * (len(shape) - 1 - position))
    return gain


def gaussian(stream_key, shape, deviation, most, shards=(), held_as=jnp.bfloat16):
    values = jax.random.normal(stream_key, shape, jnp.float32) * deviation
    if len(shards) > 0:
        values = block_scale(stream_key, shape, shards, -0.22, 0.18) * values
    return jnp.clip(values, min=-most, max=most).astype(held_as)


def setup_inputs(seed: int = 0) -> dict:
    splits = jax.random.split(jax.random.key(seed), 10)
    latents = gaussian(splits[0], (FRAMES, FT, D), 1.0, 6.0, ((0, 8),))
    levels = plant(jax.random.randint(splits[1], (FRAMES,), 0, LEVELS), jax.random.fold_in(splits[1], 1), 0, LEVELS - 1).astype(jnp.int32)
    mod_table = gaussian(splits[2], (LEVELS, 3 * D), 0.5, 3.0)
    step_size = jnp.clip(jnp.exp(jax.random.uniform(splits[3], (LEVELS,), jnp.float32, math.log(0.2), math.log(1.0))), 0.2, 1.0)
    qkv_weight = gaussian(splits[4], (3, D, HEADS * HD), D ** -0.5, 0.109375, ((2, 4),))
    q_gain = draw_q_gain(jax.random.fold_in(splits[9], 71), 0)
    k_gain = draw_k_gain(jax.random.fold_in(splits[9], 71), 0)
    out_weight = gaussian(splits[7], (HEADS * HD, D), (HEADS * HD) ** -0.5, 0.109375, ((0, 4),))
    fresh_noise = gaussian(splits[8], (STEPS, FT, D), 1.0, 6.0, ((1, 4),))
    return {"latents": latents, "levels": levels, "mod_table": mod_table, "step_size": step_size, "qkv_weight": qkv_weight, "q_gain": q_gain, "k_gain": k_gain, "out_weight": out_weight, "fresh_noise": fresh_noise}


def normalize(values, epsilon):
    return values * lax.rsqrt(lax.optimization_barrier(jnp.mean(values * values, axis=-1, keepdims=True)) + epsilon)

def reference(latents, levels, mod_table, step_size, qkv_weight, q_gain, k_gain, out_weight, fresh_noise):
    group_count = N_TENSOR
    per_group = HEADS // group_count
    onehot = (levels[:, None] == jnp.arange(LEVELS, dtype=jnp.int32)[None, :]).astype(jnp.float32)
    modulation = jnp.dot(onehot, mod_table.astype(jnp.float32), precision=lax.Precision.HIGHEST)
    rates = jnp.dot(onehot, step_size, precision=lax.Precision.HIGHEST)
    grouped_out = out_weight.reshape(group_count, per_group * HD, D).astype(jnp.float32)
    first_flags = jnp.arange(FRAMES) == 0
    queue = latents
    for step_index in range(STEPS):
        queue = jnp.concatenate([fresh_noise[step_index][None], queue[:-1]], axis=0)

        def project(items):
            frame, modrow = items
            state = frame.astype(jnp.float32)
            normed = (normalize(state, 1e-06) * (1.0 + modrow[D:2 * D]) + modrow[:D]).astype(jnp.bfloat16)
            query = jnp.dot(normed, qkv_weight[0], preferred_element_type=jnp.float32).reshape(FT, HEADS, HD)
            keys = jnp.dot(normed, qkv_weight[1], preferred_element_type=jnp.float32).reshape(FT, HEADS, HD)
            values = jnp.dot(normed, qkv_weight[2], preferred_element_type=jnp.float32).reshape(FT, HEADS, HD)
            query = (normalize(query, 1e-06) * q_gain).astype(jnp.bfloat16)
            keys = (normalize(keys, 1e-06) * k_gain).astype(jnp.bfloat16)
            return (query, keys, values.astype(jnp.bfloat16))
        query, keys, values = lax.map(project, (queue, modulation))
        prior_keys = jnp.concatenate([jnp.zeros_like(keys[:1]), keys[:-1]], axis=0)
        prior_values = jnp.concatenate([jnp.zeros_like(values[:1]), values[:-1]], axis=0)

        def attend(items):
            frame_query, frame_keys, frame_values, old_keys, old_values, is_first, modrow, rate, frame = items
            all_keys = jnp.concatenate([old_keys, frame_keys], axis=0).astype(jnp.float32)
            all_values = jnp.concatenate([old_values, frame_values], axis=0).astype(jnp.float32)
            scores = jnp.einsum('qhd,khd->hqk', frame_query.astype(jnp.float32), all_keys) / jnp.sqrt(jnp.float32(HD))
            key_valid = jnp.logical_or(jnp.arange(2 * FT) >= FT, jnp.logical_not(is_first))
            scores = jnp.where(key_valid[None, None, :], scores, jnp.float32(-1e+30))
            row_top = lax.optimization_barrier(jnp.max(scores, axis=-1, keepdims=True))
            raised = jnp.exp(scores - row_top)
            weights = (raised / lax.optimization_barrier(jnp.sum(raised, axis=-1, keepdims=True))).astype(jnp.bfloat16)
            attended = jnp.einsum('hqk,khd->qhd', weights.astype(jnp.float32), all_values).astype(jnp.bfloat16)
            attended = attended.reshape(FT, group_count, per_group * HD).astype(jnp.float32)
            partials = jnp.einsum('tgc,gcd->gtd', attended, grouped_out).astype(jnp.bfloat16)
            update = lax.optimization_barrier(jnp.sum(partials.astype(jnp.float32), axis=0))
            state = frame.astype(jnp.float32)
            return (state + rate * modrow[2 * D:] * update).astype(jnp.bfloat16)
        queue = lax.map(attend, (query, keys, values, prior_keys, prior_values, first_flags, modulation, rates, queue))
    return queue
```

```python
import functools
import math

import jax
import jax.numpy as jnp
from jax import lax
from jax.experimental import pallas as pl
from jax.experimental.pallas import tpu as pltpu
from jax.sharding import PartitionSpec as P

HD = 128
STEPS = 2
CHUNKS = 2
EPS = 1e-6
AXES = ("queue", "tensor")
F32 = jnp.float32
BF16 = jnp.bfloat16
SCORE_SCALE = math.log2(math.e) / math.sqrt(HD)


def compiler_params(mib):
    return pltpu.CompilerParams(vmem_limit_bytes=mib * 2**20)


def cost(flops, nbytes, transcendentals=0):
    return pl.CostEstimate(
        flops=int(flops), bytes_accessed=int(nbytes), transcendentals=int(transcendentals)
    )


def head_normalize(values, gain):
    parts = []
    for h in range(values.shape[1] // HD):
        part = values[:, h * HD : (h + 1) * HD]
        mean = jnp.mean(part * part, axis=-1, keepdims=True)
        parts.append(part * lax.rsqrt(mean + EPS) * gain)
    return parts[0] if len(parts) == 1 else jnp.concatenate(parts, axis=1)


def key_value_kernel(z_ref, scale_ref, shift_ref, w_ref, gain_ref, kv_ref, normed_ref, *, blocks):
    step = pl.program_id(0)
    rows = z_ref.shape[0]

    @pl.when(step == 0)
    def _():
        def one(i, carry):
            at = pl.ds(pl.multiple_of(i * 16, 16), 16)
            state = z_ref[at, :].astype(F32)
            mean = jnp.mean(state * state, axis=-1, keepdims=True)
            state = state * lax.rsqrt(mean + EPS) * scale_ref[...] + shift_ref[...]
            normed_ref[at, :] = state.astype(BF16)
            return carry

        lax.fori_loop(0, rows // 16, one, 0)

    product = jnp.dot(normed_ref[...], w_ref[0], preferred_element_type=F32)

    @pl.when(step < blocks)
    def _():
        kv_ref[0] = head_normalize(product, gain_ref[...]).astype(BF16)

    @pl.when(step >= blocks)
    def _():
        kv_ref[0] = product.astype(BF16)


def key_value(z, scale1, shift, qkv_weight, k_gain):
    rows, width = z.shape
    head_cols = qkv_weight.shape[2]
    cols = 256 if head_cols % 256 == 0 else HD
    blocks = head_cols // cols
    return pl.pallas_call(
        functools.partial(key_value_kernel, blocks=blocks),
        grid=(2 * blocks,),
        in_specs=[
            pl.BlockSpec((rows, width), lambda j: (0, 0)),
            pl.BlockSpec((1, width), lambda j: (0, 0)),
            pl.BlockSpec((1, width), lambda j: (0, 0)),
            pl.BlockSpec((1, width, cols), lambda j: (1 + j // blocks, 0, j % blocks)),
            pl.BlockSpec((1, HD), lambda j: (0, 0)),
        ],
        out_specs=[
            pl.BlockSpec((1, rows, cols), lambda j: (j // blocks, 0, j % blocks)),
            pl.BlockSpec((rows, width), lambda j: (0, 0)),
        ],
        out_shape=[
            jax.ShapeDtypeStruct((2, rows, head_cols), BF16),
            jax.ShapeDtypeStruct((rows, width), BF16),
        ],
        compiler_params=compiler_params(48),
        cost_estimate=cost(
            4 * rows * width * head_cols, 4 * (rows * width + width * head_cols + rows * head_cols)
        ),
        name="norm_keys_values",
    )(z, scale1, shift, qkv_weight, k_gain)


def attend_parts(query, kv_refs, at):
    scores = [
        lax.dot_general(
            query, ref[0, :, at], (((1,), (1,)), ((), ())), preferred_element_type=F32
        )
        for ref in kv_refs
    ]
    tops = [jnp.max(s, axis=-1, keepdims=True) for s in scores]
    return scores, functools.reduce(jnp.maximum, tops)


def weigh_parts(scores, top, kv_refs, at):
    total = None
    for s, ref in zip(scores, kv_refs):
        weights = jnp.exp2(s - top).astype(BF16)
        values = ref[1, :, at]
        extended = jnp.concatenate([values, jnp.ones_like(values)], axis=1)
        term = jnp.dot(weights, extended, preferred_element_type=F32)
        total = term if total is None else total + term
    return total[:, :HD], total[:, HD:]


def own_kernel(*refs, chunks):
    normed_ref, w_ref, gain_ref = refs[:3]
    kv_refs = refs[3 : 3 + chunks]
    query_ref, acc_ref, top_ref, total_ref = refs[3 + chunks :]
    product = jnp.dot(normed_ref[...], w_ref[0], preferred_element_type=F32)
    query = head_normalize(product, gain_ref[...]).astype(BF16)
    query_ref[...] = query
    for h in range(query.shape[1] // HD):
        at = slice(h * HD, (h + 1) * HD)
        scores, top = attend_parts(query[:, at], kv_refs, at)
        acc, total = weigh_parts(scores, top, kv_refs, at)
        acc_ref[:, at] = acc
        total_ref[:, at] = total
        top_ref[:, at] = jnp.broadcast_to(top, acc.shape)


def own_attention(normed, qkv_weight, q_gain, kvs):
    rows, width = normed.shape
    head_cols = qkv_weight.shape[2]
    cols = 256 if head_cols % 256 == 0 else HD
    chunks = len(kvs)
    key_rows = kvs[0].shape[1]
    keys = chunks * key_rows
    by_heads = pl.BlockSpec((rows, cols), lambda j: (0, j))
    return pl.pallas_call(
        functools.partial(own_kernel, chunks=chunks),
        grid=(head_cols // cols,),
        in_specs=[
            pl.BlockSpec((rows, width), lambda j: (0, 0)),
            pl.BlockSpec((1, width, cols), lambda j: (0, 0, j)),
            pl.BlockSpec((1, HD), lambda j: (0, 0)),
        ]
        + [pl.BlockSpec((2, key_rows, cols), lambda j: (0, 0, j))] * chunks,
        out_specs=[by_heads] * 4,
        out_shape=[jax.ShapeDtypeStruct((rows, head_cols), BF16)]
        + [jax.ShapeDtypeStruct((rows, head_cols), F32)] * 3,
        compiler_params=compiler_params(48),
        cost_estimate=cost(
            2 * rows * width * head_cols + 8 * rows * keys * head_cols,
            2 * (rows * width + width * head_cols) + 14 * rows * head_cols + 4 * keys * head_cols,
            rows * keys * head_cols // HD,
        ),
        name="queries_own_frame",
    )(normed, qkv_weight, q_gain, *kvs)


def earlier_kernel(*refs, chunks):
    has_earlier_ref, query_ref, acc_ref, top_ref, total_ref = refs[:5]
    kv_refs = refs[5 : 5 + chunks]
    out_ref = refs[5 + chunks]
    heads = query_ref.shape[1] // HD

    @pl.when(has_earlier_ref[0] == 0)
    def _():
        out_ref[...] = (acc_ref[...] / total_ref[...]).astype(BF16)

    @pl.when(has_earlier_ref[0] != 0)
    def _():
        for h in range(heads):
            at = slice(h * HD, (h + 1) * HD)
            old_top = top_ref[:, at][:, :1]
            scores, top = attend_parts(query_ref[:, at], kv_refs, at)
            top = jnp.maximum(top, old_top)
            acc, total = weigh_parts(scores, top, kv_refs, at)
            kept = jnp.exp2(old_top - top)
            acc = acc + acc_ref[:, at] * kept
            total = total + total_ref[:, at] * kept
            out_ref[:, at] = (acc / total).astype(BF16)


def earlier_attention(has_earlier, query, acc, top, total, kvs):
    rows, head_cols = query.shape
    cols = 256 if head_cols % 256 == 0 else HD
    chunks = len(kvs)
    key_rows = kvs[0].shape[1]
    keys = chunks * key_rows
    by_heads = pl.BlockSpec((rows, cols), lambda j, flag: (0, j))
    return pl.pallas_call(
        functools.partial(earlier_kernel, chunks=chunks),
        grid_spec=pltpu.PrefetchScalarGridSpec(
            num_scalar_prefetch=1,
            grid=(head_cols // cols,),
            in_specs=[by_heads] * 4
            + [pl.BlockSpec((2, key_rows, cols), lambda j, flag: (0, 0, j))] * chunks,
            out_specs=by_heads,
        ),
        out_shape=jax.ShapeDtypeStruct((rows, head_cols), BF16),
        compiler_params=compiler_params(48),
        cost_estimate=cost(
            8 * rows * keys * head_cols,
            16 * rows * head_cols + 4 * keys * head_cols,
            rows * keys * head_cols // HD,
        ),
        name="earlier_frame",
    )(has_earlier, query, acc, top, total, *kvs)


def output_kernel(*refs, piece_counts, half_blocks):
    parity_ref, resid_ref, gate_ref = refs[:3]
    del parity_ref
    step = pl.program_id(0)
    at = 3
    pieces = []
    for count in piece_counts:
        pieces.append(refs[at : at + count])
        at += count
    others = len(piece_counts) - 1
    own_w = refs[at]
    mine = refs[at + 1 : at + 1 + others]
    sibling = refs[at + 1 + others : at + 1 + 2 * others]
    out_ref, held_ref = refs[at + 1 + 2 * others :]

    @pl.when(step == 0)
    def _():
        for k, parts in enumerate(pieces):
            row = 0
            for part in parts:
                held_ref[k, row : row + part.shape[0], :] = part[...]
                row += part.shape[0]

    def run(weights):
        update = jnp.dot(held_ref[0], own_w[...], preferred_element_type=F32)
        for k, w_ref in enumerate(weights):
            update += jnp.dot(held_ref[k + 1], w_ref[...], preferred_element_type=F32)
        out_ref[...] = (resid_ref[...].astype(F32) + gate_ref[...] * update).astype(BF16)

    @pl.when(step < half_blocks)
    def _():
        run(mine)

    @pl.when(step >= half_blocks)
    def _():
        run(sibling)


def output_projection(parity, resid, resid_chunk, gate, pieces, own_w, mine, sibling):
    head_cols, width = own_w.shape
    rows = pieces[0][0].shape[0]
    cols = 512 if (width // 2) % 512 == 0 else HD
    half_blocks = width // 2 // cols

    def column(j, parity):
        return (j // half_blocks) ^ parity[0], j % half_blocks

    def absolute(j, parity):
        half, block = column(j, parity)
        return half * half_blocks + block

    flat = [part for parts in pieces for part in parts]
    return pl.pallas_call(
        functools.partial(
            output_kernel,
            piece_counts=tuple(len(parts) for parts in pieces),
            half_blocks=half_blocks,
        ),
        grid_spec=pltpu.PrefetchScalarGridSpec(
            num_scalar_prefetch=1,
            grid=(2 * half_blocks,),
            in_specs=[
                pl.BlockSpec((rows, cols), lambda j, p: (resid_chunk, absolute(j, p))),
                pl.BlockSpec((1, cols), lambda j, p: (0, absolute(j, p))),
            ]
            + [pl.BlockSpec(part.shape, lambda j, p: (0, 0)) for part in flat]
            + [pl.BlockSpec((head_cols, cols), lambda j, p: (0, absolute(j, p)))]
            + [
                pl.BlockSpec((head_cols, cols), lambda j, p: (0, jnp.minimum(j, half_blocks - 1)))
                for _ in mine
            ]
            + [
                pl.BlockSpec((head_cols, cols), lambda j, p: (0, jnp.maximum(j - half_blocks, 0)))
                for _ in sibling
            ],
            out_specs=pl.BlockSpec((rows, cols), lambda j, p: (0, absolute(j, p))),
            scratch_shapes=[pltpu.VMEM((len(pieces), rows, head_cols), BF16)],
        ),
        out_shape=jax.ShapeDtypeStruct((rows, width), BF16),
        compiler_params=compiler_params(52),
        cost_estimate=cost(
            2 * rows * width * head_cols * len(pieces),
            2 * (2 * rows * width + head_cols * width * len(pieces)),
        ),
        name="output_projection",
    )(parity, resid, gate, *flat, own_w, *mine, *sibling)


def send(block, move, queue_size, tensor_size, frames=None):
    pairs = []
    for q in range(queue_size) if frames is None else frames:
        for t in range(tensor_size):
            to_q, to_t = move(q, t)
            pairs.append((q * tensor_size + t, to_q * tensor_size + to_t))
    return lax.ppermute(block, AXES, pairs)


def gather_pieces(block, queue_size, tensor_size, frames=None):
    half = tensor_size // 2

    def low(q, t):
        return q, t ^ 1

    def high(j):
        return lambda q, t: (q, (t // 2 - j) % half * 2 + t % 2)

    args = (queue_size, tensor_size, frames)
    rows = block.shape[0] // 2
    near = send(block, low, *args)
    far = [send(block, high(j), *args) for j in range(1, half)]
    pieces = [[block], [near]]
    for j in range(1, half):
        top = send(near[:rows], high(j), *args)
        bottom = send(far[j - 1][rows:], low, *args)
        pieces += [[far[j - 1]], [top, bottom]]
    return pieces


def gather_noise(noise, queue_size, tensor_size):
    index = lax.axis_index("tensor")
    last = [queue_size - 1]
    rows = noise.shape[0]
    frame = jnp.zeros((tensor_size,) + noise.shape, noise.dtype)
    frame = lax.dynamic_update_slice(frame, noise[None], (index, 0, 0))
    for d in range(1, tensor_size):
        came = send(
            noise, lambda q, t: (q, (t - d) % tensor_size), queue_size, tensor_size, last
        )
        frame = lax.dynamic_update_slice(
            frame, came[None], ((index + d) % tensor_size, 0, 0)
        )
    return frame.reshape(tensor_size * rows, noise.shape[1])


def body(
    latents, levels, mod_table, step_size, qkv_weight, q_gain, k_gain, out_weight, fresh_noise
):
    queue_size = lax.axis_size("queue")
    tensor_size = lax.axis_size("tensor")
    rows, width = latents.shape[1:]
    mesh_sizes = (queue_size, tensor_size)
    queue_index = lax.axis_index("queue")
    is_last = queue_index == queue_size - 1
    parity = (queue_index % 2).astype(jnp.int32)

    def ring(block):
        return send(block, lambda q, t: ((q + 1) % queue_size, t), *mesh_sizes)

    def sibling(block):
        return send(block, lambda q, t: (q ^ 1, t), *mesh_sizes)

    worked_level = send(levels, lambda q, t: ((q - 1) % queue_size, t), *mesh_sizes)[0]
    held_level = levels[0]

    def modulation(level):
        row = lax.dynamic_slice(mod_table, (level, 0), (1, 3 * width)).astype(F32)
        return row[:, :width], row[:, width : 2 * width], row[:, 2 * width :]

    shift, scale, _ = modulation(worked_level)
    _, _, gate = modulation(held_level)
    gate = gate * lax.dynamic_slice(step_size, (held_level,), (1,))[:, None]
    scale1 = 1.0 + scale
    has_earlier = jnp.where(is_last, 0, 1).astype(jnp.int32)[None]

    noise = [gather_noise(fresh_noise[s], *mesh_sizes) for s in range(STEPS)]

    half_weight = lax.dynamic_slice(
        out_weight, (0, parity * (width // 2)), (out_weight.shape[0], width // 2)
    )
    gathered = gather_pieces(half_weight, *mesh_sizes)[1:]
    mine = [jnp.concatenate(parts, axis=0) if len(parts) > 1 else parts[0] for parts in gathered]
    theirs = [sibling(block) for block in mine]

    q_gain = (q_gain * SCORE_SCALE)[None]
    k_gain = k_gain[None]
    chunk_rows = rows // CHUNKS
    frame = jnp.where(is_last, noise[0], latents[0])
    frames = [frame[c * chunk_rows : (c + 1) * chunk_rows] for c in range(CHUNKS)]
    for step_index in range(STEPS):
        final = step_index == STEPS - 1
        made = [key_value(part, scale1, shift, qkv_weight, k_gain) for part in frames]
        kvs = [kv for kv, _ in made]
        earlier = [ring(kv) for kv in kvs]
        own = [own_attention(normed, qkv_weight, q_gain, kvs) for _, normed in made]
        attended = [earlier_attention(has_earlier, *parts, earlier) for parts in own]
        resid = [ring(part) for part in frames]
        targets = range(queue_size) if final else range(queue_size - 1)
        pieces = [gather_pieces(ring(block), *mesh_sizes, targets) for block in attended]
        step_gate = gate
        if not final:
            step_gate = jnp.where(is_last, 0.0, gate)
            resid = [
                jnp.where(
                    is_last,
                    noise[step_index + 1][c * chunk_rows : (c + 1) * chunk_rows],
                    part,
                )
                for c, part in enumerate(resid)
            ]
        frames = [
            output_projection(
                parity[None], part, 0, step_gate, block, out_weight, mine, theirs
            )
            for part, block in zip(resid, pieces)
        ]
    return jnp.concatenate(frames, axis=0)[None]


def solution(mesh):
    return jax.shard_map(
        body,
        mesh=mesh,
        in_specs=(
            P("queue", None, None),
            P("queue"),
            P(),
            P(),
            P(None, None, "tensor"),
            P(),
            P(),
            P("tensor", None),
            P(None, "tensor", None),
        ),
        out_specs=P("queue", None, None),
        check_vma=False,
    )
```

```python
import functools
import math

import jax
import jax.numpy as jnp
from jax import lax
from jax.experimental import pallas as pl
from jax.experimental.pallas import tpu as pltpu
from jax.sharding import PartitionSpec as P

HD = 128
STEPS = 2
CHUNKS = 2
EPS = 1e-6
AXES = ("queue", "tensor")
F32 = jnp.float32
BF16 = jnp.bfloat16
SCORE_SCALE = math.log2(math.e) / math.sqrt(HD)
ANY = pl.BlockSpec(memory_space=pl.ANY)


def compiler_params(mib):
    return pltpu.CompilerParams(vmem_limit_bytes=mib * 2**20)


def cost(flops, nbytes, transcendentals=0):
    return pl.CostEstimate(
        flops=int(flops), bytes_accessed=int(nbytes), transcendentals=int(transcendentals)
    )


def qkv_kernel(*refs, tensor_size, first_row, noise_first_row, noise_step, k_blocks):
    info_ref, scale_ref, shift_ref, w_ref, gain_ref, z_any, noise_any = refs[:7]
    piece_refs = refs[7 : 7 + tensor_size - 1]
    kv_ref, query_ref, state_ref, normed_ref, acc_ref, sem = refs[6 + tensor_size :]
    part, block = pl.program_id(0), pl.program_id(1)
    rows, width = state_ref.shape
    piece_rows = noise_any.shape[1]
    block_width = width // k_blocks

    @pl.when(jnp.logical_and(part == 0, block == 0))
    def _():
        @pl.when(info_ref[0] == 0)
        def _():
            copy = pltpu.make_async_copy(z_any.at[pl.ds(first_row, rows)], state_ref, sem.at[0])
            copy.start()
            copy.wait()

        @pl.when(info_ref[0] != 0)
        def _():
            unit = math.gcd(rows, piece_rows)
            for b in range(rows // unit):
                row = noise_first_row + b * unit
                away = lax.rem(row // piece_rows + tensor_size - info_ref[1], tensor_size)
                inside = pl.ds(row % piece_rows, unit)
                for d in range(tensor_size):
                    source = noise_any.at[noise_step] if d == 0 else piece_refs[d - 1]

                    @pl.when(away == d)
                    def _():
                        copy = pltpu.make_async_copy(
                            source.at[inside], state_ref.at[pl.ds(b * unit, unit)], sem.at[0]
                        )
                        copy.start()
                        copy.wait()

        def one(i, carry):
            at = pl.ds(pl.multiple_of(i * 16, 16), 16)
            state = state_ref[at, :].astype(F32)
            mean = jnp.mean(state * state, axis=-1, keepdims=True)
            state = state * lax.rsqrt(mean + EPS) * scale_ref[...] + shift_ref[...]
            state = state.astype(BF16)
            for k in range(k_blocks):
                normed_ref[k, at, :] = state[:, k * block_width : (k + 1) * block_width]
            return carry

        lax.fori_loop(0, rows // 16, one, 0)

    product = jnp.dot(normed_ref[block], w_ref[0], preferred_element_type=F32)

    @pl.when(block == 0)
    def _():
        acc_ref[...] = product

    @pl.when(jnp.logical_and(block > 0, block < k_blocks - 1))
    def _():
        acc_ref[...] += product

    @pl.when(block == k_blocks - 1)
    def _():
        def normalized(gain):
            for h in range(product.shape[1] // HD):
                at = slice(h * HD, (h + 1) * HD)
                head = acc_ref[:, at] + product[:, at]
                mean = jnp.mean(head * head, axis=-1, keepdims=True)
                yield at, (head * lax.rsqrt(mean + EPS) * gain).astype(BF16)

        @pl.when(part == 0)
        def _():
            for at, head in normalized(gain_ref[1:2]):
                kv_ref[0, :, at] = head

        @pl.when(part == 1)
        def _():
            kv_ref[0] = (acc_ref[...] + product).astype(BF16)

        @pl.when(part == 2)
        def _():
            for at, head in normalized(gain_ref[0:1]):
                query_ref[:, at] = head


def project_qkv(info, scale1, shift, qkv_weight, gains, z, first_row, rows, noise):
    width, head_cols = qkv_weight.shape[1:]
    noise_all, noise_step, pieces, noise_first_row = noise
    tensor_size = len(pieces) + 1
    k_blocks = 4
    block_width = width // k_blocks
    return pl.pallas_call(
        functools.partial(
            qkv_kernel,
            tensor_size=tensor_size,
            first_row=first_row,
            noise_first_row=noise_first_row,
            noise_step=noise_step,
            k_blocks=k_blocks,
        ),
        grid_spec=pltpu.PrefetchScalarGridSpec(
            num_scalar_prefetch=1,
            grid=(3, k_blocks),
            in_specs=[
                pl.BlockSpec((1, width), lambda p, k, i: (0, 0)),
                pl.BlockSpec((1, width), lambda p, k, i: (0, 0)),
                pl.BlockSpec((1, block_width, head_cols), lambda p, k, i: ((p + 1) % 3, k, 0)),
                pl.BlockSpec((2, HD), lambda p, k, i: (0, 0)),
            ]
            + [ANY] * (1 + tensor_size),
            out_specs=[
                pl.BlockSpec((1, rows, head_cols), lambda p, k, i: (jnp.minimum(p, 1), 0, 0)),
                pl.BlockSpec((rows, head_cols), lambda p, k, i: (0, 0)),
                pl.BlockSpec((rows, width), lambda p, k, i: (0, 0)),
            ],
            scratch_shapes=[
                pltpu.VMEM((k_blocks, rows, block_width), BF16),
                pltpu.VMEM((rows, head_cols), F32),
                pltpu.SemaphoreType.DMA((1,)),
            ],
        ),
        out_shape=[
            jax.ShapeDtypeStruct((2, rows, head_cols), BF16),
            jax.ShapeDtypeStruct((rows, head_cols), BF16),
            jax.ShapeDtypeStruct((rows, width), BF16),
        ],
        compiler_params=compiler_params(32),
        cost_estimate=cost(
            6 * rows * width * head_cols,
            4 * rows * width + 6 * width * head_cols + 6 * rows * head_cols,
        ),
        name="norm_qkv",
    )(info, scale1, shift, qkv_weight, gains, z, noise_all, *pieces)


def attend_parts(query, kv_refs, at):
    scores = [
        lax.dot_general(
            query, ref[0, :, at], (((1,), (1,)), ((), ())), preferred_element_type=F32
        )
        for ref in kv_refs
    ]
    tops = [jnp.max(s, axis=-1, keepdims=True) for s in scores]
    return scores, functools.reduce(jnp.maximum, tops)


def weigh_parts(scores, top, kv_refs, at):
    total = None
    for s, ref in zip(scores, kv_refs):
        weights = jnp.exp2(s - top).astype(BF16)
        values = ref[1, :, at]
        extended = jnp.concatenate([values, jnp.ones_like(values)], axis=1)
        term = jnp.dot(weights, extended, preferred_element_type=F32)
        total = term if total is None else total + term
    return total[:, :HD], total[:, HD:]


def own_kernel(*refs, chunks):
    query_ref = refs[0]
    kv_refs = refs[1 : 1 + chunks]
    acc_ref, top_ref, total_ref = refs[1 + chunks :]
    for h in range(query_ref.shape[1] // HD):
        at = slice(h * HD, (h + 1) * HD)
        scores, top = attend_parts(query_ref[:, at], kv_refs, at)
        acc, total = weigh_parts(scores, top, kv_refs, at)
        acc_ref[:, at] = acc
        total_ref[:, at] = total
        top_ref[:, at] = jnp.broadcast_to(top, acc.shape)


def own_attention(query, kvs):
    rows, head_cols = query.shape
    cols = 256 if head_cols % 256 == 0 else HD
    chunks = len(kvs)
    key_rows = kvs[0].shape[1]
    keys = chunks * key_rows
    by_heads = pl.BlockSpec((rows, cols), lambda j: (0, j))
    return pl.pallas_call(
        functools.partial(own_kernel, chunks=chunks),
        grid=(head_cols // cols,),
        in_specs=[by_heads] + [pl.BlockSpec((2, key_rows, cols), lambda j: (0, 0, j))] * chunks,
        out_specs=[by_heads] * 3,
        out_shape=[jax.ShapeDtypeStruct((rows, head_cols), F32)] * 3,
        compiler_params=compiler_params(32),
        cost_estimate=cost(
            8 * rows * keys * head_cols,
            14 * rows * head_cols + 4 * keys * head_cols,
            rows * keys * head_cols // HD,
        ),
        name="own_frame",
    )(query, *kvs)


def earlier_kernel(*refs, chunks):
    info_ref, query_ref, acc_ref, top_ref, total_ref = refs[:5]
    kv_refs = refs[5 : 5 + chunks]
    out_ref = refs[5 + chunks]
    heads = query_ref.shape[1] // HD

    @pl.when(info_ref[0] != 0)
    def _():
        out_ref[...] = (acc_ref[...] / total_ref[...]).astype(BF16)

    @pl.when(info_ref[0] == 0)
    def _():
        for h in range(heads):
            at = slice(h * HD, (h + 1) * HD)
            old_top = top_ref[:, at][:, :1]
            scores, top = attend_parts(query_ref[:, at], kv_refs, at)
            top = jnp.maximum(top, old_top)
            acc, total = weigh_parts(scores, top, kv_refs, at)
            kept = jnp.exp2(old_top - top)
            acc = acc + acc_ref[:, at] * kept
            total = total + total_ref[:, at] * kept
            out_ref[:, at] = (acc / total).astype(BF16)


def earlier_attention(info, query, acc, top, total, kvs):
    rows, head_cols = query.shape
    cols = 256 if head_cols % 256 == 0 else HD
    chunks = len(kvs)
    key_rows = kvs[0].shape[1]
    keys = chunks * key_rows
    by_heads = pl.BlockSpec((rows, cols), lambda j, i: (0, j))
    return pl.pallas_call(
        functools.partial(earlier_kernel, chunks=chunks),
        grid_spec=pltpu.PrefetchScalarGridSpec(
            num_scalar_prefetch=1,
            grid=(head_cols // cols,),
            in_specs=[by_heads] * 4
            + [pl.BlockSpec((2, key_rows, cols), lambda j, i: (0, 0, j))] * chunks,
            out_specs=by_heads,
        ),
        out_shape=jax.ShapeDtypeStruct((rows, head_cols), BF16),
        compiler_params=compiler_params(32),
        cost_estimate=cost(
            8 * rows * keys * head_cols,
            16 * rows * head_cols + 4 * keys * head_cols,
            rows * keys * head_cols // HD,
        ),
        name="earlier_frame",
    )(info, query, acc, top, total, *kvs)


def output_kernel(*refs, piece_counts, aliased):
    parity_ref, resid_ref, gate_ref = refs[:3]
    at = 3
    pieces = []
    for count in piece_counts:
        pieces.append(refs[at : at + count])
        at += count
    size = len(piece_counts)
    own_w = refs[at]
    others = refs[at + 1 : at + 2 * size - 1]
    at += 2 * size - 1 + aliased
    out_ref, held_ref, w_buf, acc_ref, held_sems, w_sems = refs[at:]
    step = pl.program_id(0)
    slots = w_buf.shape[0]
    half_width = w_buf.shape[2]

    def weight_copy(i):
        if i % size == 0:
            column = (parity_ref[0] ^ (i // size)) * half_width
            source = own_w.at[:, pl.ds(pl.multiple_of(column, HD), half_width)]
        else:
            source = others[i // size * (size - 1) + i % size - 1]
        return pltpu.make_async_copy(source, w_buf.at[i % slots], w_sems.at[i % slots])

    def held_copies(k):
        row = 0
        for number, part in enumerate(pieces[k]):
            count = part.shape[0]
            yield pltpu.make_async_copy(
                part, held_ref.at[k, pl.ds(row, count)], held_sems.at[k, number]
            )
            row += count

    @pl.when(step == 0)
    def _():
        for i in range(slots - 1):
            weight_copy(i).start()
            for copy in held_copies(i):
                copy.start()
        for k in range(slots - 1, size):
            for copy in held_copies(k):
                copy.start()

    for i in range(slots - 1, 2 * size):

        @pl.when(step == i - (slots - 1))
        def _():
            weight_copy(i).start()

    for k in range(size):

        @pl.when(step == k)
        def _():
            for copy in held_copies(k):
                copy.wait()

    for i in range(2 * size):

        @pl.when(step == i)
        def _():
            weight_copy(i).wait()

    k = lax.rem(step, size)
    product = jnp.dot(held_ref[k], w_buf[lax.rem(step, slots)], preferred_element_type=F32)

    @pl.when(k == 0)
    def _():
        acc_ref[...] = product

    @pl.when(jnp.logical_and(k > 0, k < size - 1))
    def _():
        acc_ref[...] += product

    @pl.when(k == size - 1)
    def _():
        update = acc_ref[...] + product
        out_ref[...] = (resid_ref[...].astype(F32) + gate_ref[...] * update).astype(BF16)


def output_projection(parity, resid, gate, pieces, own_w, mine, theirs, out_rows, chunk, into):
    head_cols, width = own_w.shape
    rows = resid.shape[0]
    size = len(pieces)
    half_width = width // 2
    parts = max(len(p) for p in pieces)
    flat = [part for group in pieces for part in group]
    alias = [] if into is None else [into]
    operands = [parity, resid, gate, *flat, own_w, *mine, *theirs, *alias]

    def column(j, parity):
        return (j // size) ^ parity[0]

    return pl.pallas_call(
        functools.partial(
            output_kernel,
            piece_counts=tuple(len(p) for p in pieces),
            aliased=len(alias),
        ),
        grid_spec=pltpu.PrefetchScalarGridSpec(
            num_scalar_prefetch=1,
            grid=(2 * size,),
            in_specs=[
                pl.BlockSpec((rows, half_width), lambda j, p: (0, column(j, p))),
                pl.BlockSpec((1, half_width), lambda j, p: (0, column(j, p))),
            ]
            + [ANY] * (len(operands) - 3),
            out_specs=pl.BlockSpec((rows, half_width), lambda j, p: (chunk, column(j, p))),
            scratch_shapes=[
                pltpu.VMEM((size, rows, head_cols), BF16),
                pltpu.VMEM((3, head_cols, half_width), BF16),
                pltpu.VMEM((rows, half_width), F32),
                pltpu.SemaphoreType.DMA((size, parts)),
                pltpu.SemaphoreType.DMA((3,)),
            ],
        ),
        out_shape=jax.ShapeDtypeStruct((out_rows, width), BF16),
        input_output_aliases={} if into is None else {len(operands) - 1: 0},
        compiler_params=compiler_params(36),
        cost_estimate=cost(
            2 * rows * width * head_cols * size,
            2 * (2 * rows * width + head_cols * width * size),
        ),
        name="output_projection",
    )(*operands)


def send(block, move, queue_size, tensor_size, frames=None):
    pairs = []
    for q in range(queue_size) if frames is None else frames:
        for t in range(tensor_size):
            to_q, to_t = move(q, t)
            pairs.append((q * tensor_size + t, to_q * tensor_size + to_t))
    return lax.ppermute(block, AXES, pairs)


def gather_pieces(block, queue_size, tensor_size, frames=None):
    half = tensor_size // 2

    def low(q, t):
        return q, t ^ 1

    def high(j):
        return lambda q, t: (q, (t // 2 - j) % half * 2 + t % 2)

    args = (queue_size, tensor_size, frames)
    rows = block.shape[0] // 2
    near = send(block, low, *args)
    far = [send(block, high(j), *args) for j in range(1, half)]
    pieces = [[block], [near]]
    for j in range(1, half):
        top = send(near[:rows], high(j), *args)
        bottom = send(far[j - 1][rows:], low, *args)
        pieces += [[far[j - 1]], [top, bottom]]
    return pieces


def body(
    latents, levels, mod_table, step_size, qkv_weight, q_gain, k_gain, out_weight, fresh_noise
):
    queue_size = lax.axis_size("queue")
    tensor_size = lax.axis_size("tensor")
    rows, width = latents.shape[1:]
    mesh_sizes = (queue_size, tensor_size)
    queue_index = lax.axis_index("queue")
    tensor_index = lax.axis_index("tensor")
    parity = (queue_index % 2).astype(jnp.int32)[None]

    def ahead(block):
        return send(block, lambda q, t: (q + 1, t), *mesh_sizes, range(queue_size - 1))

    def sibling(block):
        return send(block, lambda q, t: (q ^ 1, t), *mesh_sizes)

    def noise_pieces(block):
        return [
            send(block, lambda q, t: (q, (t - d) % tensor_size), *mesh_sizes, [0])
            for d in range(1, tensor_size)
        ]

    frame = ahead(latents[0])
    half_weight = lax.dynamic_slice(
        out_weight, (0, parity[0] * (width // 2)), (out_weight.shape[0], width // 2)
    )
    half_weight, fresh_noise, levels = lax.optimization_barrier(
        (half_weight, fresh_noise, levels)
    )
    gathered = gather_pieces(half_weight, *mesh_sizes)[1:]
    mine = [jnp.concatenate(parts, axis=0) if len(parts) > 1 else parts[0] for parts in gathered]
    theirs = [sibling(block) for block in mine]

    arriving_level = ahead(levels)[0]

    def modulation(level):
        row = lax.dynamic_slice(mod_table, (level, 0), (1, 3 * width)).astype(F32)
        rate = lax.dynamic_slice(step_size, (level,), (1,))[:, None]
        return row[:, :width], 1.0 + row[:, width : 2 * width], rate * row[:, 2 * width :]

    shift, scale1, gate = modulation(levels[0])
    arriving_gate = modulation(arriving_level)[2]
    info = jnp.stack([(queue_index == 0).astype(jnp.int32), tensor_index.astype(jnp.int32)])
    gains = jnp.stack([q_gain * SCORE_SCALE, k_gain])

    chunk_rows = rows // CHUNKS
    noise = noise_pieces(fresh_noise[0])
    frames = [(frame, c * chunk_rows) for c in range(CHUNKS)]
    for step_index in range(STEPS):
        final = step_index == STEPS - 1
        made = [
            project_qkv(
                info,
                scale1,
                shift,
                qkv_weight,
                gains,
                part,
                first_row,
                chunk_rows,
                (fresh_noise, step_index, noise, c * chunk_rows),
            )
            for c, (part, first_row) in enumerate(frames)
        ]
        kvs = [kv for kv, _, _ in made]
        earlier = [ahead(kv) for kv in kvs]
        own = [own_attention(query, kvs) for _, query, _ in made]
        attended = [
            earlier_attention(info, query, *parts, earlier)
            for (_, query, _), parts in zip(made, own)
        ]
        resid = [state for _, _, state in made]
        if final:
            pieces = [gather_pieces(block, *mesh_sizes) for block in attended]
            result = None
            for c in range(CHUNKS):
                result = output_projection(
                    parity, resid[c], gate, pieces[c], out_weight, mine, theirs, rows, c, result
                )
        else:
            attended = [ahead(block) for block in attended]
            attended, resid = lax.optimization_barrier((attended, resid))
            resid = [ahead(state) for state in resid]
            pieces = [
                gather_pieces(block, *mesh_sizes, range(1, queue_size)) for block in attended
            ]
            later_noise, _ = lax.optimization_barrier(
                (fresh_noise[step_index + 1], pieces[-1][1][0])
            )
            noise = noise_pieces(later_noise)
            frames = [
                (
                    output_projection(
                        parity,
                        resid[c],
                        arriving_gate,
                        pieces[c],
                        out_weight,
                        mine,
                        theirs,
                        chunk_rows,
                        0,
                        None,
                    ),
                    0,
                )
                for c in range(CHUNKS)
            ]
    return result[None]


def solution(mesh):
    return jax.shard_map(
        body,
        mesh=mesh,
        in_specs=(
            P("queue", None, None),
            P("queue"),
            P(),
            P(),
            P(None, None, "tensor"),
            P(),
            P(),
            P("tensor", None),
            P(None, "tensor", None),
        ),
        out_specs=P("queue", None, None),
        check_vma=False,
    )
```

```python
import functools
import math

import jax
import jax.numpy as jnp
from jax import lax
from jax.experimental import pallas as pl
from jax.experimental.pallas import tpu as pltpu
from jax.sharding import PartitionSpec as P

HD = 128
STEPS = 2
CHUNKS = 2
EPS = 1e-6
AXES = ("queue", "tensor")
F32 = jnp.float32
BF16 = jnp.bfloat16
SCORE_SCALE = math.log2(math.e) / math.sqrt(HD)
ANY = pl.BlockSpec(memory_space=pl.ANY)


def compiler_params(mib):
    return pltpu.CompilerParams(vmem_limit_bytes=mib * 2**20)


def in_hbm(array):
    return pltpu.with_memory_space_constraint(array, pltpu.HBM)


def cost(flops, nbytes, transcendentals=0):
    return pl.CostEstimate(
        flops=int(flops), bytes_accessed=int(nbytes), transcendentals=int(transcendentals)
    )


def head_normalized(values, gain):
    heads = []
    for h in range(values.shape[1] // HD):
        head = values[:, h * HD : (h + 1) * HD]
        mean = jnp.mean(head * head, axis=-1, keepdims=True)
        heads.append((head * lax.rsqrt(mean + EPS) * gain).astype(BF16))
    return heads[0] if len(heads) == 1 else jnp.concatenate(heads, axis=1)


def qkv_kernel(*refs, tensor_size, first_row, noise_first_row, noise_step, blocks):
    info_ref, scale_ref, shift_ref, gain_ref, w_any, z_any, noise_any = refs[:7]
    piece_refs = refs[7 : 7 + tensor_size - 1]
    kv_ref, query_ref, state_ref, normed_ref, w_ref, sem, w_sems = refs[6 + tensor_size :]
    step = pl.program_id(0)
    rows, width = state_ref.shape
    piece_rows = noise_any.shape[1]
    cols = query_ref.shape[1]
    splits = w_sems.shape[1]
    split_rows = width // splits

    def weight_copies(part):
        for i in range(splits):
            at = pl.ds(i * split_rows, split_rows)
            yield pltpu.make_async_copy(
                w_any.at[part, at], w_ref.at[part, at], w_sems.at[part, i]
            )

    @pl.when(step == 0)
    def _():
        for part in (1, 2, 0):
            for copy in weight_copies(part):
                copy.start()

        @pl.when(info_ref[0] == 0)
        def _():
            copy = pltpu.make_async_copy(z_any.at[pl.ds(first_row, rows)], state_ref, sem.at[0])
            copy.start()
            copy.wait()

        @pl.when(info_ref[0] != 0)
        def _():
            unit = math.gcd(rows, piece_rows)
            for b in range(rows // unit):
                row = noise_first_row + b * unit
                away = lax.rem(row // piece_rows + tensor_size - info_ref[1], tensor_size)
                inside = pl.ds(row % piece_rows, unit)
                for d in range(tensor_size):
                    source = noise_any if d == 0 else piece_refs[d - 1]

                    @pl.when(away == d)
                    def _():
                        copy = pltpu.make_async_copy(
                            source.at[noise_step, inside],
                            state_ref.at[pl.ds(b * unit, unit)],
                            sem.at[0],
                        )
                        copy.start()
                        copy.wait()

        def one(i, carry):
            at = pl.ds(pl.multiple_of(i * 16, 16), 16)
            state = state_ref[at, :].astype(F32)
            mean = jnp.mean(state * state, axis=-1, keepdims=True)
            state = state * lax.rsqrt(mean + EPS) * scale_ref[...] + shift_ref[...]
            normed_ref[at, :] = state.astype(BF16)
            return carry

        lax.fori_loop(0, rows // 16, one, 0)

    for order, part in enumerate((1, 2, 0)):

        @pl.when(step == order * blocks)
        def _():
            for copy in weight_copies(part):
                copy.wait()

    def project(part):
        at = pl.ds(pl.multiple_of(lax.rem(step, blocks) * cols, HD), cols)
        return jnp.dot(normed_ref[...], w_ref[part, :, at], preferred_element_type=F32)

    @pl.when(step < blocks)
    def _():
        kv_ref[0] = head_normalized(project(1), gain_ref[1:2])

    @pl.when(jnp.logical_and(step >= blocks, step < 2 * blocks))
    def _():
        kv_ref[0] = project(2).astype(BF16)

    @pl.when(step >= 2 * blocks)
    def _():
        query_ref[...] = head_normalized(project(0), gain_ref[0:1])


def project_qkv(info, scale1, shift, qkv_weight, gains, z, first_row, rows, noise):
    width, head_cols = qkv_weight.shape[1:]
    noise_all, noise_step, pieces, noise_first_row = noise
    tensor_size = len(pieces) + 1
    cols = 256 if head_cols % 256 == 0 else HD
    blocks = head_cols // cols

    def kv_block(j, i):
        j = jnp.minimum(j, 2 * blocks - 1)
        return j // blocks, 0, j % blocks

    return pl.pallas_call(
        functools.partial(
            qkv_kernel,
            tensor_size=tensor_size,
            first_row=first_row,
            noise_first_row=noise_first_row,
            noise_step=noise_step,
            blocks=blocks,
        ),
        grid_spec=pltpu.PrefetchScalarGridSpec(
            num_scalar_prefetch=1,
            grid=(3 * blocks,),
            in_specs=[
                pl.BlockSpec((1, width), lambda j, i: (0, 0)),
                pl.BlockSpec((1, width), lambda j, i: (0, 0)),
                pl.BlockSpec((2, HD), lambda j, i: (0, 0)),
            ]
            + [ANY] * (2 + tensor_size),
            out_specs=[
                pl.BlockSpec((1, rows, cols), kv_block),
                pl.BlockSpec((rows, cols), lambda j, i: (0, jnp.maximum(j - 2 * blocks, 0))),
                pl.BlockSpec((rows, width), lambda j, i: (0, 0)),
            ],
            scratch_shapes=[
                pltpu.VMEM((rows, width), BF16),
                pltpu.VMEM(qkv_weight.shape, BF16),
                pltpu.SemaphoreType.DMA((1,)),
                pltpu.SemaphoreType.DMA((3, 4)),
            ],
        ),
        out_shape=[
            jax.ShapeDtypeStruct((2, rows, head_cols), BF16),
            jax.ShapeDtypeStruct((rows, head_cols), BF16),
            pltpu.HBM((rows, width), BF16),
        ],
        compiler_params=compiler_params(36),
        cost_estimate=cost(
            6 * rows * width * head_cols,
            4 * rows * width + 6 * rows * head_cols + 6 * width * head_cols,
        ),
        name="norm_qkv",
    )(info, scale1, shift, gains, *[in_hbm(a) for a in (qkv_weight, z, noise_all, *pieces)])


def attend_parts(query, kv_refs, at):
    scores = [
        lax.dot_general(
            query, ref[0, :, at], (((1,), (1,)), ((), ())), preferred_element_type=F32
        )
        for ref in kv_refs
    ]
    tops = [jnp.max(s, axis=-1, keepdims=True) for s in scores]
    return scores, functools.reduce(jnp.maximum, tops)


def weigh_parts(scores, top, kv_refs, at):
    total = None
    for s, ref in zip(scores, kv_refs):
        weights = jnp.exp2(s - top).astype(BF16)
        values = ref[1, :, at]
        extended = jnp.concatenate([values, jnp.ones_like(values)], axis=1)
        term = jnp.dot(weights, extended, preferred_element_type=F32)
        total = term if total is None else total + term
    return total[:, :HD], total[:, HD:]


def own_kernel(*refs, chunks):
    query_ref = refs[0]
    kv_refs = refs[1 : 1 + chunks]
    acc_ref, top_ref, total_ref = refs[1 + chunks :]
    for h in range(query_ref.shape[1] // HD):
        at = slice(h * HD, (h + 1) * HD)
        scores, top = attend_parts(query_ref[:, at], kv_refs, at)
        acc, total = weigh_parts(scores, top, kv_refs, at)
        acc_ref[:, at] = acc
        total_ref[:, at] = total
        top_ref[:, at] = jnp.broadcast_to(top, acc.shape)


def own_attention(query, kvs):
    rows, head_cols = query.shape
    cols = 256 if head_cols % 256 == 0 else HD
    chunks = len(kvs)
    key_rows = kvs[0].shape[1]
    keys = chunks * key_rows
    by_heads = pl.BlockSpec((rows, cols), lambda j: (0, j))
    return pl.pallas_call(
        functools.partial(own_kernel, chunks=chunks),
        grid=(head_cols // cols,),
        in_specs=[by_heads] + [pl.BlockSpec((2, key_rows, cols), lambda j: (0, 0, j))] * chunks,
        out_specs=[by_heads] * 3,
        out_shape=[jax.ShapeDtypeStruct((rows, head_cols), F32)] * 3,
        compiler_params=compiler_params(24),
        cost_estimate=cost(
            8 * rows * keys * head_cols,
            14 * rows * head_cols + 4 * keys * head_cols,
            rows * keys * head_cols // HD,
        ),
        name="own_frame",
    )(query, *kvs)


def earlier_kernel(*refs, chunks):
    info_ref, query_ref, acc_ref, top_ref, total_ref = refs[:5]
    kv_refs = refs[5 : 5 + chunks]
    out_ref = refs[5 + chunks]
    heads = query_ref.shape[1] // HD

    @pl.when(info_ref[0] != 0)
    def _():
        out_ref[...] = (acc_ref[...] / total_ref[...]).astype(BF16)

    @pl.when(info_ref[0] == 0)
    def _():
        for h in range(heads):
            at = slice(h * HD, (h + 1) * HD)
            old_top = top_ref[:, at][:, :1]
            scores, top = attend_parts(query_ref[:, at], kv_refs, at)
            top = jnp.maximum(top, old_top)
            acc, total = weigh_parts(scores, top, kv_refs, at)
            kept = jnp.exp2(old_top - top)
            acc = acc + acc_ref[:, at] * kept
            total = total + total_ref[:, at] * kept
            out_ref[:, at] = (acc / total).astype(BF16)


def earlier_attention(info, query, acc, top, total, kvs):
    rows, head_cols = query.shape
    cols = 256 if head_cols % 256 == 0 else HD
    chunks = len(kvs)
    key_rows = kvs[0].shape[1]
    keys = chunks * key_rows
    by_heads = pl.BlockSpec((rows, cols), lambda j, i: (0, j))
    return pl.pallas_call(
        functools.partial(earlier_kernel, chunks=chunks),
        grid_spec=pltpu.PrefetchScalarGridSpec(
            num_scalar_prefetch=1,
            grid=(head_cols // cols,),
            in_specs=[by_heads] * 4
            + [pl.BlockSpec((2, key_rows, cols), lambda j, i: (0, 0, j))] * chunks,
            out_specs=by_heads,
        ),
        out_shape=jax.ShapeDtypeStruct((rows, head_cols), BF16),
        compiler_params=compiler_params(24),
        cost_estimate=cost(
            8 * rows * keys * head_cols,
            16 * rows * head_cols + 4 * keys * head_cols,
            rows * keys * head_cols // HD,
        ),
        name="earlier_frame",
    )(info, query, acc, top, total, *kvs)


def output_kernel(*refs, piece_counts, half_blocks, aliased):
    parity_ref, resid_ref, gate_ref = refs[:3]
    at = 3
    pieces = []
    for count in piece_counts:
        pieces.append(refs[at : at + count])
        at += count
    size = len(piece_counts)
    own_w = refs[at]
    others = refs[at + 1 : at + 2 * size - 1]
    out_ref, held_ref, w_ref, held_sems, w_sems = refs[at + 2 * size - 1 + aliased :]
    step = pl.program_id(0)
    cols = out_ref.shape[1]
    head_cols, half_width = w_ref.shape[2:]

    def weight_copy(half, k):
        if k == 0:
            column = (parity_ref[0] ^ half) * half_width
            source = own_w.at[:, pl.ds(pl.multiple_of(column, HD), half_width)]
        else:
            source = others[half * (size - 1) + k - 1]
        return pltpu.make_async_copy(source, w_ref.at[half, k], w_sems.at[half, k])

    def held_copies(k):
        row = 0
        for number, part in enumerate(pieces[k]):
            count = part.shape[0]
            yield pltpu.make_async_copy(
                part, held_ref.at[k, pl.ds(row, count)], held_sems.at[k, number]
            )
            row += count

    @pl.when(step == 0)
    def _():
        for k in range(size):
            for copy in held_copies(k):
                copy.start()
        for half in range(2):
            for k in range(size):
                weight_copy(half, k).start()
        for k in range(size):
            for copy in held_copies(k):
                copy.wait()

    for half in range(2):

        @pl.when(step == half * half_blocks)
        def _():
            for k in range(size):
                weight_copy(half, k).wait()

    half = step // half_blocks
    inside = pl.ds(pl.multiple_of(lax.rem(step, half_blocks) * cols, HD), cols)
    update = jnp.dot(held_ref[0], w_ref[half, 0, :, inside], preferred_element_type=F32)
    for k in range(1, size):
        update += jnp.dot(held_ref[k], w_ref[half, k, :, inside], preferred_element_type=F32)
    out_ref[...] = (resid_ref[...].astype(F32) + gate_ref[...] * update).astype(BF16)


def output_projection(parity, resid, gate, pieces, own_w, mine, theirs, out_rows, chunk, into):
    head_cols, width = own_w.shape
    rows = resid.shape[0]
    size = len(pieces)
    cols = 256 if (width // 2) % 256 == 0 else HD
    half_blocks = width // 2 // cols
    parts = max(len(p) for p in pieces)
    flat = [part for group in pieces for part in group]
    alias = [] if into is None else [into]
    held = [in_hbm(array) for array in [own_w, *mine, *theirs, *alias]]
    operands = [parity, resid, gate, *flat, *held]

    def column(j, parity):
        return ((j // half_blocks) ^ parity[0]) * half_blocks + j % half_blocks

    return pl.pallas_call(
        functools.partial(
            output_kernel,
            piece_counts=tuple(len(p) for p in pieces),
            half_blocks=half_blocks,
            aliased=len(alias),
        ),
        grid_spec=pltpu.PrefetchScalarGridSpec(
            num_scalar_prefetch=1,
            grid=(2 * half_blocks,),
            in_specs=[
                pl.BlockSpec((rows, cols), lambda j, p: (0, column(j, p))),
                pl.BlockSpec((1, cols), lambda j, p: (0, column(j, p))),
            ]
            + [ANY] * (len(operands) - 3),
            out_specs=pl.BlockSpec((rows, cols), lambda j, p: (chunk, column(j, p))),
            scratch_shapes=[
                pltpu.VMEM((size, rows, head_cols), BF16),
                pltpu.VMEM((2, size, head_cols, width // 2), BF16),
                pltpu.SemaphoreType.DMA((size, parts)),
                pltpu.SemaphoreType.DMA((2, size)),
            ],
        ),
        out_shape=pltpu.HBM((out_rows, width), BF16),
        input_output_aliases={} if into is None else {len(operands) - 1: 0},
        compiler_params=compiler_params(36),
        cost_estimate=cost(
            2 * rows * width * head_cols * size,
            4 * rows * width + 2 * head_cols * width * size,
        ),
        name="output_projection",
    )(*operands)


def send(block, move, queue_size, tensor_size, frames=None):
    pairs = []
    for q in range(queue_size) if frames is None else frames:
        for t in range(tensor_size):
            to_q, to_t = move(q, t)
            pairs.append((q * tensor_size + t, to_q * tensor_size + to_t))
    return lax.ppermute(block, AXES, pairs)


def gather_pieces(block, queue_size, tensor_size, frames=None, after=None):
    half = tensor_size // 2

    def low(q, t):
        return q, t ^ 1

    def high(j):
        return lambda q, t: (q, (t // 2 - j) % half * 2 + t % 2)

    args = (queue_size, tensor_size, frames)
    rows = block.shape[0] // 2
    near = send(block, low, *args)
    if after is not None:
        block, _ = lax.optimization_barrier((block, after))
    far = [send(block, high(j), *args) for j in range(1, half)]
    pieces = [[block], [near]]
    for j in range(1, half):
        top = send(near[:rows], high(j), *args)
        bottom = send(far[j - 1][rows:], low, *args)
        pieces += [[far[j - 1]], [top, bottom]]
    return pieces


def body(
    latents, levels, mod_table, step_size, qkv_weight, q_gain, k_gain, out_weight, fresh_noise
):
    queue_size = lax.axis_size("queue")
    tensor_size = lax.axis_size("tensor")
    rows, width = latents.shape[1:]
    mesh_sizes = (queue_size, tensor_size)
    queue_index = lax.axis_index("queue")
    tensor_index = lax.axis_index("tensor")
    parity = (queue_index % 2).astype(jnp.int32)[None]

    def ahead(block):
        return send(block, lambda q, t: (q + 1, t), *mesh_sizes, range(queue_size - 1))

    def sibling(block):
        return send(block, lambda q, t: (q ^ 1, t), *mesh_sizes)

    def noise_pieces(block):
        return [
            send(block, lambda q, t: (q, (t - d) % tensor_size), *mesh_sizes, [0])
            for d in range(1, tensor_size)
        ]

    frame = ahead(latents[0])
    noise = noise_pieces(fresh_noise)
    half_weight = lax.dynamic_slice(
        out_weight, (0, parity[0] * (width // 2)), (out_weight.shape[0], width // 2)
    )
    gathered = gather_pieces(half_weight, *mesh_sizes, after=noise)[1:]
    mine = [jnp.concatenate(parts, axis=0) if len(parts) > 1 else parts[0] for parts in gathered]
    theirs = [sibling(block) for block in mine]

    def modulation(level):
        row = lax.dynamic_slice(mod_table, (level, 0), (1, 3 * width)).astype(F32)
        rate = lax.dynamic_slice(step_size, (level,), (1,))[:, None]
        return row[:, :width], 1.0 + row[:, width : 2 * width], rate * row[:, 2 * width :]

    shift, scale1, gate = modulation(levels[0])
    info = jnp.stack([(queue_index == 0).astype(jnp.int32), tensor_index.astype(jnp.int32)])
    gains = jnp.stack([q_gain * SCORE_SCALE, k_gain])

    chunk_rows = rows // CHUNKS
    frames = [(frame, c * chunk_rows) for c in range(CHUNKS)]
    for step_index in range(STEPS):
        final = step_index == STEPS - 1
        made = [
            project_qkv(
                info,
                scale1,
                shift,
                qkv_weight,
                gains,
                part,
                first_row,
                chunk_rows,
                (fresh_noise, step_index, noise, c * chunk_rows),
            )
            for c, (part, first_row) in enumerate(frames)
        ]
        kvs = [kv for kv, _, _ in made]
        earlier = [ahead(kv) for kv in kvs]
        own = [own_attention(query, kvs) for _, query, _ in made]
        attended = [
            earlier_attention(info, query, *parts, earlier)
            for (_, query, _), parts in zip(made, own)
        ]
        resid = [state for _, _, state in made]
        if final:
            pieces = [gather_pieces(block, *mesh_sizes) for block in attended]
            result = None
            for c in range(CHUNKS):
                result = output_projection(
                    parity, resid[c], gate, pieces[c], out_weight, mine, theirs, rows, c, result
                )
        else:
            attended = [ahead(block) for block in attended]
            attended, resid = lax.optimization_barrier((attended, resid))
            resid = [ahead(state) for state in resid]
            pieces = [
                gather_pieces(block, *mesh_sizes, range(1, queue_size)) for block in attended
            ]
            sent_level, _ = lax.optimization_barrier((levels, kvs))
            arriving_gate = modulation(ahead(sent_level)[0])[2]
            frames = [
                (
                    output_projection(
                        parity,
                        resid[c],
                        arriving_gate,
                        pieces[c],
                        out_weight,
                        mine,
                        theirs,
                        chunk_rows,
                        0,
                        None,
                    ),
                    0,
                )
                for c in range(CHUNKS)
            ]
    return result[None]


def solution(mesh):
    return jax.shard_map(
        body,
        mesh=mesh,
        in_specs=(
            P("queue", None, None),
            P("queue"),
            P(),
            P(),
            P(None, None, "tensor"),
            P(),
            P(),
            P("tensor", None),
            P(None, "tensor", None),
        ),
        out_specs=P("queue", None, None),
        check_vma=False,
    )
```

```python
import functools
import math

import jax
import jax.numpy as jnp
from jax import lax
from jax.experimental import pallas as pl
from jax.experimental.pallas import tpu as pltpu
from jax.sharding import PartitionSpec as P

HD = 128
STEPS = 2
CHUNKS = 2
EPS = 1e-6
AXES = ("queue", "tensor")
F32 = jnp.float32
BF16 = jnp.bfloat16
SCORE_SCALE = math.log2(math.e) / math.sqrt(HD)
ANY = pl.BlockSpec(memory_space=pl.ANY)


def compiler_params(mib):
    return pltpu.CompilerParams(vmem_limit_bytes=mib * 2**20)


def in_hbm(array):
    return pltpu.with_memory_space_constraint(array, pltpu.HBM)


def cost(flops, nbytes, transcendentals=0):
    return pl.CostEstimate(
        flops=int(flops) // 1000,
        bytes_accessed=int(nbytes) // 1000,
        transcendentals=int(transcendentals) // 1000,
    )


def head_normalized(values, gain):
    heads = []
    for h in range(values.shape[1] // HD):
        head = values[:, h * HD : (h + 1) * HD]
        mean = jnp.mean(head * head, axis=-1, keepdims=True)
        heads.append((head * lax.rsqrt(mean + EPS) * gain).astype(BF16))
    return heads[0] if len(heads) == 1 else jnp.concatenate(heads, axis=1)


def tile_cols(head_cols):
    return 256 if head_cols % 256 == 0 else HD


def weight_copies(w_any, part, w_ref, w_sems):
    splits = w_sems.shape[0]
    split_rows = w_ref.shape[0] // splits
    for i in range(splits):
        at = pl.ds(i * split_rows, split_rows)
        yield pltpu.make_async_copy(w_any.at[part, at], w_ref.at[at], w_sems.at[i])


def key_kernel(*refs, tensor_size, noise_step):
    info_ref, scale_ref, shift_ref, gain_ref, w_any, z_any, noise_any = refs[:7]
    piece_refs = refs[7 : 7 + tensor_size - 1]
    key_ref, normed_ref, state_ref, w_ref, sem, w_sems = refs[6 + tensor_size :]
    step = pl.program_id(0)
    rows = state_ref.shape[0]
    piece_rows = noise_any.shape[1]
    cols = key_ref.shape[1]

    @pl.when(step == 0)
    def _():
        for copy in weight_copies(w_any, 1, w_ref, w_sems):
            copy.start()

        @pl.when(info_ref[0] == 0)
        def _():
            copy = pltpu.make_async_copy(z_any, state_ref, sem.at[0])
            copy.start()
            copy.wait()

        @pl.when(info_ref[0] != 0)
        def _():
            for block in range(tensor_size):
                away = lax.rem(block + tensor_size - info_ref[1], tensor_size)
                for d in range(tensor_size):
                    source = noise_any if d == 0 else piece_refs[d - 1]

                    @pl.when(away == d)
                    def _():
                        copy = pltpu.make_async_copy(
                            source.at[noise_step],
                            state_ref.at[pl.ds(block * piece_rows, piece_rows)],
                            sem.at[0],
                        )
                        copy.start()
                        copy.wait()

        def one(i, carry):
            at = pl.ds(pl.multiple_of(i * 16, 16), 16)
            state = state_ref[at, :].astype(F32)
            mean = jnp.mean(state * state, axis=-1, keepdims=True)
            state = state * lax.rsqrt(mean + EPS) * scale_ref[...] + shift_ref[...]
            normed_ref[at, :] = state.astype(BF16)
            return carry

        lax.fori_loop(0, rows // 16, one, 0, unroll=4)
        for copy in weight_copies(w_any, 1, w_ref, w_sems):
            copy.wait()

    at = pl.ds(pl.multiple_of(step * cols, HD), cols)
    product = jnp.dot(normed_ref[...], w_ref[:, at], preferred_element_type=F32)
    key_ref[...] = head_normalized(product, gain_ref[1:2])


def project_keys(info, scale1, shift, gains, qkv_weight, z, noise_all, noise_step, noise_pieces):
    rows, width = z.shape
    head_cols = qkv_weight.shape[2]
    cols = tile_cols(head_cols)
    tensor_size = len(noise_pieces) + 1
    return pl.pallas_call(
        functools.partial(key_kernel, tensor_size=tensor_size, noise_step=noise_step),
        grid_spec=pltpu.PrefetchScalarGridSpec(
            num_scalar_prefetch=1,
            grid=(head_cols // cols,),
            in_specs=[
                pl.BlockSpec((1, width), lambda j, i: (0, 0)),
                pl.BlockSpec((1, width), lambda j, i: (0, 0)),
                pl.BlockSpec((2, HD), lambda j, i: (0, 0)),
            ]
            + [ANY] * (2 + tensor_size),
            out_specs=[
                pl.BlockSpec((rows, cols), lambda j, i: (0, j)),
                pl.BlockSpec((rows, width), lambda j, i: (0, 0)),
                pl.BlockSpec((rows, width), lambda j, i: (0, 0)),
            ],
            scratch_shapes=[
                pltpu.VMEM((width, head_cols), BF16),
                pltpu.SemaphoreType.DMA((1,)),
                pltpu.SemaphoreType.DMA((4,)),
            ],
        ),
        out_shape=[
            jax.ShapeDtypeStruct((rows, head_cols), BF16),
            jax.ShapeDtypeStruct((rows, width), BF16),
            pltpu.HBM((rows, width), BF16),
        ],
        compiler_params=compiler_params(26),
        cost_estimate=cost(
            2 * rows * width * head_cols,
            6 * rows * width + 2 * rows * head_cols + 2 * width * head_cols,
        ),
        name="norm_keys",
    )(
        info,
        scale1,
        shift,
        gains,
        *[in_hbm(a) for a in (qkv_weight, z, noise_all)],
        *noise_pieces,
    )


def value_kernel(normed_ref, w_any, value_ref, w_ref, w_sems):
    step = pl.program_id(0)
    cols = value_ref.shape[1]

    @pl.when(step == 0)
    def _():
        for copy in weight_copies(w_any, 2, w_ref, w_sems):
            copy.start()
        for copy in weight_copies(w_any, 2, w_ref, w_sems):
            copy.wait()

    at = pl.ds(pl.multiple_of(step * cols, HD), cols)
    product = jnp.dot(normed_ref[...], w_ref[:, at], preferred_element_type=F32)
    value_ref[...] = product.astype(BF16)


def project_values(normed, qkv_weight):
    rows, width = normed.shape
    head_cols = qkv_weight.shape[2]
    cols = tile_cols(head_cols)
    return pl.pallas_call(
        value_kernel,
        grid=(head_cols // cols,),
        in_specs=[pl.BlockSpec((rows, width), lambda j: (0, 0)), ANY],
        out_specs=pl.BlockSpec((rows, cols), lambda j: (0, j)),
        scratch_shapes=[
            pltpu.VMEM((width, head_cols), BF16),
            pltpu.SemaphoreType.DMA((4,)),
        ],
        out_shape=jax.ShapeDtypeStruct((rows, head_cols), BF16),
        compiler_params=compiler_params(20),
        cost_estimate=cost(
            2 * rows * width * head_cols,
            2 * rows * width + 2 * rows * head_cols + 2 * width * head_cols,
        ),
        name="values",
    )(normed, in_hbm(qkv_weight))


def attend(query, key):
    return lax.dot_general(query, key, (((1,), (1,)), ((), ())), preferred_element_type=F32)


def weigh(scores, top, values):
    weights = jnp.exp2(scores - top).astype(BF16)
    extended = jnp.concatenate([values, jnp.ones_like(values)], axis=1)
    total = jnp.dot(weights, extended, preferred_element_type=F32)
    return total[:, :HD], total[:, HD:]


def own_kernel(
    gain_ref, normed_ref, key_ref, value_ref, w_any,
    query_ref, acc_ref, top_ref, total_ref, w_ref, w_sems,
):
    step = pl.program_id(0)
    cols = query_ref.shape[1]

    @pl.when(step == 0)
    def _():
        for copy in weight_copies(w_any, 0, w_ref, w_sems):
            copy.start()
        for copy in weight_copies(w_any, 0, w_ref, w_sems):
            copy.wait()

    inside = pl.ds(pl.multiple_of(step * cols, HD), cols)
    product = jnp.dot(normed_ref[...], w_ref[:, inside], preferred_element_type=F32)
    query = head_normalized(product, gain_ref[0:1])
    query_ref[...] = query
    for h in range(cols // HD):
        at = slice(h * HD, (h + 1) * HD)
        scores = attend(query[:, at], key_ref[:, at])
        top = jnp.max(scores, axis=-1, keepdims=True)
        acc, total = weigh(scores, top, value_ref[:, at])
        acc_ref[:, at] = acc
        total_ref[:, at] = total
        top_ref[:, at] = jnp.broadcast_to(top, acc.shape)


def own_attention(gains, normed, qkv_weight, key, value):
    rows, width = normed.shape
    head_cols = qkv_weight.shape[2]
    cols = tile_cols(head_cols)
    by_heads = pl.BlockSpec((rows, cols), lambda j: (0, j))
    return pl.pallas_call(
        own_kernel,
        grid=(head_cols // cols,),
        in_specs=[
            pl.BlockSpec((2, HD), lambda j: (0, 0)),
            pl.BlockSpec((rows, width), lambda j: (0, 0)),
            by_heads,
            by_heads,
            ANY,
        ],
        out_specs=[by_heads] * 4,
        scratch_shapes=[
            pltpu.VMEM((width, head_cols), BF16),
            pltpu.SemaphoreType.DMA((4,)),
        ],
        out_shape=[jax.ShapeDtypeStruct((rows, head_cols), BF16)]
        + [jax.ShapeDtypeStruct((rows, head_cols), F32)] * 3,
        compiler_params=compiler_params(32),
        cost_estimate=cost(
            2 * rows * width * head_cols + 8 * rows * rows * head_cols,
            2 * rows * width + 18 * rows * head_cols + 2 * width * head_cols,
            rows * rows * head_cols // HD,
        ),
        name="queries_own_frame",
    )(gains, normed, key, value, in_hbm(qkv_weight))


def earlier_kernel(*refs, chunks):
    info_ref, query_ref, acc_ref, top_ref, total_ref, key_ref, value_ref = refs[:7]
    out_refs = refs[7:]
    rows = query_ref.shape[0] // chunks

    def store(at, result):
        for c, out_ref in enumerate(out_refs):
            out_ref[:, at] = result[c * rows : (c + 1) * rows]

    @pl.when(info_ref[0] != 0)
    def _():
        store(slice(None), (acc_ref[...] / total_ref[...]).astype(BF16))

    @pl.when(info_ref[0] == 0)
    def _():
        for h in range(query_ref.shape[1] // HD):
            at = slice(h * HD, (h + 1) * HD)
            old_top = top_ref[:, at][:, :1]
            scores = attend(query_ref[:, at], key_ref[:, at])
            top = jnp.maximum(jnp.max(scores, axis=-1, keepdims=True), old_top)
            acc, total = weigh(scores, top, value_ref[:, at])
            kept = jnp.exp2(old_top - top)
            acc = acc + acc_ref[:, at] * kept
            total = total + total_ref[:, at] * kept
            store(at, (acc / total).astype(BF16))


def earlier_attention(info, query, acc, top, total, key, value, chunks):
    rows, head_cols = query.shape
    cols = tile_cols(head_cols)
    return pl.pallas_call(
        functools.partial(earlier_kernel, chunks=chunks),
        grid_spec=pltpu.PrefetchScalarGridSpec(
            num_scalar_prefetch=1,
            grid=(head_cols // cols,),
            in_specs=[pl.BlockSpec((rows, cols), lambda j, i: (0, j))] * 6,
            out_specs=[pl.BlockSpec((rows // chunks, cols), lambda j, i: (0, j))] * chunks,
        ),
        out_shape=[jax.ShapeDtypeStruct((rows // chunks, head_cols), BF16)] * chunks,
        compiler_params=compiler_params(24),
        cost_estimate=cost(
            8 * rows * rows * head_cols,
            20 * rows * head_cols,
            rows * rows * head_cols // HD,
        ),
        name="earlier_frame",
    )(info, query, acc, top, total, key, value)


def output_kernel(*refs, part_counts, whole_weights, half_blocks, last):
    parity_ref = refs[0]
    at = 1
    acc_in = resid_ref = gate_ref = None
    if last:
        acc_in, resid_ref, gate_ref = refs[1:4]
        at = 4
    pieces = []
    for count in part_counts:
        pieces.append(refs[at : at + count])
        at += count
    size = len(part_counts)
    wholes = refs[at : at + whole_weights]
    at += whole_weights
    halves = refs[at : at + 2 * (size - whole_weights)]
    at += 2 * (size - whole_weights)
    out_ref, held_ref, w_ref, held_sems, w_sems = refs[at:]
    step = pl.program_id(0)
    cols = out_ref.shape[1]
    half_width = w_ref.shape[3]

    def weight_copy(half, k):
        if k < whole_weights:
            column = (parity_ref[0] ^ half) * half_width
            source = wholes[k].at[:, pl.ds(pl.multiple_of(column, HD), half_width)]
        else:
            source = halves[half * (size - whole_weights) + k - whole_weights]
        return pltpu.make_async_copy(source, w_ref.at[half, k], w_sems.at[half, k])

    def held_copies(k):
        row = 0
        for number, part in enumerate(pieces[k]):
            count = part.shape[0]
            yield pltpu.make_async_copy(
                part, held_ref.at[k, pl.ds(row, count)], held_sems.at[k, number]
            )
            row += count

    @pl.when(step == 0)
    def _():
        for k in range(size):
            for copy in held_copies(k):
                copy.start()
        for half in range(2):
            for k in range(size):
                weight_copy(half, k).start()
        for k in range(size):
            for copy in held_copies(k):
                copy.wait()

    for half in range(2):

        @pl.when(step == half * half_blocks)
        def _():
            for k in range(size):
                weight_copy(half, k).wait()

    half = step // half_blocks
    inside = pl.ds(pl.multiple_of(lax.rem(step, half_blocks) * cols, HD), cols)
    update = acc_in[...] if last else None
    for k in range(size):
        term = jnp.dot(held_ref[k], w_ref[half, k, :, inside], preferred_element_type=F32)
        update = term if update is None else update + term
    if last:
        update = resid_ref[...].astype(F32) + gate_ref[...] * update
    out_ref[...] = update.astype(out_ref.dtype)


def output_projection(parity, pieces, wholes, mine, theirs, finish=None):
    head_cols, half_width = mine[0].shape
    rows = sum(part.shape[0] for part in pieces[0])
    width = 2 * half_width
    size = len(pieces)
    cols = tile_cols(half_width)
    half_blocks = half_width // cols
    parts = max(len(p) for p in pieces)
    flat = [part for group in pieces for part in group]
    weights = [in_hbm(array) for array in [*wholes, *mine, *theirs]]
    last = finish is not None

    def column(j, parity):
        return 0, ((j // half_blocks) ^ parity[0]) * half_blocks + j % half_blocks

    block = pl.BlockSpec((rows, cols), column)
    return pl.pallas_call(
        functools.partial(
            output_kernel,
            part_counts=tuple(len(p) for p in pieces),
            whole_weights=len(wholes),
            half_blocks=half_blocks,
            last=last,
        ),
        grid_spec=pltpu.PrefetchScalarGridSpec(
            num_scalar_prefetch=1,
            grid=(2 * half_blocks,),
            in_specs=([block, block, pl.BlockSpec((1, cols), column)] if last else [])
            + [ANY] * (len(flat) + len(weights)),
            out_specs=block,
            scratch_shapes=[
                pltpu.VMEM((size, rows, head_cols), BF16),
                pltpu.VMEM((2, size, head_cols, half_width), BF16),
                pltpu.SemaphoreType.DMA((size, parts)),
                pltpu.SemaphoreType.DMA((2, size)),
            ],
        ),
        out_shape=(pltpu.HBM if last else jax.ShapeDtypeStruct)((rows, width), BF16 if last else F32),
        compiler_params=compiler_params(16 if last else 28),
        cost_estimate=cost(
            2 * rows * width * head_cols * size,
            (8 if last else 4) * rows * width + 2 * head_cols * width * size,
        ),
        name="projection_end" if last else "projection_start",
    )(parity, *(finish if last else ()), *flat, *weights)


def send(block, move, queue_size, tensor_size, frames=None):
    pairs = []
    for q in range(queue_size) if frames is None else frames:
        for t in range(tensor_size):
            to_q, to_t = move(q, t)
            pairs.append((q * tensor_size + t, to_q * tensor_size + to_t))
    return lax.ppermute(block, AXES, pairs)


def gather_pieces(block, queue_size, tensor_size, frames=None, after=None):
    half = tensor_size // 2

    def low(q, t):
        return q, t ^ 1

    def high(j):
        return lambda q, t: (q, (t // 2 - j) % half * 2 + t % 2)

    args = (queue_size, tensor_size, frames)
    rows = block.shape[0] // 2
    near = send(block, low, *args)
    if after is not None:
        block, _ = lax.optimization_barrier((block, after))
    far = [send(block, high(j), *args) for j in range(1, half)]
    corners = []
    for j in range(1, half):
        top = send(near[:rows], high(j), *args)
        bottom = send(far[j - 1][rows:], low, *args)
        corners.append([top, bottom])
    return [near, *far], corners


def body(
    latents, levels, mod_table, step_size, qkv_weight, q_gain, k_gain, out_weight, fresh_noise
):
    queue_size = lax.axis_size("queue")
    tensor_size = lax.axis_size("tensor")
    rows, width = latents.shape[1:]
    mesh_sizes = (queue_size, tensor_size)
    queue_index = lax.axis_index("queue")
    tensor_index = lax.axis_index("tensor")
    is_last = queue_index == queue_size - 1
    parity = (queue_index % 2).astype(jnp.int32)[None]

    def ring(block):
        return send(block, lambda q, t: ((q + 1) % queue_size, t), *mesh_sizes)

    def sibling(block):
        return send(block, lambda q, t: (q ^ 1, t), *mesh_sizes)

    worked_level = send(levels, lambda q, t: ((q - 1) % queue_size, t), *mesh_sizes)[0]
    noise_pieces = [
        send(
            fresh_noise,
            lambda q, t: (q, (t - d) % tensor_size),
            *mesh_sizes,
            [queue_size - 1],
        )
        for d in range(1, tensor_size)
    ]
    half_weight = lax.dynamic_slice(
        out_weight, (0, parity[0] * (width // 2)), (out_weight.shape[0], width // 2)
    )
    half_weight, latents = lax.optimization_barrier((half_weight, latents))
    mine, mine_corners = gather_pieces(half_weight, *mesh_sizes, after=noise_pieces)
    theirs = [sibling(block) for block in mine]
    mine_corners = [jnp.concatenate(parts, axis=0) for parts in mine_corners]
    theirs_corners = [sibling(block) for block in mine_corners]

    def modulation(level):
        row = lax.dynamic_slice(mod_table, (level, 0), (1, 3 * width)).astype(F32)
        rate = lax.dynamic_slice(step_size, (level,), (1,))[:, None]
        return row[:, :width], 1.0 + row[:, width : 2 * width], rate * row[:, 2 * width :]

    shift, scale1, _ = modulation(worked_level)
    _, _, gate = modulation(levels[0])
    info = jnp.stack([is_last.astype(jnp.int32), tensor_index.astype(jnp.int32)])
    gains = jnp.stack([q_gain * SCORE_SCALE, k_gain])

    frame = latents[0]
    for step_index in range(STEPS):
        final = step_index == STEPS - 1
        key, normed, state = project_keys(
            info, scale1, shift, gains, qkv_weight, frame, fresh_noise, step_index, noise_pieces
        )
        earlier_key = ring(key)
        value = project_values(normed, qkv_weight)
        earlier_value = ring(value)
        normed, earlier_key = lax.optimization_barrier((normed, earlier_key))
        query, *own = own_attention(gains, normed, qkv_weight, key, value)
        if not final:
            query, mine = lax.optimization_barrier((query, mine))
        attended = earlier_attention(
            info, query, *own, earlier_key, earlier_value, CHUNKS
        )
        attended = [ring(block) for block in attended]
        targets = range(queue_size) if final else range(queue_size - 1)
        gathered = [gather_pieces(block, *mesh_sizes, targets) for block in attended]
        sent_state, _ = lax.optimization_barrier((state, attended))
        resid = ring(sent_state)
        direct = [attended] + [list(p) for p in zip(*[near for near, _ in gathered])]
        corners = [
            [half for parts in p for half in parts] for p in zip(*[c for _, c in gathered])
        ]
        begun = output_projection(parity, direct, [out_weight], mine, theirs)
        frame = output_projection(
            parity, corners, [], mine_corners, theirs_corners, (begun, resid, gate)
        )
    return frame[None]


def solution(mesh):
    return jax.shard_map(
        body,
        mesh=mesh,
        in_specs=(
            P("queue", None, None),
            P("queue"),
            P(),
            P(),
            P(None, None, "tensor"),
            P(),
            P(),
            P("tensor", None),
            P(None, "tensor", None),
        ),
        out_specs=P("queue", None, None),
        check_vma=False,
    )
```

```python
import functools
import math

import jax
import jax.numpy as jnp
from jax import lax
from jax.experimental import pallas as pl
from jax.experimental.pallas import tpu as pltpu
from jax.sharding import PartitionSpec as P

HD = 128
STEPS = 2
CHUNKS = 2
EPS = 1e-6
AXES = ("queue", "tensor")
F32 = jnp.float32
BF16 = jnp.bfloat16
SCORE_SCALE = math.log2(math.e) / math.sqrt(HD)
ANY = pl.BlockSpec(memory_space=pl.ANY)


def compiler_params(mib):
    return pltpu.CompilerParams(vmem_limit_bytes=mib * 2**20)


def in_hbm(array):
    return pltpu.with_memory_space_constraint(array, pltpu.HBM)


def cost(flops, nbytes, transcendentals=0, share=1000):
    return pl.CostEstimate(
        flops=int(flops) // share,
        bytes_accessed=int(nbytes) // share,
        transcendentals=int(transcendentals) // share,
    )


def head_normalized(values, gain):
    heads = []
    for h in range(values.shape[1] // HD):
        head = values[:, h * HD : (h + 1) * HD]
        mean = jnp.mean(head * head, axis=-1, keepdims=True)
        heads.append((head * lax.rsqrt(mean + EPS) * gain).astype(BF16))
    return heads[0] if len(heads) == 1 else jnp.concatenate(heads, axis=1)


def tile_cols(head_cols):
    return 256 if head_cols % 256 == 0 else HD


def weight_copies(w_any, part, w_ref, w_sems):
    splits = w_sems.shape[0]
    split_rows = w_ref.shape[0] // splits
    for i in range(splits):
        at = pl.ds(i * split_rows, split_rows)
        yield pltpu.make_async_copy(w_any.at[part, at], w_ref.at[at], w_sems.at[i])


def key_kernel(*refs, tensor_size):
    info_ref, scale_ref, shift_ref, gain_ref, w_any, z_any, noise_any = refs[:7]
    piece_refs = refs[7 : 7 + tensor_size - 1]
    key_ref, normed_any, state_any = refs[6 + tensor_size : 9 + tensor_size]
    state_ref, normed_ref, inverse_ref, w_ref, sem, out_sems, w_sems = refs[9 + tensor_size :]
    step = pl.program_id(0)
    rows = state_ref.shape[0]
    piece_rows = noise_any.shape[0]
    cols = key_ref.shape[1]
    state_copy = pltpu.make_async_copy(state_ref, state_any, out_sems.at[0])
    normed_copy = pltpu.make_async_copy(normed_ref, normed_any, out_sems.at[1])

    @pl.when(step == 0)
    def _():
        @pl.when(info_ref[0] == 0)
        def _():
            copy = pltpu.make_async_copy(z_any, state_ref, sem.at[0])
            copy.start()
            for weight_copy in weight_copies(w_any, 1, w_ref, w_sems):
                weight_copy.start()
            copy.wait()

        @pl.when(info_ref[0] != 0)
        def _():
            for weight_copy in weight_copies(w_any, 1, w_ref, w_sems):
                weight_copy.start()
            for block in range(tensor_size):
                away = lax.rem(block + tensor_size - info_ref[1], tensor_size)
                for d in range(tensor_size):
                    source = noise_any if d == 0 else piece_refs[d - 1]

                    @pl.when(away == d)
                    def _():
                        copy = pltpu.make_async_copy(
                            source,
                            state_ref.at[pl.ds(block * piece_rows, piece_rows)],
                            sem.at[0],
                        )
                        copy.start()
                        copy.wait()

        state_copy.start()

        def measure(i, carry):
            at = pl.ds(pl.multiple_of(i * 16, 16), 16)
            state = state_ref[at, :].astype(F32)
            mean = jnp.mean(state * state, axis=-1, keepdims=True)
            inverse_ref[at, :] = jnp.broadcast_to(lax.rsqrt(mean + EPS), (16, HD))
            return carry

        def apply(i, carry):
            at = pl.ds(pl.multiple_of(i * 16, 16), 16)
            inverse = inverse_ref[at, :][:, :1]
            state = state_ref[at, :].astype(F32) * inverse
            normed_ref[at, :] = (state * scale_ref[...] + shift_ref[...]).astype(BF16)
            return carry

        lax.fori_loop(0, rows // 16, measure, 0, unroll=4)
        lax.fori_loop(0, rows // 16, apply, 0, unroll=2)
        normed_copy.start()
        for copy in weight_copies(w_any, 1, w_ref, w_sems):
            copy.wait()

    at = pl.ds(pl.multiple_of(step * cols, HD), cols)
    product = jnp.dot(normed_ref[...], w_ref[:, at], preferred_element_type=F32)
    key_ref[...] = head_normalized(product, gain_ref[1:2])

    @pl.when(step == pl.num_programs(0) - 1)
    def _():
        state_copy.wait()
        normed_copy.wait()


def project_keys(info, scale1, shift, gains, qkv_weight, z, noise, noise_pieces):
    rows, width = z.shape
    head_cols = qkv_weight.shape[2]
    cols = tile_cols(head_cols)
    tensor_size = len(noise_pieces) + 1
    return pl.pallas_call(
        functools.partial(key_kernel, tensor_size=tensor_size),
        grid_spec=pltpu.PrefetchScalarGridSpec(
            num_scalar_prefetch=1,
            grid=(head_cols // cols,),
            in_specs=[
                pl.BlockSpec((1, width), lambda j, i: (0, 0)),
                pl.BlockSpec((1, width), lambda j, i: (0, 0)),
                pl.BlockSpec((2, HD), lambda j, i: (0, 0)),
            ]
            + [ANY] * (2 + tensor_size),
            out_specs=[pl.BlockSpec((rows, cols), lambda j, i: (0, j)), ANY, ANY],
            scratch_shapes=[
                pltpu.VMEM((rows, width), BF16),
                pltpu.VMEM((rows, width), BF16),
                pltpu.VMEM((rows, HD), F32),
                pltpu.VMEM((width, head_cols), BF16),
                pltpu.SemaphoreType.DMA((1,)),
                pltpu.SemaphoreType.DMA((2,)),
                pltpu.SemaphoreType.DMA((4,)),
            ],
        ),
        out_shape=[
            jax.ShapeDtypeStruct((rows, head_cols), BF16),
            jax.ShapeDtypeStruct((rows, width), BF16),
            pltpu.HBM((rows, width), BF16),
        ],
        compiler_params=compiler_params(26),
        cost_estimate=cost(
            2 * rows * width * head_cols,
            6 * rows * width + 2 * rows * head_cols + 2 * width * head_cols,
        ),
        name="norm_keys",
    )(
        info,
        scale1,
        shift,
        gains,
        *[in_hbm(a) for a in (qkv_weight, z)],
        noise,
        *noise_pieces,
    )


def value_kernel(normed_ref, w_any, value_ref, w_ref, w_sems):
    step = pl.program_id(0)
    cols = value_ref.shape[1]

    @pl.when(step == 0)
    def _():
        for copy in weight_copies(w_any, 2, w_ref, w_sems):
            copy.start()
        for copy in weight_copies(w_any, 2, w_ref, w_sems):
            copy.wait()

    at = pl.ds(pl.multiple_of(step * cols, HD), cols)
    product = jnp.dot(normed_ref[...], w_ref[:, at], preferred_element_type=F32)
    value_ref[...] = product.astype(BF16)


def project_values(normed, qkv_weight):
    rows, width = normed.shape
    head_cols = qkv_weight.shape[2]
    cols = tile_cols(head_cols)
    return pl.pallas_call(
        value_kernel,
        grid=(head_cols // cols,),
        in_specs=[pl.BlockSpec((rows, width), lambda j: (0, 0)), ANY],
        out_specs=pl.BlockSpec((rows, cols), lambda j: (0, j)),
        scratch_shapes=[
            pltpu.VMEM((width, head_cols), BF16),
            pltpu.SemaphoreType.DMA((4,)),
        ],
        out_shape=jax.ShapeDtypeStruct((rows, head_cols), BF16),
        compiler_params=compiler_params(20),
        cost_estimate=cost(
            2 * rows * width * head_cols,
            2 * rows * width + 2 * rows * head_cols + 2 * width * head_cols,
        ),
        name="values",
    )(normed, in_hbm(qkv_weight))


def attend(query, key):
    return lax.dot_general(query, key, (((1,), (1,)), ((), ())), preferred_element_type=F32)


def weigh(scores, top, values):
    weights = jnp.exp2(scores - top).astype(BF16)
    extended = jnp.concatenate([values, jnp.ones_like(values)], axis=1)
    total = jnp.dot(weights, extended, preferred_element_type=F32)
    return total[:, :HD], total[:, HD:]


def attention_tiles(query, key_ref, value_ref, finish):
    rows, cols = query.shape
    tile = math.gcd(rows, 256)
    waiting = None
    for h in range(cols // HD):
        at = slice(h * HD, (h + 1) * HD)
        for r in range(rows // tile):
            row = slice(r * tile, (r + 1) * tile)
            scores = attend(query[row, at], key_ref[:, at])
            if waiting is not None:
                finish(*waiting)
            waiting = (scores, row, at)
    finish(*waiting)


def own_kernel(
    gain_ref, normed_ref, key_ref, value_ref, w_any,
    query_ref, acc_ref, top_ref, total_ref, w_ref, w_sems,
):
    step = pl.program_id(0)
    cols = query_ref.shape[1]

    @pl.when(step == 0)
    def _():
        for copy in weight_copies(w_any, 0, w_ref, w_sems):
            copy.start()
        for copy in weight_copies(w_any, 0, w_ref, w_sems):
            copy.wait()

    inside = pl.ds(pl.multiple_of(step * cols, HD), cols)
    product = jnp.dot(normed_ref[...], w_ref[:, inside], preferred_element_type=F32)
    query = head_normalized(product, gain_ref[0:1])
    query_ref[...] = query

    def finish(scores, row, at):
        top = jnp.max(scores, axis=-1, keepdims=True)
        acc, total = weigh(scores, top, value_ref[:, at])
        acc_ref[row, at] = acc
        total_ref[row, at] = total
        top_ref[row, at] = jnp.broadcast_to(top, acc.shape)

    attention_tiles(query, key_ref, value_ref, finish)


def own_attention(gains, normed, qkv_weight, key, value):
    rows, width = normed.shape
    head_cols = qkv_weight.shape[2]
    cols = tile_cols(head_cols)
    by_heads = pl.BlockSpec((rows, cols), lambda j: (0, j))
    return pl.pallas_call(
        own_kernel,
        grid=(head_cols // cols,),
        in_specs=[
            pl.BlockSpec((2, HD), lambda j: (0, 0)),
            pl.BlockSpec((rows, width), lambda j: (0, 0)),
            by_heads,
            by_heads,
            ANY,
        ],
        out_specs=[by_heads] * 4,
        scratch_shapes=[
            pltpu.VMEM((width, head_cols), BF16),
            pltpu.SemaphoreType.DMA((4,)),
        ],
        out_shape=[jax.ShapeDtypeStruct((rows, head_cols), BF16)]
        + [jax.ShapeDtypeStruct((rows, head_cols), F32)] * 3,
        compiler_params=compiler_params(32),
        cost_estimate=cost(
            2 * rows * width * head_cols + 8 * rows * rows * head_cols,
            2 * rows * width + 18 * rows * head_cols + 2 * width * head_cols,
            rows * rows * head_cols // HD,
        ),
        name="queries_own_frame",
    )(gains, normed, key, value, in_hbm(qkv_weight))


def earlier_kernel(*refs, chunks):
    info_ref, query_ref, acc_ref, top_ref, total_ref, key_ref, value_ref = refs[:7]
    out_refs = refs[7:]
    rows = query_ref.shape[0] // chunks

    def store(row, at, result):
        for c, out_ref in enumerate(out_refs):
            first, end = max(row.start, c * rows), min(row.stop, (c + 1) * rows)
            if first < end:
                inside = slice(first - c * rows, end - c * rows)
                out_ref[inside, at] = result[first - row.start : end - row.start]

    @pl.when(info_ref[0] != 0)
    def _():
        every = slice(0, query_ref.shape[0])
        store(every, slice(None), (acc_ref[...] / total_ref[...]).astype(BF16))

    @pl.when(info_ref[0] == 0)
    def _():
        def finish(scores, row, at):
            old_top = top_ref[row, at][:, :1]
            top = jnp.maximum(jnp.max(scores, axis=-1, keepdims=True), old_top)
            acc, total = weigh(scores, top, value_ref[:, at])
            kept = jnp.exp2(old_top - top)
            acc = acc + acc_ref[row, at] * kept
            total = total + total_ref[row, at] * kept
            store(row, at, (acc / total).astype(BF16))

        attention_tiles(query_ref[...], key_ref, value_ref, finish)


def earlier_attention(info, query, acc, top, total, key, value, chunks):
    rows, head_cols = query.shape
    cols = tile_cols(head_cols)
    return pl.pallas_call(
        functools.partial(earlier_kernel, chunks=chunks),
        grid_spec=pltpu.PrefetchScalarGridSpec(
            num_scalar_prefetch=1,
            grid=(head_cols // cols,),
            in_specs=[pl.BlockSpec((rows, cols), lambda j, i: (0, j))] * 6,
            out_specs=[pl.BlockSpec((rows // chunks, cols), lambda j, i: (0, j))] * chunks,
        ),
        out_shape=[jax.ShapeDtypeStruct((rows // chunks, head_cols), BF16)] * chunks,
        compiler_params=compiler_params(24),
        cost_estimate=cost(
            8 * rows * rows * head_cols,
            20 * rows * head_cols,
            rows * rows * head_cols // HD,
        ),
        name="earlier_frame",
    )(info, query, acc, top, total, key, value)


def output_kernel(*refs, part_counts, whole_weights, half_blocks, last):
    parity_ref = refs[0]
    at = 1
    acc_in = resid_ref = gate_ref = None
    if last:
        acc_in, resid_ref, gate_ref = refs[1:4]
        at = 4
    pieces = []
    for count in part_counts:
        pieces.append(refs[at : at + count])
        at += count
    size = len(part_counts)
    wholes = refs[at : at + whole_weights]
    at += whole_weights
    halves = refs[at : at + 2 * (size - whole_weights)]
    at += 2 * (size - whole_weights)
    out_ref, held_ref, w_ref, held_sems, w_sems = refs[at:]
    step = pl.program_id(0)
    cols = out_ref.shape[1]
    half_width = w_ref.shape[3]

    def weight_copy(half, k):
        if k < whole_weights:
            column = (parity_ref[0] ^ half) * half_width
            source = wholes[k].at[:, pl.ds(pl.multiple_of(column, HD), half_width)]
        else:
            source = halves[half * (size - whole_weights) + k - whole_weights]
        return pltpu.make_async_copy(source, w_ref.at[half, k], w_sems.at[half, k])

    def held_copies(k):
        row = 0
        for number, part in enumerate(pieces[k]):
            count = part.shape[0]
            yield pltpu.make_async_copy(
                part, held_ref.at[k, pl.ds(row, count)], held_sems.at[k, number]
            )
            row += count

    @pl.when(step == 0)
    def _():
        for k in range(size):
            for copy in held_copies(k):
                copy.start()
        for half in range(2):
            for k in range(size):
                weight_copy(half, k).start()
        for k in range(size):
            for copy in held_copies(k):
                copy.wait()

    for half in range(2):

        @pl.when(step == half * half_blocks)
        def _():
            for k in range(size):
                weight_copy(half, k).wait()

    half = step // half_blocks
    tile = tile_cols(cols)
    for t in range(cols // tile):
        at = slice(t * tile, (t + 1) * tile)
        first = lax.rem(step, half_blocks) * cols + t * tile
        inside = pl.ds(pl.multiple_of(first, HD), tile)
        update = acc_in[:, at].astype(F32) if last else None
        for k in range(size):
            term = jnp.dot(held_ref[k], w_ref[half, k, :, inside], preferred_element_type=F32)
            update = term if update is None else update + term
        if last:
            update = resid_ref[:, at].astype(F32) + gate_ref[:, at] * update
        out_ref[:, at] = update.astype(BF16)


def output_projection(parity, pieces, wholes, mine, theirs, finish=None):
    head_cols, half_width = mine[0].shape
    rows = sum(part.shape[0] for part in pieces[0])
    width = 2 * half_width
    size = len(pieces)
    cols = half_width // 2 if half_width % 512 == 0 else half_width
    half_blocks = half_width // cols
    parts = max(len(p) for p in pieces)
    flat = [part for group in pieces for part in group]
    weights = [in_hbm(array) for array in [*wholes, *mine, *theirs]]
    last = finish is not None

    def column(j, parity):
        return 0, ((j // half_blocks) ^ parity[0]) * half_blocks + j % half_blocks

    block = pl.BlockSpec((rows, cols), column)
    return pl.pallas_call(
        functools.partial(
            output_kernel,
            part_counts=tuple(len(p) for p in pieces),
            whole_weights=len(wholes),
            half_blocks=half_blocks,
            last=last,
        ),
        grid_spec=pltpu.PrefetchScalarGridSpec(
            num_scalar_prefetch=1,
            grid=(2 * half_blocks,),
            in_specs=([block, block, pl.BlockSpec((1, cols), column)] if last else [])
            + [ANY] * (len(flat) + len(weights)),
            out_specs=block,
            scratch_shapes=[
                pltpu.VMEM((size, rows, head_cols), BF16),
                pltpu.VMEM((2, size, head_cols, half_width), BF16),
                pltpu.SemaphoreType.DMA((size, parts)),
                pltpu.SemaphoreType.DMA((2, size)),
            ],
        ),
        out_shape=(pltpu.HBM if last else jax.ShapeDtypeStruct)((rows, width), BF16),
        compiler_params=compiler_params(24 if last else 32),
        cost_estimate=cost(
            2 * rows * width * head_cols * size,
            (6 if last else 2) * rows * width + 2 * head_cols * width * size,
        ),
        name="projection_end" if last else "projection_start",
    )(parity, *(finish if last else ()), *flat, *weights)


def send(block, move, queue_size, tensor_size, frames=None):
    pairs = []
    for q in range(queue_size) if frames is None else frames:
        for t in range(tensor_size):
            to_q, to_t = move(q, t)
            pairs.append((q * tensor_size + t, to_q * tensor_size + to_t))
    return lax.ppermute(block, AXES, pairs)


def one_hop(block, queue_size, tensor_size, frames=None):
    half = tensor_size // 2
    args = (queue_size, tensor_size, frames)
    near = send(block, lambda q, t: (q, t ^ 1), *args)
    return [near] + [send(block, away(j, half), *args) for j in range(1, half)]


def two_hops(blocks, queue_size, tensor_size, frames=None):
    half = tensor_size // 2
    args = (queue_size, tensor_size, frames)
    near, far = blocks[0], blocks[1:]
    rows = near.shape[0] // 2
    corners = []
    for j in range(1, half):
        top = send(near[:rows], away(j, half), *args)
        bottom = send(far[j - 1][rows:], lambda q, t: (q, t ^ 1), *args)
        corners.append([top, bottom])
    return corners


def away(j, half):
    return lambda q, t: (q, (t // 2 - j) % half * 2 + t % 2)


def body(
    latents, levels, mod_table, step_size, qkv_weight, q_gain, k_gain, out_weight, fresh_noise
):
    queue_size = lax.axis_size("queue")
    tensor_size = lax.axis_size("tensor")
    rows, width = latents.shape[1:]
    mesh_sizes = (queue_size, tensor_size)
    queue_index = lax.axis_index("queue")
    tensor_index = lax.axis_index("tensor")
    is_last = queue_index == queue_size - 1
    parity = (queue_index % 2).astype(jnp.int32)[None]

    def ring(block):
        return send(block, lambda q, t: ((q + 1) % queue_size, t), *mesh_sizes)

    def sibling(block):
        return send(block, lambda q, t: (q ^ 1, t), *mesh_sizes)

    worked_level = send(levels, lambda q, t: ((q - 1) % queue_size, t), *mesh_sizes)[0]

    def gather_noise(noise):
        return [
            send(noise, lambda q, t: (q, (t - d) % tensor_size), *mesh_sizes, [queue_size - 1])
            for d in range(1, tensor_size)
        ]

    noise = fresh_noise[0]
    noise_pieces = gather_noise(noise)
    half_weight = lax.dynamic_slice(
        out_weight, (0, parity[0] * (width // 2)), (out_weight.shape[0], width // 2)
    )
    half_weight, latents, noise_pieces = lax.optimization_barrier(
        (half_weight, latents, noise_pieces)
    )
    mine = one_hop(half_weight, *mesh_sizes)

    def modulation(level):
        row = lax.dynamic_slice(mod_table, (level, 0), (1, 3 * width)).astype(F32)
        rate = lax.dynamic_slice(step_size, (level,), (1,))[:, None]
        return row[:, :width], 1.0 + row[:, width : 2 * width], rate * row[:, 2 * width :]

    shift, scale1, _ = modulation(worked_level)
    _, _, gate = modulation(levels[0])
    info = jnp.stack([is_last.astype(jnp.int32), tensor_index.astype(jnp.int32)])
    gains = jnp.stack([q_gain * SCORE_SCALE, k_gain])

    frame = latents[0]
    for step_index in range(STEPS):
        final = step_index == STEPS - 1
        key, normed, state = project_keys(
            info, scale1, shift, gains, qkv_weight, frame, noise, noise_pieces
        )
        earlier_key = ring(key)
        value = project_values(normed, qkv_weight)
        earlier_value = ring(value)
        normed, earlier_key = lax.optimization_barrier((normed, earlier_key))
        query, *own = own_attention(gains, normed, qkv_weight, key, value)
        sent_state, query, earlier_value = lax.optimization_barrier(
            (state, query, earlier_value)
        )
        resid = ring(sent_state)
        if not final:
            query, mine = lax.optimization_barrier((query, mine))
            mine_corners = [
                jnp.concatenate(parts, axis=0) for parts in two_hops(mine, *mesh_sizes)
            ]
            theirs = [sibling(block) for block in mine]
            query, theirs = lax.optimization_barrier((query, theirs))
        attended = earlier_attention(
            info, query, *own, earlier_key, earlier_value, CHUNKS if final else 1
        )
        attended = [ring(block) for block in attended]
        if not final:
            attended, mine_corners = lax.optimization_barrier((attended, mine_corners))
            theirs_corners = [sibling(block) for block in mine_corners]
        targets = range(queue_size) if final else range(queue_size - 1)
        near = [one_hop(block, *mesh_sizes, targets) for block in attended]
        beyond = [two_hops(blocks, *mesh_sizes, targets) for blocks in near]
        direct = [attended] + [list(parts) for parts in zip(*near)]
        corners = [[half for parts in p for half in parts] for p in zip(*beyond)]
        if not final:
            noise, corners = lax.optimization_barrier((fresh_noise[step_index + 1], corners))
            noise_pieces = gather_noise(noise)
        begun = output_projection(parity, direct, [out_weight], mine, theirs)
        frame = output_projection(
            parity, corners, [], mine_corners, theirs_corners, (begun, resid, gate)
        )
    return frame[None]


def solution(mesh):
    return jax.shard_map(
        body,
        mesh=mesh,
        in_specs=(
            P("queue", None, None),
            P("queue"),
            P(),
            P(),
            P(None, None, "tensor"),
            P(),
            P(),
            P("tensor", None),
            P(None, "tensor", None),
        ),
        out_specs=P("queue", None, None),
        check_vma=False,
    )
```

```python
import functools
import math

import jax
import jax.numpy as jnp
from jax import lax
from jax.experimental import pallas as pl
from jax.experimental.pallas import tpu as pltpu
from jax.sharding import PartitionSpec as P

HD = 128
STEPS = 2
CHUNKS = 2
EPS = 1e-6
AXES = ("queue", "tensor")
F32 = jnp.float32
BF16 = jnp.bfloat16
SCORE_SCALE = math.log2(math.e) / math.sqrt(HD)
ANY = pl.BlockSpec(memory_space=pl.ANY)


def compiler_params(mib):
    return pltpu.CompilerParams(vmem_limit_bytes=mib * 2**20)


def in_hbm(array):
    return pltpu.with_memory_space_constraint(array, pltpu.HBM)


def cost(flops, nbytes, transcendentals=0, share=1000):
    return pl.CostEstimate(
        flops=int(flops) // share,
        bytes_accessed=int(nbytes) // share,
        transcendentals=int(transcendentals) // share,
    )


def head_normalized(values, gain):
    heads = []
    for h in range(values.shape[1] // HD):
        head = values[:, h * HD : (h + 1) * HD]
        mean = jnp.mean(head * head, axis=-1, keepdims=True)
        heads.append((head * lax.rsqrt(mean + EPS) * gain).astype(BF16))
    return heads[0] if len(heads) == 1 else jnp.concatenate(heads, axis=1)


def tile_cols(head_cols):
    return 256 if head_cols % 256 == 0 else HD


def weight_copies(w_any, part, w_ref, w_sems):
    splits = w_sems.shape[0]
    split_rows = w_ref.shape[0] // splits
    for i in range(splits):
        at = pl.ds(i * split_rows, split_rows)
        yield pltpu.make_async_copy(w_any.at[part, at], w_ref.at[at], w_sems.at[i])


def key_kernel(*refs, half):
    info_ref, scale_ref, shift_ref, gain_ref, w_any, z_any, noise_any, near_any = refs[:8]
    pair_refs = refs[8 : 7 + half]
    key_ref, normed_any, state_any = refs[7 + half : 10 + half]
    state_ref, normed_ref, inverse_ref, w_ref, sem, out_sems, w_sems = refs[10 + half :]
    step = pl.program_id(0)
    rows = state_ref.shape[0]
    piece_rows = noise_any.shape[0]

    def piece_at(j, f):
        if j > 0:
            return pair_refs[j - 1], f * piece_rows
        return (noise_any, near_any)[f], 0

    cols = key_ref.shape[1]
    state_copy = pltpu.make_async_copy(state_ref, state_any, out_sems.at[0])
    normed_copy = pltpu.make_async_copy(normed_ref, normed_any, out_sems.at[1])

    @pl.when(step == 0)
    def _():
        @pl.when(info_ref[0] == 0)
        def _():
            copy = pltpu.make_async_copy(z_any, state_ref, sem.at[0])
            copy.start()
            for weight_copy in weight_copies(w_any, 1, w_ref, w_sems):
                weight_copy.start()
            copy.wait()

        @pl.when(info_ref[0] != 0)
        def _():
            for weight_copy in weight_copies(w_any, 1, w_ref, w_sems):
                weight_copy.start()
            for block in range(2 * half):
                high, low = block // 2, block % 2
                steps = lax.rem(high + half - info_ref[1], half)
                other = jnp.abs(low - info_ref[2])
                for j in range(half):
                    for f in range(2):
                        source, row = piece_at(j, f)

                        @pl.when(jnp.logical_and(steps == j, other == f))
                        def _():
                            copy = pltpu.make_async_copy(
                                source.at[pl.ds(row, piece_rows)],
                                state_ref.at[pl.ds(block * piece_rows, piece_rows)],
                                sem.at[0],
                            )
                            copy.start()
                            copy.wait()

        state_copy.start()

        def measure(i, carry):
            at = pl.ds(pl.multiple_of(i * 16, 16), 16)
            state = state_ref[at, :].astype(F32)
            mean = jnp.mean(state * state, axis=-1, keepdims=True)
            inverse_ref[at, :] = jnp.broadcast_to(lax.rsqrt(mean + EPS), (16, HD))
            return carry

        def apply(i, carry):
            at = pl.ds(pl.multiple_of(i * 16, 16), 16)
            inverse = inverse_ref[at, :][:, :1]
            state = state_ref[at, :].astype(F32) * inverse
            normed_ref[at, :] = (state * scale_ref[...] + shift_ref[...]).astype(BF16)
            return carry

        lax.fori_loop(0, rows // 16, measure, 0, unroll=4)
        lax.fori_loop(0, rows // 16, apply, 0, unroll=2)
        normed_copy.start()
        for copy in weight_copies(w_any, 1, w_ref, w_sems):
            copy.wait()

    at = pl.ds(pl.multiple_of(step * cols, HD), cols)
    product = jnp.dot(normed_ref[...], w_ref[:, at], preferred_element_type=F32)
    key_ref[...] = head_normalized(product, gain_ref[1:2])

    @pl.when(step == pl.num_programs(0) - 1)
    def _():
        state_copy.wait()
        normed_copy.wait()


def project_keys(info, scale1, shift, gains, qkv_weight, z, noise, noise_pieces):
    rows, width = z.shape
    head_cols = qkv_weight.shape[2]
    cols = tile_cols(head_cols)
    half = len(noise_pieces)
    return pl.pallas_call(
        functools.partial(key_kernel, half=half),
        grid_spec=pltpu.PrefetchScalarGridSpec(
            num_scalar_prefetch=1,
            grid=(head_cols // cols,),
            in_specs=[
                pl.BlockSpec((1, width), lambda j, i: (0, 0)),
                pl.BlockSpec((1, width), lambda j, i: (0, 0)),
                pl.BlockSpec((2, HD), lambda j, i: (0, 0)),
            ]
            + [ANY] * (3 + half),
            out_specs=[pl.BlockSpec((rows, cols), lambda j, i: (0, j)), ANY, ANY],
            scratch_shapes=[
                pltpu.VMEM((rows, width), BF16),
                pltpu.VMEM((rows, width), BF16),
                pltpu.VMEM((rows, HD), F32),
                pltpu.VMEM((width, head_cols), BF16),
                pltpu.SemaphoreType.DMA((1,)),
                pltpu.SemaphoreType.DMA((2,)),
                pltpu.SemaphoreType.DMA((4,)),
            ],
        ),
        out_shape=[
            jax.ShapeDtypeStruct((rows, head_cols), BF16),
            jax.ShapeDtypeStruct((rows, width), BF16),
            pltpu.HBM((rows, width), BF16),
        ],
        compiler_params=compiler_params(26),
        cost_estimate=cost(
            2 * rows * width * head_cols,
            6 * rows * width + 2 * rows * head_cols + 2 * width * head_cols,
        ),
        name="norm_keys",
    )(
        info,
        scale1,
        shift,
        gains,
        *[in_hbm(a) for a in (qkv_weight, z)],
        noise,
        *noise_pieces,
    )


def value_kernel(normed_ref, w_any, value_ref, w_ref, w_sems):
    step = pl.program_id(0)
    cols = value_ref.shape[1]

    @pl.when(step == 0)
    def _():
        for copy in weight_copies(w_any, 2, w_ref, w_sems):
            copy.start()
        for copy in weight_copies(w_any, 2, w_ref, w_sems):
            copy.wait()

    at = pl.ds(pl.multiple_of(step * cols, HD), cols)
    product = jnp.dot(normed_ref[...], w_ref[:, at], preferred_element_type=F32)
    value_ref[...] = product.astype(BF16)


def project_values(normed, qkv_weight):
    rows, width = normed.shape
    head_cols = qkv_weight.shape[2]
    cols = tile_cols(head_cols)
    return pl.pallas_call(
        value_kernel,
        grid=(head_cols // cols,),
        in_specs=[pl.BlockSpec((rows, width), lambda j: (0, 0)), ANY],
        out_specs=pl.BlockSpec((rows, cols), lambda j: (0, j)),
        scratch_shapes=[
            pltpu.VMEM((width, head_cols), BF16),
            pltpu.SemaphoreType.DMA((4,)),
        ],
        out_shape=jax.ShapeDtypeStruct((rows, head_cols), BF16),
        compiler_params=compiler_params(20),
        cost_estimate=cost(
            2 * rows * width * head_cols,
            2 * rows * width + 2 * rows * head_cols + 2 * width * head_cols,
        ),
        name="values",
    )(normed, in_hbm(qkv_weight))


def attend(query, key):
    return lax.dot_general(query, key, (((1,), (1,)), ((), ())), preferred_element_type=F32)


def weigh(scores, top, values):
    weights = jnp.exp2(scores - top).astype(BF16)
    extended = jnp.concatenate([values, jnp.ones_like(values)], axis=1)
    total = jnp.dot(weights, extended, preferred_element_type=F32)
    return total[:, :HD], total[:, HD:]


def attention_tiles(query, key, finish):
    rows, cols = query.shape
    tile = math.gcd(rows, 256)
    waiting = None
    for h in range(cols // HD):
        at = slice(h * HD, (h + 1) * HD)
        for r in range(rows // tile):
            row = slice(r * tile, (r + 1) * tile)
            scores = attend(query[row, at], key[:, at])
            if waiting is not None:
                finish(*waiting)
            waiting = (scores, row, at)
    finish(*waiting)


def own_kernel(
    gain_ref, normed_ref, key_ref, value_ref, w_any,
    query_ref, acc_ref, top_ref, total_ref, w_ref, w_sems,
):
    step = pl.program_id(0)
    cols = query_ref.shape[1]

    @pl.when(step == 0)
    def _():
        for copy in weight_copies(w_any, 0, w_ref, w_sems):
            copy.start()
        for copy in weight_copies(w_any, 0, w_ref, w_sems):
            copy.wait()

    inside = pl.ds(pl.multiple_of(step * cols, HD), cols)
    product = jnp.dot(normed_ref[...], w_ref[:, inside], preferred_element_type=F32)
    query = head_normalized(product, gain_ref[0:1])
    query_ref[...] = query

    def finish(scores, row, at):
        top = jnp.max(scores, axis=-1, keepdims=True)
        acc, total = weigh(scores, top, value_ref[:, at])
        acc_ref[row, at] = acc
        total_ref[row, at] = total
        top_ref[row, at] = jnp.broadcast_to(top, acc.shape)

    attention_tiles(query, key_ref, finish)


def own_attention(gains, normed, qkv_weight, key, value):
    rows, width = normed.shape
    head_cols = qkv_weight.shape[2]
    cols = tile_cols(head_cols)
    by_heads = pl.BlockSpec((rows, cols), lambda j: (0, j))
    return pl.pallas_call(
        own_kernel,
        grid=(head_cols // cols,),
        in_specs=[
            pl.BlockSpec((2, HD), lambda j: (0, 0)),
            pl.BlockSpec((rows, width), lambda j: (0, 0)),
            by_heads,
            by_heads,
            ANY,
        ],
        out_specs=[by_heads] * 4,
        scratch_shapes=[
            pltpu.VMEM((width, head_cols), BF16),
            pltpu.SemaphoreType.DMA((4,)),
        ],
        out_shape=[jax.ShapeDtypeStruct((rows, head_cols), BF16)]
        + [jax.ShapeDtypeStruct((rows, head_cols), F32)] * 3,
        compiler_params=compiler_params(32),
        cost_estimate=cost(
            2 * rows * width * head_cols + 8 * rows * rows * head_cols,
            2 * rows * width + 18 * rows * head_cols + 2 * width * head_cols,
            rows * rows * head_cols // HD,
        ),
        name="queries_own_frame",
    )(gains, normed, key, value, in_hbm(qkv_weight))


def earlier_kernel(*refs, chunks):
    info_ref, query_ref, acc_ref, top_ref, total_ref = refs[:5]
    key_ref, first_key_ref, value_ref, first_value_ref = refs[5:9]
    out_refs = refs[9:]
    rows = query_ref.shape[0] // chunks

    def store(row, at, result):
        for c, out_ref in enumerate(out_refs):
            first, end = max(row.start, c * rows), min(row.stop, (c + 1) * rows)
            if first < end:
                inside = slice(first - c * rows, end - c * rows)
                out_ref[inside, at] = result[first - row.start : end - row.start]

    @pl.when(info_ref[0] != 0)
    def _():
        every = slice(0, query_ref.shape[0])
        store(every, slice(None), (acc_ref[...] / total_ref[...]).astype(BF16))

    @pl.when(info_ref[0] == 0)
    def _():
        keys = jnp.where(info_ref[3] != 0, first_key_ref[...], key_ref[...])
        values = jnp.where(info_ref[3] != 0, first_value_ref[...], value_ref[...])

        def finish(scores, row, at):
            old_top = top_ref[row, at][:, :1]
            top = jnp.maximum(jnp.max(scores, axis=-1, keepdims=True), old_top)
            acc, total = weigh(scores, top, values[:, at])
            kept = jnp.exp2(old_top - top)
            acc = acc + acc_ref[row, at] * kept
            total = total + total_ref[row, at] * kept
            store(row, at, (acc / total).astype(BF16))

        attention_tiles(query_ref[...], keys, finish)


def earlier_attention(
    info, query, acc, top, total, key, first_key, value, first_value, chunks
):
    rows, head_cols = query.shape
    cols = tile_cols(head_cols)
    return pl.pallas_call(
        functools.partial(earlier_kernel, chunks=chunks),
        grid_spec=pltpu.PrefetchScalarGridSpec(
            num_scalar_prefetch=1,
            grid=(head_cols // cols,),
            in_specs=[pl.BlockSpec((rows, cols), lambda j, i: (0, j))] * 8,
            out_specs=[pl.BlockSpec((rows // chunks, cols), lambda j, i: (0, j))] * chunks,
        ),
        out_shape=[jax.ShapeDtypeStruct((rows // chunks, head_cols), BF16)] * chunks,
        compiler_params=compiler_params(24),
        cost_estimate=cost(
            8 * rows * rows * head_cols,
            22 * rows * head_cols,
            rows * rows * head_cols // HD,
        ),
        name="earlier_frame",
    )(info, query, acc, top, total, key, first_key, value, first_value)


def output_kernel(*refs, part_counts, whole_weights, half_blocks, last):
    parity_ref = refs[0]
    at = 1
    acc_in = resid_ref = gate_ref = None
    if last:
        acc_in, resid_ref, gate_ref = refs[1:4]
        at = 4
    pieces = []
    for count in part_counts:
        pieces.append(refs[at : at + count])
        at += count
    size = len(part_counts)
    wholes = refs[at : at + whole_weights]
    at += whole_weights
    halves = refs[at : at + 2 * (size - whole_weights)]
    at += 2 * (size - whole_weights)
    out_ref, held_ref, w_ref, held_sems, w_sems = refs[at:]
    step = pl.program_id(0)
    cols = out_ref.shape[1]
    half_width = w_ref.shape[3]

    def weight_copy(half, k):
        if k < whole_weights:
            column = (parity_ref[0] ^ half) * half_width
            source = wholes[k].at[:, pl.ds(pl.multiple_of(column, HD), half_width)]
        else:
            source = halves[half * (size - whole_weights) + k - whole_weights]
        return pltpu.make_async_copy(source, w_ref.at[half, k], w_sems.at[half, k])

    def held_copies(k):
        row = 0
        for number, part in enumerate(pieces[k]):
            count = part.shape[0]
            yield pltpu.make_async_copy(
                part, held_ref.at[k, pl.ds(row, count)], held_sems.at[k, number]
            )
            row += count

    @pl.when(step == 0)
    def _():
        for k in range(size):
            for copy in held_copies(k):
                copy.start()
        for half in range(2):
            for k in range(size):
                weight_copy(half, k).start()
        for k in range(size):
            for copy in held_copies(k):
                copy.wait()

    for half in range(2):

        @pl.when(step == half * half_blocks)
        def _():
            for k in range(size):
                weight_copy(half, k).wait()

    half = step // half_blocks
    tile = tile_cols(cols)
    for t in range(cols // tile):
        at = slice(t * tile, (t + 1) * tile)
        first = lax.rem(step, half_blocks) * cols + t * tile
        inside = pl.ds(pl.multiple_of(first, HD), tile)
        update = acc_in[:, at].astype(F32) if last else None
        for k in range(size):
            term = jnp.dot(held_ref[k], w_ref[half, k, :, inside], preferred_element_type=F32)
            update = term if update is None else update + term
        if last:
            update = resid_ref[:, at].astype(F32) + gate_ref[:, at] * update
        out_ref[:, at] = update.astype(BF16)


def output_projection(parity, pieces, wholes, mine, theirs, finish=None):
    head_cols, half_width = mine[0].shape
    rows = sum(part.shape[0] for part in pieces[0])
    width = 2 * half_width
    size = len(pieces)
    cols = half_width // 2 if half_width % 512 == 0 else half_width
    half_blocks = half_width // cols
    parts = max(len(p) for p in pieces)
    flat = [part for group in pieces for part in group]
    weights = [in_hbm(array) for array in [*wholes, *mine, *theirs]]
    last = finish is not None

    def column(j, parity):
        return 0, ((j // half_blocks) ^ parity[0]) * half_blocks + j % half_blocks

    block = pl.BlockSpec((rows, cols), column)
    return pl.pallas_call(
        functools.partial(
            output_kernel,
            part_counts=tuple(len(p) for p in pieces),
            whole_weights=len(wholes),
            half_blocks=half_blocks,
            last=last,
        ),
        grid_spec=pltpu.PrefetchScalarGridSpec(
            num_scalar_prefetch=1,
            grid=(2 * half_blocks,),
            in_specs=([block, block, pl.BlockSpec((1, cols), column)] if last else [])
            + [ANY] * (len(flat) + len(weights)),
            out_specs=block,
            scratch_shapes=[
                pltpu.VMEM((size, rows, head_cols), BF16),
                pltpu.VMEM((2, size, head_cols, half_width), BF16),
                pltpu.SemaphoreType.DMA((size, parts)),
                pltpu.SemaphoreType.DMA((2, size)),
            ],
        ),
        out_shape=(pltpu.HBM if last else jax.ShapeDtypeStruct)((rows, width), BF16),
        compiler_params=compiler_params(24 if last else 32),
        cost_estimate=cost(
            2 * rows * width * head_cols * size,
            (6 if last else 2) * rows * width + 2 * head_cols * width * size,
        ),
        name="projection_end" if last else "projection_start",
    )(parity, *(finish if last else ()), *flat, *weights)


def send(block, move, queue_size, tensor_size, frames=None):
    pairs = []
    for q in range(queue_size) if frames is None else frames:
        for t in range(tensor_size):
            to_q, to_t = move(q, t)
            pairs.append((q * tensor_size + t, to_q * tensor_size + to_t))
    return lax.ppermute(block, AXES, pairs)


def one_hop(block, queue_size, tensor_size, frames=None):
    half = tensor_size // 2
    args = (queue_size, tensor_size, frames)
    near = send(block, lambda q, t: (q, t ^ 1), *args)
    return [near] + [send(block, away(j, half), *args) for j in range(1, half)]


def two_hops(blocks, queue_size, tensor_size, frames=None):
    half = tensor_size // 2
    args = (queue_size, tensor_size, frames)
    near, far = blocks[0], blocks[1:]
    rows = near.shape[0] // 2
    corners = []
    for j in range(1, half):
        top = send(near[:rows], away(j, half), *args)
        bottom = send(far[j - 1][rows:], lambda q, t: (q, t ^ 1), *args)
        corners.append([top, bottom])
    return corners


def away(j, half):
    return lambda q, t: (q, (t // 2 - j) % half * 2 + t % 2)


def body(
    latents, levels, mod_table, step_size, qkv_weight, q_gain, k_gain, out_weight, fresh_noise
):
    queue_size = lax.axis_size("queue")
    tensor_size = lax.axis_size("tensor")
    rows, width = latents.shape[1:]
    mesh_sizes = (queue_size, tensor_size)
    queue_index = lax.axis_index("queue")
    tensor_index = lax.axis_index("tensor")
    is_last = queue_index == queue_size - 1
    parity = (queue_index % 2).astype(jnp.int32)[None]

    def ring(block, frames=None):
        return send(block, lambda q, t: ((q + 1) % queue_size, t), *mesh_sizes, frames)

    def sibling(block):
        return send(block, lambda q, t: (q ^ 1, t), *mesh_sizes)

    worked_level = send(levels, lambda q, t: ((q - 1) % queue_size, t), *mesh_sizes)[0]

    def gather_noise(noise, at_once):
        args = (*mesh_sizes, [queue_size - 1])
        half = tensor_size // 2
        near = send(noise, lambda q, t: (q, t ^ 1), *args)
        pairs = []
        if at_once:
            for j in range(1, half):
                straight = send(noise, away(j, half), *args)
                across = send(noise, lambda q, t: away(j, half)(q, t ^ 1), *args)
                pairs.append(jnp.concatenate([straight, across], axis=0))
        else:
            pair = jnp.concatenate([noise, near], axis=0)
            pairs = [send(pair, away(j, half), *args) for j in range(1, half)]
        return [near, *pairs]

    noise = fresh_noise[0]
    noise_pieces = gather_noise(noise, True)
    half_weight = lax.dynamic_slice(
        out_weight, (0, parity[0] * (width // 2)), (out_weight.shape[0], width // 2)
    )
    half_weight, latents, noise_pieces = lax.optimization_barrier(
        (half_weight, latents, noise_pieces)
    )
    mine = one_hop(half_weight, *mesh_sizes)

    def modulation(level):
        row = lax.dynamic_slice(mod_table, (level, 0), (1, 3 * width)).astype(F32)
        rate = lax.dynamic_slice(step_size, (level,), (1,))[:, None]
        return row[:, :width], 1.0 + row[:, width : 2 * width], rate * row[:, 2 * width :]

    shift, scale1, _ = modulation(worked_level)
    _, _, gate = modulation(levels[0])
    info = jnp.stack([is_last, tensor_index // 2, tensor_index % 2, queue_index == 0])
    info = info.astype(jnp.int32)
    gains = jnp.stack([q_gain * SCORE_SCALE, k_gain])

    frame = latents[0]
    for step_index in range(STEPS):
        final = step_index == STEPS - 1
        key, normed, state = project_keys(
            info, scale1, shift, gains, qkv_weight, frame, noise, noise_pieces
        )
        earlier_key = ring(key, range(queue_size - 2))
        first_key = ring(key, [queue_size - 1])
        value = project_values(normed, qkv_weight)
        earlier_value = ring(value, range(queue_size - 2))
        first_value = ring(value, [queue_size - 1])
        normed, earlier_key = lax.optimization_barrier((normed, earlier_key))
        query, *own = own_attention(gains, normed, qkv_weight, key, value)
        if not final:
            query, mine, earlier_value, first_key, first_value = lax.optimization_barrier(
                (query, mine, earlier_value, first_key, first_value)
            )
            mine_corners = [
                jnp.concatenate(parts, axis=0) for parts in two_hops(mine, *mesh_sizes)
            ]
            theirs = [sibling(block) for block in mine]
            query, theirs = lax.optimization_barrier((query, theirs))
        attended = earlier_attention(
            info,
            query,
            *own,
            earlier_key,
            first_key,
            earlier_value,
            first_value,
            CHUNKS if final else 1,
        )
        senders = [q for q in range(queue_size) if final or q != queue_size - 2]
        targets = range(queue_size if final else queue_size - 1)
        attended = [ring(block, senders) for block in attended]
        if not final:
            attended, mine_corners = lax.optimization_barrier((attended, mine_corners))
            theirs_corners = [sibling(block) for block in mine_corners]
        sent_state, _ = lax.optimization_barrier((state, attended))
        resid = ring(sent_state, senders)
        near = [one_hop(block, *mesh_sizes, targets) for block in attended]
        beyond = [two_hops(blocks, *mesh_sizes, targets) for blocks in near]
        direct = [attended] + [list(parts) for parts in zip(*near)]
        corners = [[half for parts in p for half in parts] for p in zip(*beyond)]
        if not final:
            noise, _ = lax.optimization_barrier((fresh_noise[step_index + 1], attended))
            noise_pieces = gather_noise(noise, False)
        begun = output_projection(parity, direct, [out_weight], mine, theirs)
        frame = output_projection(
            parity, corners, [], mine_corners, theirs_corners, (begun, resid, gate)
        )
    return frame[None]


def solution(mesh):
    return jax.shard_map(
        body,
        mesh=mesh,
        in_specs=(
            P("queue", None, None),
            P("queue"),
            P(),
            P(),
            P(None, None, "tensor"),
            P(),
            P(),
            P("tensor", None),
            P(None, "tensor", None),
        ),
        out_specs=P("queue", None, None),
        check_vma=False,
    )
```

```python
import functools
import math

import jax
import jax.numpy as jnp
from jax import lax
from jax.experimental import pallas as pl
from jax.experimental.pallas import tpu as pltpu
from jax.sharding import PartitionSpec as P

HD = 128
STEPS = 2
CHUNKS = 2
EPS = 1e-6
AXES = ("queue", "tensor")
F32 = jnp.float32
BF16 = jnp.bfloat16
SCORE_SCALE = math.log2(math.e) / math.sqrt(HD)
ANY = pl.BlockSpec(memory_space=pl.ANY)


def compiler_params(mib):
    return pltpu.CompilerParams(vmem_limit_bytes=mib * 2**20)


def in_hbm(array):
    return pltpu.with_memory_space_constraint(array, pltpu.HBM)


def cost(flops, nbytes, transcendentals=0, share=1000):
    return pl.CostEstimate(
        flops=int(flops) // share,
        bytes_accessed=int(nbytes) // share,
        transcendentals=int(transcendentals) // share,
    )


def head_normalized(values, gain):
    heads = []
    for h in range(values.shape[1] // HD):
        head = values[:, h * HD : (h + 1) * HD]
        mean = jnp.mean(head * head, axis=-1, keepdims=True)
        heads.append((head * lax.rsqrt(mean + EPS) * gain).astype(BF16))
    return heads[0] if len(heads) == 1 else jnp.concatenate(heads, axis=1)


def tile_cols(head_cols):
    return 256 if head_cols % 256 == 0 else HD


def weight_copies(w_any, part, w_ref, w_sems):
    splits = w_sems.shape[0]
    split_rows = w_ref.shape[0] // splits
    for i in range(splits):
        at = pl.ds(i * split_rows, split_rows)
        yield pltpu.make_async_copy(w_any.at[part, at], w_ref.at[at], w_sems.at[i])


def key_kernel(*refs, half):
    info_ref, scale_ref, shift_ref, gain_ref, w_any, z_any, noise_any, near_any = refs[:8]
    pair_refs = refs[8 : 7 + half]
    key_ref, normed_any, state_any = refs[7 + half : 10 + half]
    state_ref, normed_ref, inverse_ref, w_ref, sem, out_sems, w_sems = refs[10 + half :]
    step = pl.program_id(0)
    rows = state_ref.shape[0]
    piece_rows = noise_any.shape[0]

    def piece_at(j, f):
        if j > 0:
            return pair_refs[j - 1], f * piece_rows
        return (noise_any, near_any)[f], 0

    cols = key_ref.shape[1]
    state_copy = pltpu.make_async_copy(state_ref, state_any, out_sems.at[0])
    normed_copy = pltpu.make_async_copy(normed_ref, normed_any, out_sems.at[1])

    @pl.when(step == 0)
    def _():
        @pl.when(info_ref[0] == 0)
        def _():
            copy = pltpu.make_async_copy(z_any, state_ref, sem.at[0])
            copy.start()
            for weight_copy in weight_copies(w_any, 1, w_ref, w_sems):
                weight_copy.start()
            copy.wait()

        @pl.when(info_ref[0] != 0)
        def _():
            for weight_copy in weight_copies(w_any, 1, w_ref, w_sems):
                weight_copy.start()
            for block in range(2 * half):
                high, low = block // 2, block % 2
                steps = lax.rem(high + half - info_ref[1], half)
                other = jnp.abs(low - info_ref[2])
                for j in range(half):
                    for f in range(2):
                        source, row = piece_at(j, f)

                        @pl.when(jnp.logical_and(steps == j, other == f))
                        def _():
                            copy = pltpu.make_async_copy(
                                source.at[pl.ds(row, piece_rows)],
                                state_ref.at[pl.ds(block * piece_rows, piece_rows)],
                                sem.at[0],
                            )
                            copy.start()
                            copy.wait()

        state_copy.start()

        def measure(i, carry):
            at = pl.ds(pl.multiple_of(i * 16, 16), 16)
            state = state_ref[at, :].astype(F32)
            mean = jnp.mean(state * state, axis=-1, keepdims=True)
            inverse_ref[at, :] = jnp.broadcast_to(lax.rsqrt(mean + EPS), (16, HD))
            return carry

        def apply(i, carry):
            at = pl.ds(pl.multiple_of(i * 16, 16), 16)
            inverse = inverse_ref[at, :][:, :1]
            state = state_ref[at, :].astype(F32) * inverse
            normed_ref[at, :] = (state * scale_ref[...] + shift_ref[...]).astype(BF16)
            return carry

        lax.fori_loop(0, rows // 16, measure, 0, unroll=4)
        lax.fori_loop(0, rows // 16, apply, 0, unroll=2)
        normed_copy.start()
        for copy in weight_copies(w_any, 1, w_ref, w_sems):
            copy.wait()

    at = pl.ds(pl.multiple_of(step * cols, HD), cols)
    product = jnp.dot(normed_ref[...], w_ref[:, at], preferred_element_type=F32)
    key_ref[...] = head_normalized(product, gain_ref[1:2])

    @pl.when(step == pl.num_programs(0) - 1)
    def _():
        state_copy.wait()
        normed_copy.wait()


def project_keys(info, scale1, shift, gains, qkv_weight, z, noise, noise_pieces):
    rows, width = z.shape
    head_cols = qkv_weight.shape[2]
    cols = tile_cols(head_cols)
    half = len(noise_pieces)
    return pl.pallas_call(
        functools.partial(key_kernel, half=half),
        grid_spec=pltpu.PrefetchScalarGridSpec(
            num_scalar_prefetch=1,
            grid=(head_cols // cols,),
            in_specs=[
                pl.BlockSpec((1, width), lambda j, i: (0, 0)),
                pl.BlockSpec((1, width), lambda j, i: (0, 0)),
                pl.BlockSpec((2, HD), lambda j, i: (0, 0)),
            ]
            + [ANY] * (3 + half),
            out_specs=[pl.BlockSpec((rows, cols), lambda j, i: (0, j)), ANY, ANY],
            scratch_shapes=[
                pltpu.VMEM((rows, width), BF16),
                pltpu.VMEM((rows, width), BF16),
                pltpu.VMEM((rows, HD), F32),
                pltpu.VMEM((width, head_cols), BF16),
                pltpu.SemaphoreType.DMA((1,)),
                pltpu.SemaphoreType.DMA((2,)),
                pltpu.SemaphoreType.DMA((4,)),
            ],
        ),
        out_shape=[
            jax.ShapeDtypeStruct((rows, head_cols), BF16),
            jax.ShapeDtypeStruct((rows, width), BF16),
            pltpu.HBM((rows, width), BF16),
        ],
        compiler_params=compiler_params(26),
        cost_estimate=cost(
            2 * rows * width * head_cols,
            6 * rows * width + 2 * rows * head_cols + 2 * width * head_cols,
        ),
        name="norm_keys",
    )(
        info,
        scale1,
        shift,
        gains,
        *[in_hbm(a) for a in (qkv_weight, z)],
        noise,
        *noise_pieces,
    )


def value_kernel(normed_ref, w_any, value_ref, w_ref, w_sems):
    step = pl.program_id(0)
    cols = value_ref.shape[1]

    @pl.when(step == 0)
    def _():
        for copy in weight_copies(w_any, 2, w_ref, w_sems):
            copy.start()
        for copy in weight_copies(w_any, 2, w_ref, w_sems):
            copy.wait()

    at = pl.ds(pl.multiple_of(step * cols, HD), cols)
    product = jnp.dot(normed_ref[...], w_ref[:, at], preferred_element_type=F32)
    value_ref[...] = product.astype(BF16)


def project_values(normed, qkv_weight):
    rows, width = normed.shape
    head_cols = qkv_weight.shape[2]
    cols = tile_cols(head_cols)
    return pl.pallas_call(
        value_kernel,
        grid=(head_cols // cols,),
        in_specs=[pl.BlockSpec((rows, width), lambda j: (0, 0)), ANY],
        out_specs=pl.BlockSpec((rows, cols), lambda j: (0, j)),
        scratch_shapes=[
            pltpu.VMEM((width, head_cols), BF16),
            pltpu.SemaphoreType.DMA((4,)),
        ],
        out_shape=jax.ShapeDtypeStruct((rows, head_cols), BF16),
        compiler_params=compiler_params(20),
        cost_estimate=cost(
            2 * rows * width * head_cols,
            2 * rows * width + 2 * rows * head_cols + 2 * width * head_cols,
        ),
        name="values",
    )(normed, in_hbm(qkv_weight))


def attend(query, key):
    return lax.dot_general(query, key, (((1,), (1,)), ((), ())), preferred_element_type=F32)


def weigh(scores, top, values):
    weights = jnp.exp2(scores - top).astype(BF16)
    extended = jnp.concatenate([values, jnp.ones_like(values)], axis=1)
    total = jnp.dot(weights, extended, preferred_element_type=F32)
    return total[:, :HD], total[:, HD:]


def attention_tiles(query, key, finish):
    rows, cols = query.shape
    tile = math.gcd(rows, 256)
    waiting = None
    for h in range(cols // HD):
        at = slice(h * HD, (h + 1) * HD)
        for r in range(rows // tile):
            row = slice(r * tile, (r + 1) * tile)
            scores = attend(query[row, at], key[:, at])
            if waiting is not None:
                finish(*waiting)
            waiting = (scores, row, at)
    finish(*waiting)


def own_kernel(
    gain_ref, normed_ref, key_ref, value_ref, w_any,
    query_ref, acc_ref, top_ref, total_ref, w_ref, w_sems,
):
    step = pl.program_id(0)
    cols = query_ref.shape[1]

    @pl.when(step == 0)
    def _():
        for copy in weight_copies(w_any, 0, w_ref, w_sems):
            copy.start()
        for copy in weight_copies(w_any, 0, w_ref, w_sems):
            copy.wait()

    inside = pl.ds(pl.multiple_of(step * cols, HD), cols)
    product = jnp.dot(normed_ref[...], w_ref[:, inside], preferred_element_type=F32)
    query = head_normalized(product, gain_ref[0:1])
    query_ref[...] = query

    def finish(scores, row, at):
        top = jnp.max(scores, axis=-1, keepdims=True)
        acc, total = weigh(scores, top, value_ref[:, at])
        acc_ref[row, at] = acc
        total_ref[row, at] = total
        top_ref[row, at] = jnp.broadcast_to(top, acc.shape)

    attention_tiles(query, key_ref, finish)


def own_attention(gains, normed, qkv_weight, key, value):
    rows, width = normed.shape
    head_cols = qkv_weight.shape[2]
    cols = tile_cols(head_cols)
    by_heads = pl.BlockSpec((rows, cols), lambda j: (0, j))
    return pl.pallas_call(
        own_kernel,
        grid=(head_cols // cols,),
        in_specs=[
            pl.BlockSpec((2, HD), lambda j: (0, 0)),
            pl.BlockSpec((rows, width), lambda j: (0, 0)),
            by_heads,
            by_heads,
            ANY,
        ],
        out_specs=[by_heads] * 4,
        scratch_shapes=[
            pltpu.VMEM((width, head_cols), BF16),
            pltpu.SemaphoreType.DMA((4,)),
        ],
        out_shape=[jax.ShapeDtypeStruct((rows, head_cols), BF16)]
        + [jax.ShapeDtypeStruct((rows, head_cols), F32)] * 3,
        compiler_params=compiler_params(32),
        cost_estimate=cost(
            2 * rows * width * head_cols + 8 * rows * rows * head_cols,
            2 * rows * width + 18 * rows * head_cols + 2 * width * head_cols,
            rows * rows * head_cols // HD,
        ),
        name="queries_own_frame",
    )(gains, normed, key, value, in_hbm(qkv_weight))


def earlier_kernel(*refs, chunks):
    info_ref, query_ref, acc_ref, top_ref, total_ref, key_ref, value_ref = refs[:7]
    out_refs = refs[7:]
    rows = query_ref.shape[0] // chunks

    def store(row, at, result):
        for c, out_ref in enumerate(out_refs):
            first, end = max(row.start, c * rows), min(row.stop, (c + 1) * rows)
            if first < end:
                inside = slice(first - c * rows, end - c * rows)
                out_ref[inside, at] = result[first - row.start : end - row.start]

    @pl.when(info_ref[0] != 0)
    def _():
        every = slice(0, query_ref.shape[0])
        store(every, slice(None), (acc_ref[...] / total_ref[...]).astype(BF16))

    @pl.when(info_ref[0] == 0)
    def _():
        def finish(scores, row, at):
            old_top = top_ref[row, at][:, :1]
            top = jnp.maximum(jnp.max(scores, axis=-1, keepdims=True), old_top)
            acc, total = weigh(scores, top, value_ref[:, at])
            kept = jnp.exp2(old_top - top)
            acc = acc + acc_ref[row, at] * kept
            total = total + total_ref[row, at] * kept
            store(row, at, (acc / total).astype(BF16))

        attention_tiles(query_ref[...], key_ref, finish)


def earlier_attention(info, query, acc, top, total, key, value, chunks):
    rows, head_cols = query.shape
    cols = tile_cols(head_cols)
    return pl.pallas_call(
        functools.partial(earlier_kernel, chunks=chunks),
        grid_spec=pltpu.PrefetchScalarGridSpec(
            num_scalar_prefetch=1,
            grid=(head_cols // cols,),
            in_specs=[pl.BlockSpec((rows, cols), lambda j, i: (0, j))] * 6,
            out_specs=[pl.BlockSpec((rows // chunks, cols), lambda j, i: (0, j))] * chunks,
        ),
        out_shape=[jax.ShapeDtypeStruct((rows // chunks, head_cols), BF16)] * chunks,
        compiler_params=compiler_params(24),
        cost_estimate=cost(
            8 * rows * rows * head_cols,
            22 * rows * head_cols,
            rows * rows * head_cols // HD,
        ),
        name="earlier_frame",
    )(info, query, acc, top, total, key, value)


def output_kernel(*refs, part_counts, whole_weights, half_blocks, last):
    parity_ref = refs[0]
    at = 1
    acc_in = resid_ref = gate_ref = None
    if last:
        acc_in, resid_ref, gate_ref = refs[1:4]
        at = 4
    pieces = []
    for count in part_counts:
        pieces.append(refs[at : at + count])
        at += count
    size = len(part_counts)
    wholes = refs[at : at + whole_weights]
    at += whole_weights
    halves = refs[at : at + 2 * (size - whole_weights)]
    at += 2 * (size - whole_weights)
    out_ref, held_ref, w_ref, held_sems, w_sems = refs[at:]
    step = pl.program_id(0)
    cols = out_ref.shape[1]
    half_width = w_ref.shape[3]

    def weight_copy(half, k):
        if k < whole_weights:
            column = (parity_ref[0] ^ half) * half_width
            source = wholes[k].at[:, pl.ds(pl.multiple_of(column, HD), half_width)]
        else:
            source = halves[half * (size - whole_weights) + k - whole_weights]
        return pltpu.make_async_copy(source, w_ref.at[half, k], w_sems.at[half, k])

    def held_copies(k):
        row = 0
        for number, part in enumerate(pieces[k]):
            count = part.shape[0]
            yield pltpu.make_async_copy(
                part, held_ref.at[k, pl.ds(row, count)], held_sems.at[k, number]
            )
            row += count

    @pl.when(step == 0)
    def _():
        for k in range(size):
            for copy in held_copies(k):
                copy.start()
        for half in range(2):
            for k in range(size):
                weight_copy(half, k).start()
        for k in range(size):
            for copy in held_copies(k):
                copy.wait()

    for half in range(2):

        @pl.when(step == half * half_blocks)
        def _():
            for k in range(size):
                weight_copy(half, k).wait()

    half = step // half_blocks
    tile = tile_cols(cols)
    for t in range(cols // tile):
        at = slice(t * tile, (t + 1) * tile)
        first = lax.rem(step, half_blocks) * cols + t * tile
        inside = pl.ds(pl.multiple_of(first, HD), tile)
        update = acc_in[:, at].astype(F32) if last else None
        for k in range(size):
            term = jnp.dot(held_ref[k], w_ref[half, k, :, inside], preferred_element_type=F32)
            update = term if update is None else update + term
        if last:
            update = resid_ref[:, at].astype(F32) + gate_ref[:, at] * update
        out_ref[:, at] = update.astype(BF16)


def output_projection(parity, pieces, wholes, mine, theirs, finish=None):
    head_cols, half_width = mine[0].shape
    rows = sum(part.shape[0] for part in pieces[0])
    width = 2 * half_width
    size = len(pieces)
    cols = half_width // 2 if half_width % 512 == 0 else half_width
    half_blocks = half_width // cols
    parts = max(len(p) for p in pieces)
    flat = [part for group in pieces for part in group]
    weights = [in_hbm(array) for array in [*wholes, *mine, *theirs]]
    last = finish is not None

    def column(j, parity):
        return 0, ((j // half_blocks) ^ parity[0]) * half_blocks + j % half_blocks

    block = pl.BlockSpec((rows, cols), column)
    return pl.pallas_call(
        functools.partial(
            output_kernel,
            part_counts=tuple(len(p) for p in pieces),
            whole_weights=len(wholes),
            half_blocks=half_blocks,
            last=last,
        ),
        grid_spec=pltpu.PrefetchScalarGridSpec(
            num_scalar_prefetch=1,
            grid=(2 * half_blocks,),
            in_specs=([block, block, pl.BlockSpec((1, cols), column)] if last else [])
            + [ANY] * (len(flat) + len(weights)),
            out_specs=block,
            scratch_shapes=[
                pltpu.VMEM((size, rows, head_cols), BF16),
                pltpu.VMEM((2, size, head_cols, half_width), BF16),
                pltpu.SemaphoreType.DMA((size, parts)),
                pltpu.SemaphoreType.DMA((2, size)),
            ],
        ),
        out_shape=(pltpu.HBM if last else jax.ShapeDtypeStruct)((rows, width), BF16),
        compiler_params=compiler_params(24 if last else 32),
        cost_estimate=cost(
            2 * rows * width * head_cols * size,
            (6 if last else 2) * rows * width + 2 * head_cols * width * size,
        ),
        name="projection_end" if last else "projection_start",
    )(parity, *(finish if last else ()), *flat, *weights)


def send(block, move, queue_size, tensor_size, frames=None):
    pairs = []
    for q in range(queue_size) if frames is None else frames:
        for t in range(tensor_size):
            to_q, to_t = move(q, t)
            pairs.append((q * tensor_size + t, to_q * tensor_size + to_t))
    return lax.ppermute(block, AXES, pairs)


def one_hop(block, queue_size, tensor_size, frames=None):
    half = tensor_size // 2
    args = (queue_size, tensor_size, frames)
    near = send(block, lambda q, t: (q, t ^ 1), *args)
    return [near] + [send(block, away(j, half), *args) for j in range(1, half)]


def two_hops(blocks, queue_size, tensor_size, frames=None):
    half = tensor_size // 2
    args = (queue_size, tensor_size, frames)
    near, far = blocks[0], blocks[1:]
    rows = near.shape[0] // 2
    corners = []
    for j in range(1, half):
        top = send(near[:rows], away(j, half), *args)
        bottom = send(far[j - 1][rows:], lambda q, t: (q, t ^ 1), *args)
        corners.append([top, bottom])
    return corners


def away(j, half):
    return lambda q, t: (q, (t // 2 - j) % half * 2 + t % 2)


def body(
    latents, levels, mod_table, step_size, qkv_weight, q_gain, k_gain, out_weight, fresh_noise
):
    queue_size = lax.axis_size("queue")
    tensor_size = lax.axis_size("tensor")
    rows, width = latents.shape[1:]
    mesh_sizes = (queue_size, tensor_size)
    queue_index = lax.axis_index("queue")
    tensor_index = lax.axis_index("tensor")
    is_last = queue_index == queue_size - 1
    parity = (queue_index % 2).astype(jnp.int32)[None]

    def ring(block, frames=None):
        return send(block, lambda q, t: ((q + 1) % queue_size, t), *mesh_sizes, frames)

    def sibling(block):
        return send(block, lambda q, t: (q ^ 1, t), *mesh_sizes)

    worked_level = send(levels, lambda q, t: ((q - 1) % queue_size, t), *mesh_sizes)[0]

    def gather_noise(noise, at_once):
        args = (*mesh_sizes, [queue_size - 1])
        half = tensor_size // 2
        near = send(noise, lambda q, t: (q, t ^ 1), *args)
        pairs = []
        if at_once:
            for j in range(1, half):
                straight = send(noise, away(j, half), *args)
                across = send(noise, lambda q, t: away(j, half)(q, t ^ 1), *args)
                pairs.append(jnp.concatenate([straight, across], axis=0))
        else:
            pair = jnp.concatenate([noise, near], axis=0)
            pairs = [send(pair, away(j, half), *args) for j in range(1, half)]
        return [near, *pairs]

    noise = fresh_noise[0]
    noise_pieces = gather_noise(noise, True)
    half_weight = lax.dynamic_slice(
        out_weight, (0, parity[0] * (width // 2)), (out_weight.shape[0], width // 2)
    )
    half_weight, latents, noise_pieces = lax.optimization_barrier(
        (half_weight, latents, noise_pieces)
    )
    mine = one_hop(half_weight, *mesh_sizes)

    def modulation(level):
        row = lax.dynamic_slice(mod_table, (level, 0), (1, 3 * width)).astype(F32)
        rate = lax.dynamic_slice(step_size, (level,), (1,))[:, None]
        return row[:, :width], 1.0 + row[:, width : 2 * width], rate * row[:, 2 * width :]

    shift, scale1, _ = modulation(worked_level)
    _, _, gate = modulation(levels[0])
    info = jnp.stack([is_last, tensor_index // 2, tensor_index % 2])
    info = info.astype(jnp.int32)
    gains = jnp.stack([q_gain * SCORE_SCALE, k_gain])

    frame = latents[0]
    for step_index in range(STEPS):
        final = step_index == STEPS - 1
        key, normed, state = project_keys(
            info, scale1, shift, gains, qkv_weight, frame, noise, noise_pieces
        )
        to_next = [q for q in range(queue_size) if q != queue_size - 2]
        earlier_key = ring(key, to_next)
        value = project_values(normed, qkv_weight)
        earlier_value = ring(value, to_next)
        normed, earlier_key = lax.optimization_barrier((normed, earlier_key))
        query, *own = own_attention(gains, normed, qkv_weight, key, value)
        if not final:
            query, mine, earlier_value = lax.optimization_barrier(
                (query, mine, earlier_value)
            )
            mine_corners = [
                jnp.concatenate(parts, axis=0) for parts in two_hops(mine, *mesh_sizes)
            ]
            theirs = [sibling(block) for block in mine]
            query, theirs = lax.optimization_barrier((query, theirs))
        attended = earlier_attention(
            info, query, *own, earlier_key, earlier_value, CHUNKS if final else 1
        )
        senders = range(queue_size) if final else to_next
        targets = range(queue_size if final else queue_size - 1)
        attended = [ring(block, senders) for block in attended]
        if not final:
            attended, mine_corners = lax.optimization_barrier((attended, mine_corners))
        sent_state, _ = lax.optimization_barrier((state, attended))
        resid = ring(sent_state, senders)
        near = [one_hop(block, *mesh_sizes, targets) for block in attended]
        if not final:
            noise, mine_corners, near = lax.optimization_barrier(
                (fresh_noise[step_index + 1], mine_corners, near)
            )
            theirs_corners = [sibling(block) for block in mine_corners]
            noise_pieces = gather_noise(noise, False)
        beyond = [two_hops(blocks, *mesh_sizes, targets) for blocks in near]
        direct = [attended] + [list(parts) for parts in zip(*near)]
        corners = [[half for parts in p for half in parts] for p in zip(*beyond)]
        begun = output_projection(parity, direct, [out_weight], mine, theirs)
        frame = output_projection(
            parity, corners, [], mine_corners, theirs_corners, (begun, resid, gate)
        )
    return frame[None]


def solution(mesh):
    return jax.shard_map(
        body,
        mesh=mesh,
        in_specs=(
            P("queue", None, None),
            P("queue"),
            P(),
            P(),
            P(None, None, "tensor"),
            P(),
            P(),
            P("tensor", None),
            P(None, "tensor", None),
        ),
        out_specs=P("queue", None, None),
        check_vma=False,
    )
```

```python
import functools
import math

import jax
import jax.numpy as jnp
from jax import lax
from jax.experimental import pallas as pl
from jax.experimental.pallas import tpu as pltpu
from jax.sharding import PartitionSpec as P

HD = 128
STEPS = 2
CHUNKS = 2
EPS = 1e-6
AXES = ("queue", "tensor")
F32 = jnp.float32
BF16 = jnp.bfloat16
SCORE_SCALE = math.log2(math.e) / math.sqrt(HD)
ANY = pl.BlockSpec(memory_space=pl.ANY)


def compiler_params(mib):
    return pltpu.CompilerParams(vmem_limit_bytes=mib * 2**20)


def in_hbm(array):
    return pltpu.with_memory_space_constraint(array, pltpu.HBM)


def cost(flops, nbytes, transcendentals=0, share=1000):
    return pl.CostEstimate(
        flops=int(flops) // share,
        bytes_accessed=int(nbytes) // share,
        transcendentals=int(transcendentals) // share,
    )


def head_normalized(values, gain):
    heads = []
    for h in range(values.shape[1] // HD):
        head = values[:, h * HD : (h + 1) * HD]
        mean = jnp.mean(head * head, axis=-1, keepdims=True)
        heads.append((head * lax.rsqrt(mean + EPS) * gain).astype(BF16))
    return heads[0] if len(heads) == 1 else jnp.concatenate(heads, axis=1)


def over_lanes(values, fold, reduce):
    parts = [values[:, i : i + HD] for i in range(0, values.shape[1], HD)]
    return reduce(functools.reduce(fold, parts), axis=-1, keepdims=True)


def tile_cols(head_cols):
    return 256 if head_cols % 256 == 0 else HD


def weight_copies(w_any, part, w_ref, w_sems):
    splits = w_sems.shape[0]
    split_rows = w_ref.shape[0] // splits
    for i in range(splits):
        at = pl.ds(i * split_rows, split_rows)
        yield pltpu.make_async_copy(w_any.at[part, at], w_ref.at[at], w_sems.at[i])


def key_value_kernel(*refs, half):
    info_ref, scale_ref, shift_ref, gain_ref, w_any, z_any, noise_any, near_any = refs[:8]
    pair_refs = refs[8 : 7 + half]
    key_ref, value_ref, normed_any, state_any = refs[7 + half : 11 + half]
    state_ref, normed_ref, inverse_ref, w_ref, sem, out_sems, w_sems = refs[11 + half :]
    step = pl.program_id(0)
    rows = state_ref.shape[0]
    piece_rows = noise_any.shape[0]

    def weights_of(part):
        return weight_copies(w_any, part + 1, w_ref.at[part], w_sems.at[part])

    def start_weights():
        for part in range(2):
            for weight_copy in weights_of(part):
                weight_copy.start()

    def piece_at(j, f):
        if j > 0:
            return pair_refs[j - 1], f * piece_rows
        return (noise_any, near_any)[f], 0

    cols = key_ref.shape[1]
    blocks = pl.num_programs(0) // 2
    state_copy = pltpu.make_async_copy(state_ref, state_any, out_sems.at[0])
    normed_copy = pltpu.make_async_copy(normed_ref, normed_any, out_sems.at[1])

    @pl.when(step == 0)
    def _():
        @pl.when(info_ref[0] == 0)
        def _():
            copy = pltpu.make_async_copy(z_any, state_ref, sem.at[0])
            copy.start()
            start_weights()
            copy.wait()

        @pl.when(info_ref[0] != 0)
        def _():
            start_weights()
            for block in range(2 * half):
                high, low = block // 2, block % 2
                steps = lax.rem(high + half - info_ref[1], half)
                other = jnp.abs(low - info_ref[2])
                for j in range(half):
                    for f in range(2):
                        source, row = piece_at(j, f)

                        @pl.when(jnp.logical_and(steps == j, other == f))
                        def _():
                            copy = pltpu.make_async_copy(
                                source.at[pl.ds(row, piece_rows)],
                                state_ref.at[pl.ds(block * piece_rows, piece_rows)],
                                sem.at[0],
                            )
                            copy.start()
                            copy.wait()

        state_copy.start()

        def measure(i, carry):
            at = pl.ds(pl.multiple_of(i * 16, 16), 16)
            state = state_ref[at, :].astype(F32)
            mean = over_lanes(state * state, jnp.add, jnp.sum) * (1.0 / state.shape[1])
            inverse_ref[at, :] = jnp.broadcast_to(lax.rsqrt(mean + EPS), (16, HD))
            return carry

        def apply(i, carry):
            at = pl.ds(pl.multiple_of(i * 16, 16), 16)
            inverse = inverse_ref[at, :][:, :1]
            state = state_ref[at, :].astype(F32) * inverse
            normed_ref[at, :] = (state * scale_ref[...] + shift_ref[...]).astype(BF16)
            return carry

        lax.fori_loop(0, rows // 16, measure, 0, unroll=4)
        lax.fori_loop(0, rows // 16, apply, 0, unroll=2)
        normed_copy.start()

    for part in range(2):

        @pl.when(step == part * blocks)
        def _():
            for copy in weights_of(part):
                copy.wait()

    at = pl.ds(pl.multiple_of(lax.rem(step, blocks) * cols, HD), cols)

    @pl.when(step < blocks)
    def _():
        product = jnp.dot(normed_ref[...], w_ref[0, :, at], preferred_element_type=F32)
        key_ref[...] = head_normalized(product, gain_ref[1:2])

    @pl.when(step >= blocks)
    def _():
        product = jnp.dot(normed_ref[...], w_ref[1, :, at], preferred_element_type=F32)
        value_ref[...] = product.astype(BF16)

    @pl.when(step == pl.num_programs(0) - 1)
    def _():
        state_copy.wait()
        normed_copy.wait()


def project_keys_values(info, scale1, shift, gains, qkv_weight, z, noise, noise_pieces):
    rows, width = z.shape
    head_cols = qkv_weight.shape[2]
    cols = tile_cols(head_cols)
    half = len(noise_pieces)
    blocks = head_cols // cols
    return pl.pallas_call(
        functools.partial(key_value_kernel, half=half),
        grid_spec=pltpu.PrefetchScalarGridSpec(
            num_scalar_prefetch=1,
            grid=(2 * blocks,),
            in_specs=[
                pl.BlockSpec((1, width), lambda j, i: (0, 0)),
                pl.BlockSpec((1, width), lambda j, i: (0, 0)),
                pl.BlockSpec((2, HD), lambda j, i: (0, 0)),
            ]
            + [ANY] * (3 + half),
            out_specs=[
                pl.BlockSpec((rows, cols), lambda j, i: (0, jnp.minimum(j, blocks - 1))),
                pl.BlockSpec((rows, cols), lambda j, i: (0, jnp.maximum(j - blocks, 0))),
                ANY,
                ANY,
            ],
            scratch_shapes=[
                pltpu.VMEM((rows, width), BF16),
                pltpu.VMEM((rows, width), BF16),
                pltpu.VMEM((rows, HD), F32),
                pltpu.VMEM((2, width, head_cols), BF16),
                pltpu.SemaphoreType.DMA((1,)),
                pltpu.SemaphoreType.DMA((2,)),
                pltpu.SemaphoreType.DMA((2, 4)),
            ],
        ),
        out_shape=[
            jax.ShapeDtypeStruct((rows, head_cols), BF16),
            jax.ShapeDtypeStruct((rows, head_cols), BF16),
            jax.ShapeDtypeStruct((rows, width), BF16),
            pltpu.HBM((rows, width), BF16),
        ],
        compiler_params=compiler_params(32),
        cost_estimate=cost(
            4 * rows * width * head_cols,
            6 * rows * width + 4 * rows * head_cols + 4 * width * head_cols,
        ),
        name="norm_keys_values",
    )(
        info,
        scale1,
        shift,
        gains,
        *[in_hbm(a) for a in (qkv_weight, z)],
        noise,
        *noise_pieces,
    )


def attend(query, key):
    return lax.dot_general(query, key, (((1,), (1,)), ((), ())), preferred_element_type=F32)


def weigh(scores, top, values):
    weights = jnp.exp2(scores - top).astype(BF16)
    extended = jnp.concatenate([values, jnp.ones_like(values)], axis=1)
    total = jnp.dot(weights, extended, preferred_element_type=F32)
    return total[:, :HD], total[:, HD:]


def attention_tiles(query, key, finish):
    rows, cols = query.shape
    tile = math.gcd(rows, 256)
    waiting = None
    for h in range(cols // HD):
        at = slice(h * HD, (h + 1) * HD)
        for r in range(rows // tile):
            row = slice(r * tile, (r + 1) * tile)
            scores = attend(query[row, at], key[:, at])
            if waiting is not None:
                finish(*waiting)
            waiting = (scores, row, at)
    finish(*waiting)


def own_kernel(
    gain_ref, normed_ref, key_ref, value_ref, w_any,
    query_ref, acc_ref, top_ref, total_ref, w_ref, w_sems,
):
    step = pl.program_id(0)
    cols = query_ref.shape[1]

    @pl.when(step == 0)
    def _():
        for copy in weight_copies(w_any, 0, w_ref, w_sems):
            copy.start()
        for copy in weight_copies(w_any, 0, w_ref, w_sems):
            copy.wait()

    inside = pl.ds(pl.multiple_of(step * cols, HD), cols)
    product = jnp.dot(normed_ref[...], w_ref[:, inside], preferred_element_type=F32)
    query = head_normalized(product, gain_ref[0:1])
    query_ref[...] = query

    def finish(scores, row, at):
        top = over_lanes(scores, jnp.maximum, jnp.max)
        acc, total = weigh(scores, top, value_ref[:, at])
        acc_ref[row, at] = acc
        total_ref[row, at] = total
        top_ref[row, at] = jnp.broadcast_to(top, acc.shape)

    attention_tiles(query, key_ref, finish)


def own_attention(gains, normed, qkv_weight, key, value):
    rows, width = normed.shape
    head_cols = qkv_weight.shape[2]
    cols = tile_cols(head_cols)
    by_heads = pl.BlockSpec((rows, cols), lambda j: (0, j))
    return pl.pallas_call(
        own_kernel,
        grid=(head_cols // cols,),
        in_specs=[
            pl.BlockSpec((2, HD), lambda j: (0, 0)),
            pl.BlockSpec((rows, width), lambda j: (0, 0)),
            by_heads,
            by_heads,
            ANY,
        ],
        out_specs=[by_heads] * 4,
        scratch_shapes=[
            pltpu.VMEM((width, head_cols), BF16),
            pltpu.SemaphoreType.DMA((4,)),
        ],
        out_shape=[jax.ShapeDtypeStruct((rows, head_cols), BF16)]
        + [jax.ShapeDtypeStruct((rows, head_cols), F32)] * 3,
        compiler_params=compiler_params(32),
        cost_estimate=cost(
            2 * rows * width * head_cols + 8 * rows * rows * head_cols,
            2 * rows * width + 18 * rows * head_cols + 2 * width * head_cols,
            rows * rows * head_cols // HD,
        ),
        name="queries_own_frame",
    )(gains, normed, key, value, in_hbm(qkv_weight))


def earlier_kernel(*refs, chunks):
    info_ref, query_ref, acc_ref, top_ref, total_ref, key_ref, value_ref = refs[:7]
    out_refs = refs[7:]
    rows = query_ref.shape[0] // chunks

    def store(row, at, result):
        for c, out_ref in enumerate(out_refs):
            first, end = max(row.start, c * rows), min(row.stop, (c + 1) * rows)
            if first < end:
                inside = slice(first - c * rows, end - c * rows)
                out_ref[inside, at] = result[first - row.start : end - row.start]

    @pl.when(info_ref[0] != 0)
    def _():
        every = slice(0, query_ref.shape[0])
        store(every, slice(None), (acc_ref[...] / total_ref[...]).astype(BF16))

    @pl.when(info_ref[0] == 0)
    def _():
        def finish(scores, row, at):
            old_top = top_ref[row, at][:, :1]
            top = jnp.maximum(over_lanes(scores, jnp.maximum, jnp.max), old_top)
            acc, total = weigh(scores, top, value_ref[:, at])
            kept = jnp.exp2(old_top - top)
            acc = acc + acc_ref[row, at] * kept
            total = total + total_ref[row, at] * kept
            store(row, at, (acc / total).astype(BF16))

        attention_tiles(query_ref[...], key_ref, finish)


def earlier_attention(info, query, acc, top, total, key, value, chunks):
    rows, head_cols = query.shape
    cols = tile_cols(head_cols)
    return pl.pallas_call(
        functools.partial(earlier_kernel, chunks=chunks),
        grid_spec=pltpu.PrefetchScalarGridSpec(
            num_scalar_prefetch=1,
            grid=(head_cols // cols,),
            in_specs=[pl.BlockSpec((rows, cols), lambda j, i: (0, j))] * 6,
            out_specs=[pl.BlockSpec((rows // chunks, cols), lambda j, i: (0, j))] * chunks,
        ),
        out_shape=[jax.ShapeDtypeStruct((rows // chunks, head_cols), BF16)] * chunks,
        compiler_params=compiler_params(24),
        cost_estimate=cost(
            8 * rows * rows * head_cols,
            22 * rows * head_cols,
            rows * rows * head_cols // HD,
        ),
        name="earlier_frame",
    )(info, query, acc, top, total, key, value)


def output_kernel(*refs, part_counts, whole_weights, half_blocks, last):
    parity_ref = refs[0]
    at = 1
    acc_in = resid_ref = gate_ref = None
    if last:
        acc_in, resid_ref, gate_ref = refs[1:4]
        at = 4
    pieces = []
    for count in part_counts:
        pieces.append(refs[at : at + count])
        at += count
    size = len(part_counts)
    wholes = refs[at : at + whole_weights]
    at += whole_weights
    halves = refs[at : at + 2 * (size - whole_weights)]
    at += 2 * (size - whole_weights)
    out_ref, held_ref, w_ref, held_sems, w_sems = refs[at:]
    step = pl.program_id(0)
    cols = out_ref.shape[1]
    half_width = w_ref.shape[3]

    def weight_copy(half, k):
        if k < whole_weights:
            column = (parity_ref[0] ^ half) * half_width
            source = wholes[k].at[:, pl.ds(pl.multiple_of(column, HD), half_width)]
        else:
            source = halves[half * (size - whole_weights) + k - whole_weights]
        return pltpu.make_async_copy(source, w_ref.at[half, k], w_sems.at[half, k])

    def held_copies(k):
        row = 0
        for number, part in enumerate(pieces[k]):
            count = part.shape[0]
            yield pltpu.make_async_copy(
                part, held_ref.at[k, pl.ds(row, count)], held_sems.at[k, number]
            )
            row += count

    @pl.when(step == 0)
    def _():
        for k in range(size):
            for copy in held_copies(k):
                copy.start()
        for half in range(2):
            for k in range(size):
                weight_copy(half, k).start()
        for k in range(size):
            for copy in held_copies(k):
                copy.wait()

    for half in range(2):

        @pl.when(step == half * half_blocks)
        def _():
            for k in range(size):
                weight_copy(half, k).wait()

    half = step // half_blocks
    tile = tile_cols(cols)
    for t in range(cols // tile):
        at = slice(t * tile, (t + 1) * tile)
        first = lax.rem(step, half_blocks) * cols + t * tile
        inside = pl.ds(pl.multiple_of(first, HD), tile)
        update = acc_in[:, at].astype(F32) if last else None
        for k in range(size):
            term = jnp.dot(held_ref[k], w_ref[half, k, :, inside], preferred_element_type=F32)
            update = term if update is None else update + term
        if last:
            update = resid_ref[:, at].astype(F32) + gate_ref[:, at] * update
        out_ref[:, at] = update.astype(BF16)


def output_projection(parity, pieces, wholes, mine, theirs, finish=None):
    head_cols, half_width = mine[0].shape
    rows = sum(part.shape[0] for part in pieces[0])
    width = 2 * half_width
    size = len(pieces)
    cols = half_width // 2 if half_width % 512 == 0 else half_width
    half_blocks = half_width // cols
    parts = max(len(p) for p in pieces)
    flat = [part for group in pieces for part in group]
    weights = [in_hbm(array) for array in [*wholes, *mine, *theirs]]
    last = finish is not None

    def column(j, parity):
        return 0, ((j // half_blocks) ^ parity[0]) * half_blocks + j % half_blocks

    block = pl.BlockSpec((rows, cols), column)
    return pl.pallas_call(
        functools.partial(
            output_kernel,
            part_counts=tuple(len(p) for p in pieces),
            whole_weights=len(wholes),
            half_blocks=half_blocks,
            last=last,
        ),
        grid_spec=pltpu.PrefetchScalarGridSpec(
            num_scalar_prefetch=1,
            grid=(2 * half_blocks,),
            in_specs=([block, block, pl.BlockSpec((1, cols), column)] if last else [])
            + [ANY] * (len(flat) + len(weights)),
            out_specs=block,
            scratch_shapes=[
                pltpu.VMEM((size, rows, head_cols), BF16),
                pltpu.VMEM((2, size, head_cols, half_width), BF16),
                pltpu.SemaphoreType.DMA((size, parts)),
                pltpu.SemaphoreType.DMA((2, size)),
            ],
        ),
        out_shape=(pltpu.HBM if last else jax.ShapeDtypeStruct)((rows, width), BF16),
        compiler_params=compiler_params(24 if last else 32),
        cost_estimate=cost(
            2 * rows * width * head_cols * size,
            (6 if last else 2) * rows * width + 2 * head_cols * width * size,
        ),
        name="projection_end" if last else "projection_start",
    )(parity, *(finish if last else ()), *flat, *weights)


def send(block, move, queue_size, tensor_size, frames=None):
    pairs = []
    for q in range(queue_size) if frames is None else frames:
        for t in range(tensor_size):
            to_q, to_t = move(q, t)
            pairs.append((q * tensor_size + t, to_q * tensor_size + to_t))
    return lax.ppermute(block, AXES, pairs)


def one_hop(block, queue_size, tensor_size, frames=None):
    half = tensor_size // 2
    args = (queue_size, tensor_size, frames)
    near = send(block, lambda q, t: (q, t ^ 1), *args)
    return [near] + [send(block, away(j, half), *args) for j in range(1, half)]


def two_hops(blocks, queue_size, tensor_size, frames=None):
    half = tensor_size // 2
    args = (queue_size, tensor_size, frames)
    near, far = blocks[0], blocks[1:]
    rows = near.shape[0] // 2
    corners = []
    for j in range(1, half):
        top = send(near[:rows], away(j, half), *args)
        bottom = send(far[j - 1][rows:], lambda q, t: (q, t ^ 1), *args)
        corners.append([top, bottom])
    return corners


def away(j, half):
    return lambda q, t: (q, (t // 2 - j) % half * 2 + t % 2)


def body(
    latents, levels, mod_table, step_size, qkv_weight, q_gain, k_gain, out_weight, fresh_noise
):
    queue_size = lax.axis_size("queue")
    tensor_size = lax.axis_size("tensor")
    rows, width = latents.shape[1:]
    mesh_sizes = (queue_size, tensor_size)
    queue_index = lax.axis_index("queue")
    tensor_index = lax.axis_index("tensor")
    is_last = queue_index == queue_size - 1
    parity = (queue_index % 2).astype(jnp.int32)[None]

    def ring(block, frames=None):
        return send(block, lambda q, t: ((q + 1) % queue_size, t), *mesh_sizes, frames)

    def sibling(block):
        return send(block, lambda q, t: (q ^ 1, t), *mesh_sizes)

    worked_level = send(levels, lambda q, t: ((q - 1) % queue_size, t), *mesh_sizes)[0]

    def gather_noise(noise, at_once):
        args = (*mesh_sizes, [queue_size - 1])
        half = tensor_size // 2
        near = send(noise, lambda q, t: (q, t ^ 1), *args)
        pairs = []
        if at_once:
            for j in range(1, half):
                straight = send(noise, away(j, half), *args)
                across = send(noise, lambda q, t: away(j, half)(q, t ^ 1), *args)
                pairs.append(jnp.concatenate([straight, across], axis=0))
        else:
            pair = jnp.concatenate([noise, near], axis=0)
            pairs = [send(pair, away(j, half), *args) for j in range(1, half)]
        return [near, *pairs]

    noise = fresh_noise[0]
    noise_pieces = gather_noise(noise, True)
    half_weight = lax.dynamic_slice(
        out_weight, (0, parity[0] * (width // 2)), (out_weight.shape[0], width // 2)
    )
    word, noise_pieces = lax.optimization_barrier((levels, noise_pieces))
    word = send(word, lambda q, t: (q - 1, t), *mesh_sizes, [queue_size - 1])
    half_weight, latents, noise_pieces, word = lax.optimization_barrier(
        (half_weight, latents, noise_pieces, word)
    )
    mine = one_hop(half_weight, *mesh_sizes)

    def modulation(level):
        row = lax.dynamic_slice(mod_table, (level, 0), (1, 3 * width)).astype(F32)
        rate = lax.dynamic_slice(step_size, (level,), (1,))[:, None]
        return row[:, :width], 1.0 + row[:, width : 2 * width], rate * row[:, 2 * width :]

    shift, scale1, _ = modulation(worked_level)
    _, _, gate = modulation(levels[0])
    info = jnp.stack([is_last, tensor_index // 2, tensor_index % 2, word[0]])
    info = info.astype(jnp.int32)
    gains = jnp.stack([q_gain * SCORE_SCALE, k_gain])

    frame = latents[0]
    for step_index in range(STEPS):
        final = step_index == STEPS - 1
        key, value, normed, state = project_keys_values(
            info, scale1, shift, gains, qkv_weight, frame, noise, noise_pieces
        )
        to_next = [q for q in range(queue_size) if q != queue_size - 2]
        earlier = [ring(block, to_next) for block in (key, value)]
        query, *own = own_attention(gains, normed, qkv_weight, key, value)
        if not final:
            query, mine = lax.optimization_barrier((query, mine))
            mine_corners = [
                jnp.concatenate(parts, axis=0) for parts in two_hops(mine, *mesh_sizes)
            ]
            mine, earlier = lax.optimization_barrier((mine, earlier))
            theirs = [sibling(block) for block in mine]
            query, theirs = lax.optimization_barrier((query, theirs))
        attended = earlier_attention(
            info, query, *own, *earlier, CHUNKS if final else 1
        )
        senders = range(queue_size) if final else to_next
        targets = range(queue_size if final else queue_size - 1)
        attended = [ring(block, senders) for block in attended]
        sent_state, _ = lax.optimization_barrier((state, attended))
        resid = ring(sent_state, senders)
        if not final:
            attended, mine_corners = lax.optimization_barrier((attended, mine_corners))
        near = [one_hop(block, *mesh_sizes, targets) for block in attended]
        if not final:
            noise, mine_corners, near = lax.optimization_barrier(
                (fresh_noise[step_index + 1], mine_corners, near)
            )
            theirs_corners = [sibling(block) for block in mine_corners]
            noise_pieces = gather_noise(noise, False)
        beyond = [two_hops(blocks, *mesh_sizes, targets) for blocks in near]
        direct = [attended] + [list(parts) for parts in zip(*near)]
        corners = [[half for parts in p for half in parts] for p in zip(*beyond)]
        begun = output_projection(parity, direct, [out_weight], mine, theirs)
        frame = output_projection(
            parity, corners, [], mine_corners, theirs_corners, (begun, resid, gate)
        )
    return frame[None]


def solution(mesh):
    return jax.shard_map(
        body,
        mesh=mesh,
        in_specs=(
            P("queue", None, None),
            P("queue"),
            P(),
            P(),
            P(None, None, "tensor"),
            P(),
            P(),
            P("tensor", None),
            P(None, "tensor", None),
        ),
        out_specs=P("queue", None, None),
        check_vma=False,
    )
```

```python
import functools
import math

import jax
import jax.numpy as jnp
from jax import lax
from jax.experimental import pallas as pl
from jax.experimental.pallas import tpu as pltpu
from jax.sharding import PartitionSpec as P

HD = 128
STEPS = 2
CHUNKS = 2
EPS = 1e-6
AXES = ("queue", "tensor")
F32 = jnp.float32
BF16 = jnp.bfloat16
SCORE_SCALE = math.log2(math.e) / math.sqrt(HD)
ANY = pl.BlockSpec(memory_space=pl.ANY)


def compiler_params(mib):
    return pltpu.CompilerParams(vmem_limit_bytes=mib * 2**20)


def in_hbm(array):
    return pltpu.with_memory_space_constraint(array, pltpu.HBM)


def cost(flops, nbytes, transcendentals=0, share=1000):
    return pl.CostEstimate(
        flops=int(flops) // share,
        bytes_accessed=int(nbytes) // share,
        transcendentals=int(transcendentals) // share,
    )


def head_normalized(values, gain):
    heads = []
    for h in range(values.shape[1] // HD):
        head = values[:, h * HD : (h + 1) * HD]
        mean = jnp.mean(head * head, axis=-1, keepdims=True)
        heads.append((head * lax.rsqrt(mean + EPS) * gain).astype(BF16))
    return heads[0] if len(heads) == 1 else jnp.concatenate(heads, axis=1)


def over_lanes(values, fold, reduce):
    parts = [values[:, i : i + HD] for i in range(0, values.shape[1], HD)]
    return reduce(functools.reduce(fold, parts), axis=-1, keepdims=True)


def tile_cols(head_cols):
    return 256 if head_cols % 256 == 0 else HD


def weight_copies(w_any, part, w_ref, w_sems):
    splits = w_sems.shape[0]
    split_rows = w_ref.shape[0] // splits
    for i in range(splits):
        at = pl.ds(i * split_rows, split_rows)
        yield pltpu.make_async_copy(w_any.at[part, at], w_ref.at[at], w_sems.at[i])


def key_value_kernel(*refs, half):
    info_ref, scale_ref, shift_ref, gain_ref, w_any, z_any, noise_any, near_any = refs[:8]
    pair_refs = refs[8 : 7 + half]
    key_ref, value_ref, normed_any, state_any = refs[7 + half : 11 + half]
    state_ref, normed_ref, inverse_ref, w_ref, sem, out_sems, w_sems = refs[11 + half :]
    step = pl.program_id(0)
    rows, width = state_ref.shape
    piece_rows = noise_any.shape[0]

    def weights_of(part):
        return weight_copies(w_any, part + 1, w_ref.at[part], w_sems.at[part])

    def start_weights():
        for part in range(2):
            for weight_copy in weights_of(part):
                weight_copy.start()

    def piece_at(j, f):
        if j > 0:
            return pair_refs[j - 1], f * piece_rows
        return (noise_any, near_any)[f], 0

    cols = key_ref.shape[1]
    blocks = pl.num_programs(0) // 2
    state_copy = pltpu.make_async_copy(state_ref, state_any, out_sems.at[0])
    normed_copy = pltpu.make_async_copy(normed_ref, normed_any, out_sems.at[1])

    @pl.when(step == 0)
    def _():
        @pl.when(info_ref[0] == 0)
        def _():
            copy = pltpu.make_async_copy(z_any, state_ref, sem.at[0])
            copy.start()
            start_weights()
            copy.wait()

        @pl.when(info_ref[0] != 0)
        def _():
            start_weights()
            for block in range(2 * half):
                high, low = block // 2, block % 2
                steps = lax.rem(high + half - info_ref[1], half)
                other = jnp.abs(low - info_ref[2])
                for j in range(half):
                    for f in range(2):
                        source, row = piece_at(j, f)

                        @pl.when(jnp.logical_and(steps == j, other == f))
                        def _():
                            copy = pltpu.make_async_copy(
                                source.at[pl.ds(row, piece_rows)],
                                state_ref.at[pl.ds(block * piece_rows, piece_rows)],
                                sem.at[0],
                            )
                            copy.start()
                            copy.wait()

        state_copy.start()

        block_rows = math.gcd(rows, 64)

        def measure(i, carry):
            at = pl.ds(pl.multiple_of(i * block_rows, block_rows), block_rows)
            squares = None
            for k in range(0, width, HD):
                part = state_ref[at, k : k + HD].astype(F32)
                squares = part * part if squares is None else squares + part * part
            mean = jnp.sum(squares, axis=-1, keepdims=True) * (1.0 / width)
            inverse_ref[at, :] = jnp.broadcast_to(lax.rsqrt(mean + EPS), (block_rows, HD))
            return carry

        def apply(k, carry):
            at = pl.ds(pl.multiple_of(k * HD, HD), HD)
            state = state_ref[:, at].astype(F32) * inverse_ref[...]
            normed_ref[:, at] = (state * scale_ref[:, at] + shift_ref[:, at]).astype(BF16)
            return carry

        lax.fori_loop(0, rows // block_rows, measure, 0)
        lax.fori_loop(0, width // HD, apply, 0)
        normed_copy.start()

    for part in range(2):

        @pl.when(step == part * blocks)
        def _():
            for copy in weights_of(part):
                copy.wait()

    at = pl.ds(pl.multiple_of(lax.rem(step, blocks) * cols, HD), cols)

    @pl.when(step < blocks)
    def _():
        product = jnp.dot(normed_ref[...], w_ref[0, :, at], preferred_element_type=F32)
        key_ref[...] = head_normalized(product, gain_ref[1:2])

    @pl.when(step >= blocks)
    def _():
        product = jnp.dot(normed_ref[...], w_ref[1, :, at], preferred_element_type=F32)
        value_ref[...] = product.astype(BF16)

    @pl.when(step == pl.num_programs(0) - 1)
    def _():
        state_copy.wait()
        normed_copy.wait()


def project_keys_values(info, scale1, shift, gains, qkv_weight, z, noise, noise_pieces):
    rows, width = z.shape
    head_cols = qkv_weight.shape[2]
    cols = tile_cols(head_cols)
    half = len(noise_pieces)
    blocks = head_cols // cols
    return pl.pallas_call(
        functools.partial(key_value_kernel, half=half),
        grid_spec=pltpu.PrefetchScalarGridSpec(
            num_scalar_prefetch=1,
            grid=(2 * blocks,),
            in_specs=[
                pl.BlockSpec((1, width), lambda j, i: (0, 0)),
                pl.BlockSpec((1, width), lambda j, i: (0, 0)),
                pl.BlockSpec((2, HD), lambda j, i: (0, 0)),
            ]
            + [ANY] * (3 + half),
            out_specs=[
                pl.BlockSpec((rows, cols), lambda j, i: (0, jnp.minimum(j, blocks - 1))),
                pl.BlockSpec((rows, cols), lambda j, i: (0, jnp.maximum(j - blocks, 0))),
                ANY,
                ANY,
            ],
            scratch_shapes=[
                pltpu.VMEM((rows, width), BF16),
                pltpu.VMEM((rows, width), BF16),
                pltpu.VMEM((rows, HD), F32),
                pltpu.VMEM((2, width, head_cols), BF16),
                pltpu.SemaphoreType.DMA((1,)),
                pltpu.SemaphoreType.DMA((2,)),
                pltpu.SemaphoreType.DMA((2, 4)),
            ],
        ),
        out_shape=[
            jax.ShapeDtypeStruct((rows, head_cols), BF16),
            jax.ShapeDtypeStruct((rows, head_cols), BF16),
            jax.ShapeDtypeStruct((rows, width), BF16),
            pltpu.HBM((rows, width), BF16),
        ],
        compiler_params=compiler_params(32),
        cost_estimate=cost(
            4 * rows * width * head_cols,
            6 * rows * width + 4 * rows * head_cols + 4 * width * head_cols,
        ),
        name="norm_keys_values",
    )(
        info,
        scale1,
        shift,
        gains,
        *[in_hbm(a) for a in (qkv_weight, z)],
        noise,
        *noise_pieces,
    )


def attend(query, key):
    return lax.dot_general(query, key, (((1,), (1,)), ((), ())), preferred_element_type=F32)


def weigh(scores, top, values):
    weights = jnp.exp2(scores - top).astype(BF16)
    extended = jnp.concatenate([values, jnp.ones_like(values)], axis=1)
    total = jnp.dot(weights, extended, preferred_element_type=F32)
    return total[:, :HD], total[:, HD:]


def attention_tiles(query, key, finish):
    rows, cols = query.shape
    tile = math.gcd(rows, 256)
    waiting = None
    for h in range(cols // HD):
        at = slice(h * HD, (h + 1) * HD)
        for r in range(rows // tile):
            row = slice(r * tile, (r + 1) * tile)
            scores = attend(query[row, at], key[:, at])
            if waiting is not None:
                finish(*waiting)
            waiting = (scores, row, at)
    finish(*waiting)


def own_kernel(
    gain_ref, normed_ref, key_ref, value_ref, w_any,
    query_ref, acc_ref, top_ref, total_ref, w_ref, w_sems,
):
    step = pl.program_id(0)
    cols = query_ref.shape[1]

    @pl.when(step == 0)
    def _():
        for copy in weight_copies(w_any, 0, w_ref, w_sems):
            copy.start()
        for copy in weight_copies(w_any, 0, w_ref, w_sems):
            copy.wait()

    inside = pl.ds(pl.multiple_of(step * cols, HD), cols)
    product = jnp.dot(normed_ref[...], w_ref[:, inside], preferred_element_type=F32)
    query = head_normalized(product, gain_ref[0:1])
    query_ref[...] = query

    def finish(scores, row, at):
        top = over_lanes(scores, jnp.maximum, jnp.max)
        acc, total = weigh(scores, top, value_ref[:, at])
        acc_ref[row, at] = acc
        total_ref[row, at] = total
        top_ref[row, at] = jnp.broadcast_to(top, acc.shape)

    attention_tiles(query, key_ref, finish)


def own_attention(gains, normed, qkv_weight, key, value):
    rows, width = normed.shape
    head_cols = qkv_weight.shape[2]
    cols = tile_cols(head_cols)
    by_heads = pl.BlockSpec((rows, cols), lambda j: (0, j))
    return pl.pallas_call(
        own_kernel,
        grid=(head_cols // cols,),
        in_specs=[
            pl.BlockSpec((2, HD), lambda j: (0, 0)),
            pl.BlockSpec((rows, width), lambda j: (0, 0)),
            by_heads,
            by_heads,
            ANY,
        ],
        out_specs=[by_heads] * 4,
        scratch_shapes=[
            pltpu.VMEM((width, head_cols), BF16),
            pltpu.SemaphoreType.DMA((4,)),
        ],
        out_shape=[jax.ShapeDtypeStruct((rows, head_cols), BF16)]
        + [jax.ShapeDtypeStruct((rows, head_cols), F32)] * 3,
        compiler_params=compiler_params(32),
        cost_estimate=cost(
            2 * rows * width * head_cols + 8 * rows * rows * head_cols,
            2 * rows * width + 18 * rows * head_cols + 2 * width * head_cols,
            rows * rows * head_cols // HD,
        ),
        name="queries_own_frame",
    )(gains, normed, key, value, in_hbm(qkv_weight))


def earlier_kernel(*refs, chunks):
    info_ref, query_ref, acc_ref, top_ref, total_ref, key_ref, value_ref = refs[:7]
    out_refs = refs[7:]
    rows = query_ref.shape[0] // chunks

    def store(row, at, result):
        for c, out_ref in enumerate(out_refs):
            first, end = max(row.start, c * rows), min(row.stop, (c + 1) * rows)
            if first < end:
                inside = slice(first - c * rows, end - c * rows)
                out_ref[inside, at] = result[first - row.start : end - row.start]

    @pl.when(info_ref[0] != 0)
    def _():
        every = slice(0, query_ref.shape[0])
        store(every, slice(None), (acc_ref[...] / total_ref[...]).astype(BF16))

    @pl.when(info_ref[0] == 0)
    def _():
        def finish(scores, row, at):
            old_top = top_ref[row, at][:, :1]
            top = jnp.maximum(over_lanes(scores, jnp.maximum, jnp.max), old_top)
            acc, total = weigh(scores, top, value_ref[:, at])
            kept = jnp.exp2(old_top - top)
            acc = acc + acc_ref[row, at] * kept
            total = total + total_ref[row, at] * kept
            store(row, at, (acc / total).astype(BF16))

        attention_tiles(query_ref[...], key_ref, finish)


def earlier_attention(info, query, acc, top, total, key, value, chunks):
    rows, head_cols = query.shape
    cols = tile_cols(head_cols)
    return pl.pallas_call(
        functools.partial(earlier_kernel, chunks=chunks),
        grid_spec=pltpu.PrefetchScalarGridSpec(
            num_scalar_prefetch=1,
            grid=(head_cols // cols,),
            in_specs=[pl.BlockSpec((rows, cols), lambda j, i: (0, j))] * 6,
            out_specs=[pl.BlockSpec((rows // chunks, cols), lambda j, i: (0, j))] * chunks,
        ),
        out_shape=[jax.ShapeDtypeStruct((rows // chunks, head_cols), BF16)] * chunks,
        compiler_params=compiler_params(24),
        cost_estimate=cost(
            8 * rows * rows * head_cols,
            22 * rows * head_cols,
            rows * rows * head_cols // HD,
        ),
        name="earlier_frame",
    )(info, query, acc, top, total, key, value)


def output_kernel(*refs, part_counts, whole_weights, half_blocks, last):
    parity_ref = refs[0]
    at = 1
    acc_in = resid_ref = gate_ref = None
    if last:
        acc_in, resid_ref, gate_ref = refs[1:4]
        at = 4
    pieces = []
    for count in part_counts:
        pieces.append(refs[at : at + count])
        at += count
    size = len(part_counts)
    wholes = refs[at : at + whole_weights]
    at += whole_weights
    halves = refs[at : at + 2 * (size - whole_weights)]
    at += 2 * (size - whole_weights)
    out_ref, held_ref, w_ref, held_sems, w_sems = refs[at:]
    step = pl.program_id(0)
    cols = out_ref.shape[1]
    half_width = w_ref.shape[3]

    def weight_copy(half, k):
        if k < whole_weights:
            column = (parity_ref[0] ^ half) * half_width
            source = wholes[k].at[:, pl.ds(pl.multiple_of(column, HD), half_width)]
        else:
            source = halves[half * (size - whole_weights) + k - whole_weights]
        return pltpu.make_async_copy(source, w_ref.at[half, k], w_sems.at[half, k])

    def held_copies(k):
        row = 0
        for number, part in enumerate(pieces[k]):
            count = part.shape[0]
            yield pltpu.make_async_copy(
                part, held_ref.at[k, pl.ds(row, count)], held_sems.at[k, number]
            )
            row += count

    @pl.when(step == 0)
    def _():
        for k in range(size):
            for copy in held_copies(k):
                copy.start()
        for half in range(2):
            for k in range(size):
                weight_copy(half, k).start()
        for k in range(size):
            for copy in held_copies(k):
                copy.wait()

    for half in range(2):

        @pl.when(step == half * half_blocks)
        def _():
            for k in range(size):
                weight_copy(half, k).wait()

    half = step // half_blocks
    tile = tile_cols(cols)
    for t in range(cols // tile):
        at = slice(t * tile, (t + 1) * tile)
        first = lax.rem(step, half_blocks) * cols + t * tile
        inside = pl.ds(pl.multiple_of(first, HD), tile)
        update = acc_in[:, at].astype(F32) if last else None
        for k in range(size):
            term = jnp.dot(held_ref[k], w_ref[half, k, :, inside], preferred_element_type=F32)
            update = term if update is None else update + term
        if last:
            update = resid_ref[:, at].astype(F32) + gate_ref[:, at] * update
        out_ref[:, at] = update.astype(BF16)


def output_projection(parity, pieces, wholes, mine, theirs, finish=None):
    head_cols, half_width = mine[0].shape
    rows = sum(part.shape[0] for part in pieces[0])
    width = 2 * half_width
    size = len(pieces)
    cols = half_width // 2 if half_width % 512 == 0 else half_width
    half_blocks = half_width // cols
    parts = max(len(p) for p in pieces)
    flat = [part for group in pieces for part in group]
    weights = [in_hbm(array) for array in [*wholes, *mine, *theirs]]
    last = finish is not None

    def column(j, parity):
        return 0, ((j // half_blocks) ^ parity[0]) * half_blocks + j % half_blocks

    block = pl.BlockSpec((rows, cols), column)
    return pl.pallas_call(
        functools.partial(
            output_kernel,
            part_counts=tuple(len(p) for p in pieces),
            whole_weights=len(wholes),
            half_blocks=half_blocks,
            last=last,
        ),
        grid_spec=pltpu.PrefetchScalarGridSpec(
            num_scalar_prefetch=1,
            grid=(2 * half_blocks,),
            in_specs=([block, block, pl.BlockSpec((1, cols), column)] if last else [])
            + [ANY] * (len(flat) + len(weights)),
            out_specs=block,
            scratch_shapes=[
                pltpu.VMEM((size, rows, head_cols), BF16),
                pltpu.VMEM((2, size, head_cols, half_width), BF16),
                pltpu.SemaphoreType.DMA((size, parts)),
                pltpu.SemaphoreType.DMA((2, size)),
            ],
        ),
        out_shape=(pltpu.HBM if last else jax.ShapeDtypeStruct)((rows, width), BF16),
        compiler_params=compiler_params(24 if last else 32),
        cost_estimate=cost(
            2 * rows * width * head_cols * size,
            (6 if last else 2) * rows * width + 2 * head_cols * width * size,
        ),
        name="projection_end" if last else "projection_start",
    )(parity, *(finish if last else ()), *flat, *weights)


def send(block, move, queue_size, tensor_size, frames=None):
    pairs = []
    for q in range(queue_size) if frames is None else frames:
        for t in range(tensor_size):
            to_q, to_t = move(q, t)
            pairs.append((q * tensor_size + t, to_q * tensor_size + to_t))
    return lax.ppermute(block, AXES, pairs)


def one_hop(block, queue_size, tensor_size, frames=None):
    half = tensor_size // 2
    args = (queue_size, tensor_size, frames)
    near = send(block, lambda q, t: (q, t ^ 1), *args)
    return [near] + [send(block, away(j, half), *args) for j in range(1, half)]


def two_hops(blocks, queue_size, tensor_size, frames=None):
    half = tensor_size // 2
    args = (queue_size, tensor_size, frames)
    near, far = blocks[0], blocks[1:]
    rows = near.shape[0] // 2
    corners = []
    for j in range(1, half):
        top = send(near[:rows], away(j, half), *args)
        bottom = send(far[j - 1][rows:], lambda q, t: (q, t ^ 1), *args)
        corners.append([top, bottom])
    return corners


def away(j, half):
    return lambda q, t: (q, (t // 2 - j) % half * 2 + t % 2)


def body(
    latents, levels, mod_table, step_size, qkv_weight, q_gain, k_gain, out_weight, fresh_noise
):
    queue_size = lax.axis_size("queue")
    tensor_size = lax.axis_size("tensor")
    rows, width = latents.shape[1:]
    mesh_sizes = (queue_size, tensor_size)
    queue_index = lax.axis_index("queue")
    tensor_index = lax.axis_index("tensor")
    is_last = queue_index == queue_size - 1
    parity = (queue_index % 2).astype(jnp.int32)[None]

    def ring(block, frames=None):
        return send(block, lambda q, t: ((q + 1) % queue_size, t), *mesh_sizes, frames)

    def sibling(block):
        return send(block, lambda q, t: (q ^ 1, t), *mesh_sizes)

    worked_level = send(levels, lambda q, t: ((q - 1) % queue_size, t), *mesh_sizes)[0]

    def gather_noise(noise, at_once):
        args = (*mesh_sizes, [queue_size - 1])
        half = tensor_size // 2
        near = send(noise, lambda q, t: (q, t ^ 1), *args)
        pairs = []
        if at_once:
            for j in range(1, half):
                straight = send(noise, away(j, half), *args)
                across = send(
                    noise,
                    lambda q, t: away(j, half)(queue_size - 1, t ^ 1),
                    *mesh_sizes,
                    [max(queue_size - 3, 0)],
                )
                pairs.append(jnp.concatenate([straight, across], axis=0))
        else:
            pair = jnp.concatenate([noise, near], axis=0)
            pairs = [send(pair, away(j, half), *args) for j in range(1, half)]
        return [near, *pairs]

    noise = fresh_noise[0]
    noise_pieces = gather_noise(noise, True)
    half_weight = lax.dynamic_slice(
        out_weight, (0, parity[0] * (width // 2)), (out_weight.shape[0], width // 2)
    )
    half_weight, latents, noise_pieces = lax.optimization_barrier(
        (half_weight, latents, noise_pieces)
    )
    mine = one_hop(half_weight, *mesh_sizes)

    def modulation(level):
        row = lax.dynamic_slice(mod_table, (level, 0), (1, 3 * width)).astype(F32)
        rate = lax.dynamic_slice(step_size, (level,), (1,))[:, None]
        return row[:, :width], 1.0 + row[:, width : 2 * width], rate * row[:, 2 * width :]

    shift, scale1, _ = modulation(worked_level)
    _, _, gate = modulation(levels[0])
    info = jnp.stack([is_last, tensor_index // 2, tensor_index % 2])
    info = info.astype(jnp.int32)
    gains = jnp.stack([q_gain * SCORE_SCALE, k_gain])

    frame = latents[0]
    for step_index in range(STEPS):
        final = step_index == STEPS - 1
        key, value, normed, state = project_keys_values(
            info, scale1, shift, gains, qkv_weight, frame, noise, noise_pieces
        )
        to_next = [q for q in range(queue_size) if q != queue_size - 2]
        earlier = [ring(block, to_next) for block in (key, value)]
        query, *own = own_attention(gains, normed, qkv_weight, key, value)
        if not final:
            query, mine = lax.optimization_barrier((query, mine))
            mine_corners = [
                jnp.concatenate(parts, axis=0) for parts in two_hops(mine, *mesh_sizes)
            ]
            mine, earlier = lax.optimization_barrier((mine, earlier))
            theirs = [sibling(block) for block in mine]
            query, theirs = lax.optimization_barrier((query, theirs))
        attended = earlier_attention(
            info, query, *own, *earlier, CHUNKS if final else 1
        )
        senders = range(queue_size) if final else to_next
        targets = range(queue_size if final else queue_size - 1)
        attended = [ring(block, senders) for block in attended]
        sent_state, _ = lax.optimization_barrier((state, attended))
        resid = ring(sent_state, senders)
        if not final:
            attended, mine_corners = lax.optimization_barrier((attended, mine_corners))
        near = [one_hop(block, *mesh_sizes, targets) for block in attended]
        if not final:
            noise, mine_corners, near = lax.optimization_barrier(
                (fresh_noise[step_index + 1], mine_corners, near)
            )
            theirs_corners = [sibling(block) for block in mine_corners]
            noise_pieces = gather_noise(noise, False)
        beyond = [two_hops(blocks, *mesh_sizes, targets) for blocks in near]
        direct = [attended] + [list(parts) for parts in zip(*near)]
        corners = [[half for parts in p for half in parts] for p in zip(*beyond)]
        begun = output_projection(parity, direct, [out_weight], mine, theirs)
        frame = output_projection(
            parity, corners, [], mine_corners, theirs_corners, (begun, resid, gate)
        )
    return frame[None]


def solution(mesh):
    return jax.shard_map(
        body,
        mesh=mesh,
        in_specs=(
            P("queue", None, None),
            P("queue"),
            P(),
            P(),
            P(None, None, "tensor"),
            P(),
            P(),
            P("tensor", None),
            P(None, "tensor", None),
        ),
        out_specs=P("queue", None, None),
        check_vma=False,
    )
```

```python
import functools
import math

import jax
import jax.numpy as jnp
from jax import lax
from jax.experimental import pallas as pl
from jax.experimental.pallas import tpu as pltpu
from jax.sharding import PartitionSpec as P

HD = 128
STEPS = 2
CHUNKS = 2
EPS = 1e-6
AXES = ("queue", "tensor")
F32 = jnp.float32
BF16 = jnp.bfloat16
SCORE_SCALE = math.log2(math.e) / math.sqrt(HD)
ANY = pl.BlockSpec(memory_space=pl.ANY)


def compiler_params(mib):
    return pltpu.CompilerParams(vmem_limit_bytes=mib * 2**20)


def in_hbm(array):
    return pltpu.with_memory_space_constraint(array, pltpu.HBM)


def cost(flops, nbytes, transcendentals=0, share=1000):
    return pl.CostEstimate(
        flops=int(flops) // share,
        bytes_accessed=int(nbytes) // share,
        transcendentals=int(transcendentals) // share,
    )


def head_normalized(values, gain):
    heads = []
    for h in range(values.shape[1] // HD):
        head = values[:, h * HD : (h + 1) * HD]
        mean = jnp.mean(head * head, axis=-1, keepdims=True)
        heads.append((head * lax.rsqrt(mean + EPS) * gain).astype(BF16))
    return heads[0] if len(heads) == 1 else jnp.concatenate(heads, axis=1)


def over_lanes(values, fold, reduce):
    parts = [values[:, i : i + HD] for i in range(0, values.shape[1], HD)]
    return reduce(functools.reduce(fold, parts), axis=-1, keepdims=True)


def tile_cols(head_cols):
    return 256 if head_cols % 256 == 0 else HD


def weight_copies(w_any, part, w_ref, w_sems):
    splits = w_sems.shape[0]
    split_rows = w_ref.shape[0] // splits
    for i in range(splits):
        at = pl.ds(i * split_rows, split_rows)
        yield pltpu.make_async_copy(w_any.at[part, at], w_ref.at[at], w_sems.at[i])


def key_value_kernel(*refs, half):
    info_ref, scale_ref, shift_ref, gain_ref, w_any, z_any, noise_any, near_any = refs[:8]
    pair_refs = refs[8 : 7 + half]
    key_ref, value_ref, normed_any, state_any = refs[7 + half : 11 + half]
    state_ref, normed_ref, inverse_ref, w_ref, sem, out_sems, w_sems = refs[11 + half :]
    step = pl.program_id(0)
    rows, width = state_ref.shape
    piece_rows = noise_any.shape[0]

    def weights_of(part):
        return weight_copies(w_any, part + 1, w_ref.at[part], w_sems.at[part])

    def start_weights():
        for part in range(2):
            for weight_copy in weights_of(part):
                weight_copy.start()

    def piece_at(j, f):
        if j > 0:
            return pair_refs[j - 1], f * piece_rows
        return (noise_any, near_any)[f], 0

    cols = key_ref.shape[1]
    blocks = pl.num_programs(0) // 2
    state_copy = pltpu.make_async_copy(state_ref, state_any, out_sems.at[0])
    normed_copy = pltpu.make_async_copy(normed_ref, normed_any, out_sems.at[1])

    @pl.when(step == 0)
    def _():
        @pl.when(info_ref[0] == 0)
        def _():
            copy = pltpu.make_async_copy(z_any, state_ref, sem.at[0])
            copy.start()
            copy.wait()
            start_weights()

        @pl.when(info_ref[0] != 0)
        def _():
            start_weights()
            for block in range(2 * half):
                high, low = block // 2, block % 2
                steps = lax.rem(high + half - info_ref[1], half)
                other = jnp.abs(low - info_ref[2])
                for j in range(half):
                    for f in range(2):
                        source, row = piece_at(j, f)

                        @pl.when(jnp.logical_and(steps == j, other == f))
                        def _():
                            copy = pltpu.make_async_copy(
                                source.at[pl.ds(row, piece_rows)],
                                state_ref.at[pl.ds(block * piece_rows, piece_rows)],
                                sem.at[0],
                            )
                            copy.start()
                            copy.wait()

        state_copy.start()

        block_rows = math.gcd(rows, 64)

        def measure(i, carry):
            at = pl.ds(pl.multiple_of(i * block_rows, block_rows), block_rows)
            squares = None
            for k in range(0, width, HD):
                part = state_ref[at, k : k + HD].astype(F32)
                squares = part * part if squares is None else squares + part * part
            mean = jnp.sum(squares, axis=-1, keepdims=True) * (1.0 / width)
            inverse_ref[at, :] = jnp.broadcast_to(lax.rsqrt(mean + EPS), (block_rows, HD))
            return carry

        def apply(k, carry):
            at = pl.ds(pl.multiple_of(k * HD, HD), HD)
            state = state_ref[:, at].astype(F32) * inverse_ref[...]
            normed_ref[:, at] = (state * scale_ref[:, at] + shift_ref[:, at]).astype(BF16)
            return carry

        lax.fori_loop(0, rows // block_rows, measure, 0)
        lax.fori_loop(0, width // HD, apply, 0)
        normed_copy.start()

    for part in range(2):

        @pl.when(step == part * blocks)
        def _():
            for copy in weights_of(part):
                copy.wait()

    at = pl.ds(pl.multiple_of(lax.rem(step, blocks) * cols, HD), cols)

    @pl.when(step < blocks)
    def _():
        product = jnp.dot(normed_ref[...], w_ref[0, :, at], preferred_element_type=F32)
        key_ref[...] = head_normalized(product, gain_ref[1:2])

    @pl.when(step >= blocks)
    def _():
        product = jnp.dot(normed_ref[...], w_ref[1, :, at], preferred_element_type=F32)
        value_ref[...] = product.astype(BF16)

    @pl.when(step == pl.num_programs(0) - 1)
    def _():
        state_copy.wait()
        normed_copy.wait()


def project_keys_values(info, scale1, shift, gains, qkv_weight, z, noise, noise_pieces):
    rows, width = z.shape
    head_cols = qkv_weight.shape[2]
    cols = tile_cols(head_cols)
    half = len(noise_pieces)
    blocks = head_cols // cols
    return pl.pallas_call(
        functools.partial(key_value_kernel, half=half),
        grid_spec=pltpu.PrefetchScalarGridSpec(
            num_scalar_prefetch=1,
            grid=(2 * blocks,),
            in_specs=[
                pl.BlockSpec((1, width), lambda j, i: (0, 0)),
                pl.BlockSpec((1, width), lambda j, i: (0, 0)),
                pl.BlockSpec((2, HD), lambda j, i: (0, 0)),
            ]
            + [ANY] * (3 + half),
            out_specs=[
                pl.BlockSpec((rows, cols), lambda j, i: (0, jnp.minimum(j, blocks - 1))),
                pl.BlockSpec((rows, cols), lambda j, i: (0, jnp.maximum(j - blocks, 0))),
                ANY,
                ANY,
            ],
            scratch_shapes=[
                pltpu.VMEM((rows, width), BF16),
                pltpu.VMEM((rows, width), BF16),
                pltpu.VMEM((rows, HD), F32),
                pltpu.VMEM((2, width, head_cols), BF16),
                pltpu.SemaphoreType.DMA((1,)),
                pltpu.SemaphoreType.DMA((2,)),
                pltpu.SemaphoreType.DMA((2, 4)),
            ],
        ),
        out_shape=[
            jax.ShapeDtypeStruct((rows, head_cols), BF16),
            jax.ShapeDtypeStruct((rows, head_cols), BF16),
            jax.ShapeDtypeStruct((rows, width), BF16),
            pltpu.HBM((rows, width), BF16),
        ],
        compiler_params=compiler_params(32),
        cost_estimate=cost(
            4 * rows * width * head_cols,
            6 * rows * width + 4 * rows * head_cols + 4 * width * head_cols,
        ),
        name="norm_keys_values",
    )(
        info,
        scale1,
        shift,
        gains,
        *[in_hbm(a) for a in (qkv_weight, z)],
        noise,
        *noise_pieces,
    )


def attend(query, key):
    return lax.dot_general(query, key, (((1,), (1,)), ((), ())), preferred_element_type=F32)


def weigh(scores, top, values):
    weights = jnp.exp2(scores - top).astype(BF16)
    extended = jnp.concatenate([values, jnp.ones_like(values)], axis=1)
    total = jnp.dot(weights, extended, preferred_element_type=F32)
    return total[:, :HD], total[:, HD:]


def attention_tiles(query, key, finish):
    rows, cols = query.shape
    tile = math.gcd(rows, 256)
    waiting = None
    for h in range(cols // HD):
        at = slice(h * HD, (h + 1) * HD)
        for r in range(rows // tile):
            row = slice(r * tile, (r + 1) * tile)
            scores = attend(query[row, at], key[:, at])
            if waiting is not None:
                finish(*waiting)
            waiting = (scores, row, at)
    finish(*waiting)


def own_kernel(
    gain_ref, normed_ref, key_ref, value_ref, w_any,
    query_ref, acc_ref, top_ref, total_ref, w_ref, w_sems,
):
    step = pl.program_id(0)
    cols = query_ref.shape[1]

    @pl.when(step == 0)
    def _():
        for copy in weight_copies(w_any, 0, w_ref, w_sems):
            copy.start()
        for copy in weight_copies(w_any, 0, w_ref, w_sems):
            copy.wait()

    inside = pl.ds(pl.multiple_of(step * cols, HD), cols)
    product = jnp.dot(normed_ref[...], w_ref[:, inside], preferred_element_type=F32)
    query = head_normalized(product, gain_ref[0:1])
    query_ref[...] = query

    def finish(scores, row, at):
        top = over_lanes(scores, jnp.maximum, jnp.max)
        acc, total = weigh(scores, top, value_ref[:, at])
        acc_ref[row, at] = acc
        total_ref[row, at] = total
        top_ref[row, at] = jnp.broadcast_to(top, acc.shape)

    attention_tiles(query, key_ref, finish)


def own_attention(gains, normed, qkv_weight, key, value):
    rows, width = normed.shape
    head_cols = qkv_weight.shape[2]
    cols = tile_cols(head_cols)
    by_heads = pl.BlockSpec((rows, cols), lambda j: (0, j))
    return pl.pallas_call(
        own_kernel,
        grid=(head_cols // cols,),
        in_specs=[
            pl.BlockSpec((2, HD), lambda j: (0, 0)),
            pl.BlockSpec((rows, width), lambda j: (0, 0)),
            by_heads,
            by_heads,
            ANY,
        ],
        out_specs=[by_heads] * 4,
        scratch_shapes=[
            pltpu.VMEM((width, head_cols), BF16),
            pltpu.SemaphoreType.DMA((4,)),
        ],
        out_shape=[jax.ShapeDtypeStruct((rows, head_cols), BF16)]
        + [jax.ShapeDtypeStruct((rows, head_cols), F32)] * 3,
        compiler_params=compiler_params(32),
        cost_estimate=cost(
            2 * rows * width * head_cols + 8 * rows * rows * head_cols,
            2 * rows * width + 18 * rows * head_cols + 2 * width * head_cols,
            rows * rows * head_cols // HD,
        ),
        name="queries_own_frame",
    )(gains, normed, key, value, in_hbm(qkv_weight))


def earlier_kernel(*refs, chunks):
    info_ref, query_ref, acc_ref, top_ref, total_ref, key_ref, value_ref = refs[:7]
    out_refs = refs[7:]
    rows = query_ref.shape[0] // chunks

    def store(row, at, result):
        for c, out_ref in enumerate(out_refs):
            first, end = max(row.start, c * rows), min(row.stop, (c + 1) * rows)
            if first < end:
                inside = slice(first - c * rows, end - c * rows)
                out_ref[inside, at] = result[first - row.start : end - row.start]

    @pl.when(info_ref[0] != 0)
    def _():
        every = slice(0, query_ref.shape[0])
        store(every, slice(None), (acc_ref[...] / total_ref[...]).astype(BF16))

    @pl.when(info_ref[0] == 0)
    def _():
        def finish(scores, row, at):
            old_top = top_ref[row, at][:, :1]
            top = jnp.maximum(over_lanes(scores, jnp.maximum, jnp.max), old_top)
            acc, total = weigh(scores, top, value_ref[:, at])
            kept = jnp.exp2(old_top - top)
            acc = acc + acc_ref[row, at] * kept
            total = total + total_ref[row, at] * kept
            store(row, at, (acc / total).astype(BF16))

        attention_tiles(query_ref[...], key_ref, finish)


def earlier_attention(info, query, acc, top, total, key, value, chunks):
    rows, head_cols = query.shape
    cols = tile_cols(head_cols)
    return pl.pallas_call(
        functools.partial(earlier_kernel, chunks=chunks),
        grid_spec=pltpu.PrefetchScalarGridSpec(
            num_scalar_prefetch=1,
            grid=(head_cols // cols,),
            in_specs=[pl.BlockSpec((rows, cols), lambda j, i: (0, j))] * 6,
            out_specs=[pl.BlockSpec((rows // chunks, cols), lambda j, i: (0, j))] * chunks,
        ),
        out_shape=[jax.ShapeDtypeStruct((rows // chunks, head_cols), BF16)] * chunks,
        compiler_params=compiler_params(24),
        cost_estimate=cost(
            8 * rows * rows * head_cols,
            22 * rows * head_cols,
            rows * rows * head_cols // HD,
        ),
        name="earlier_frame",
    )(info, query, acc, top, total, key, value)


def output_kernel(*refs, part_counts, whole_weights, half_blocks, last):
    parity_ref = refs[0]
    at = 1
    acc_in = resid_ref = gate_ref = None
    if last:
        acc_in, resid_ref, gate_ref = refs[1:4]
        at = 4
    pieces = []
    for count in part_counts:
        pieces.append(refs[at : at + count])
        at += count
    size = len(part_counts)
    wholes = refs[at : at + whole_weights]
    at += whole_weights
    halves = refs[at : at + 2 * (size - whole_weights)]
    at += 2 * (size - whole_weights)
    out_ref, held_ref, w_ref, held_sems, w_sems = refs[at:]
    step = pl.program_id(0)
    cols = out_ref.shape[1]
    half_width = w_ref.shape[3]

    def weight_copy(half, k):
        if k < whole_weights:
            column = (parity_ref[0] ^ half) * half_width
            source = wholes[k].at[:, pl.ds(pl.multiple_of(column, HD), half_width)]
        else:
            source = halves[half * (size - whole_weights) + k - whole_weights]
        return pltpu.make_async_copy(source, w_ref.at[half, k], w_sems.at[half, k])

    def held_copies(k):
        row = 0
        for number, part in enumerate(pieces[k]):
            count = part.shape[0]
            yield pltpu.make_async_copy(
                part, held_ref.at[k, pl.ds(row, count)], held_sems.at[k, number]
            )
            row += count

    @pl.when(step == 0)
    def _():
        for k in range(size):
            for copy in held_copies(k):
                copy.start()
        for half in range(2):
            for k in range(size):
                weight_copy(half, k).start()
        for k in range(size):
            for copy in held_copies(k):
                copy.wait()

    for half in range(2):

        @pl.when(step == half * half_blocks)
        def _():
            for k in range(size):
                weight_copy(half, k).wait()

    half = step // half_blocks
    tile = tile_cols(cols)
    for t in range(cols // tile):
        at = slice(t * tile, (t + 1) * tile)
        first = lax.rem(step, half_blocks) * cols + t * tile
        inside = pl.ds(pl.multiple_of(first, HD), tile)
        update = acc_in[:, at].astype(F32) if last else None
        for k in range(size):
            term = jnp.dot(held_ref[k], w_ref[half, k, :, inside], preferred_element_type=F32)
            update = term if update is None else update + term
        if last:
            update = resid_ref[:, at].astype(F32) + gate_ref[:, at] * update
        out_ref[:, at] = update.astype(BF16)


def output_projection(parity, pieces, wholes, mine, theirs, finish=None):
    head_cols, half_width = mine[0].shape
    rows = sum(part.shape[0] for part in pieces[0])
    width = 2 * half_width
    size = len(pieces)
    cols = half_width // 2 if half_width % 512 == 0 else half_width
    half_blocks = half_width // cols
    parts = max(len(p) for p in pieces)
    flat = [part for group in pieces for part in group]
    weights = [in_hbm(array) for array in [*wholes, *mine, *theirs]]
    last = finish is not None

    def column(j, parity):
        return 0, ((j // half_blocks) ^ parity[0]) * half_blocks + j % half_blocks

    block = pl.BlockSpec((rows, cols), column)
    return pl.pallas_call(
        functools.partial(
            output_kernel,
            part_counts=tuple(len(p) for p in pieces),
            whole_weights=len(wholes),
            half_blocks=half_blocks,
            last=last,
        ),
        grid_spec=pltpu.PrefetchScalarGridSpec(
            num_scalar_prefetch=1,
            grid=(2 * half_blocks,),
            in_specs=([block, block, pl.BlockSpec((1, cols), column)] if last else [])
            + [ANY] * (len(flat) + len(weights)),
            out_specs=block,
            scratch_shapes=[
                pltpu.VMEM((size, rows, head_cols), BF16),
                pltpu.VMEM((2, size, head_cols, half_width), BF16),
                pltpu.SemaphoreType.DMA((size, parts)),
                pltpu.SemaphoreType.DMA((2, size)),
            ],
        ),
        out_shape=(pltpu.HBM if last else jax.ShapeDtypeStruct)((rows, width), BF16),
        compiler_params=compiler_params(24 if last else 32),
        cost_estimate=cost(
            2 * rows * width * head_cols * size,
            (6 if last else 2) * rows * width + 2 * head_cols * width * size,
        ),
        name="projection_end" if last else "projection_start",
    )(parity, *(finish if last else ()), *flat, *weights)


def send(block, move, queue_size, tensor_size, frames=None):
    pairs = []
    for q in range(queue_size) if frames is None else frames:
        for t in range(tensor_size):
            to_q, to_t = move(q, t)
            pairs.append((q * tensor_size + t, to_q * tensor_size + to_t))
    return lax.ppermute(block, AXES, pairs)


def one_hop(block, queue_size, tensor_size, frames=None):
    half = tensor_size // 2
    args = (queue_size, tensor_size, frames)
    near = send(block, lambda q, t: (q, t ^ 1), *args)
    return [near] + [send(block, away(j, half), *args) for j in range(1, half)]


def two_hops(blocks, queue_size, tensor_size, frames=None):
    half = tensor_size // 2
    args = (queue_size, tensor_size, frames)
    near, far = blocks[0], blocks[1:]
    rows = near.shape[0] // 2
    corners = []
    for j in range(1, half):
        top = send(near[:rows], away(j, half), *args)
        bottom = send(far[j - 1][rows:], lambda q, t: (q, t ^ 1), *args)
        corners.append([top, bottom])
    return corners


def away(j, half):
    return lambda q, t: (q, (t // 2 - j) % half * 2 + t % 2)


def body(
    latents, levels, mod_table, step_size, qkv_weight, q_gain, k_gain, out_weight, fresh_noise
):
    queue_size = lax.axis_size("queue")
    tensor_size = lax.axis_size("tensor")
    rows, width = latents.shape[1:]
    mesh_sizes = (queue_size, tensor_size)
    queue_index = lax.axis_index("queue")
    tensor_index = lax.axis_index("tensor")
    is_last = queue_index == queue_size - 1
    parity = (queue_index % 2).astype(jnp.int32)[None]

    def ring(block, frames=None):
        return send(block, lambda q, t: ((q + 1) % queue_size, t), *mesh_sizes, frames)

    def sibling(block):
        return send(block, lambda q, t: (q ^ 1, t), *mesh_sizes)

    worked_level = send(levels, lambda q, t: ((q - 1) % queue_size, t), *mesh_sizes)[0]

    def gather_noise(noise, at_once):
        args = (*mesh_sizes, [queue_size - 1])
        half = tensor_size // 2
        near = send(noise, lambda q, t: (q, t ^ 1), *args)
        pairs = []
        if at_once:
            for j in range(1, half):
                straight = send(noise, away(j, half), *args)
                across = send(
                    noise,
                    lambda q, t: away(j, half)(queue_size - 1, t ^ 1),
                    *mesh_sizes,
                    [max(queue_size - 3, 0)],
                )
                pairs.append(jnp.concatenate([straight, across], axis=0))
        else:
            pair = jnp.concatenate([noise, near], axis=0)
            pairs = [send(pair, away(j, half), *args) for j in range(1, half)]
        return [near, *pairs]

    noise = fresh_noise[0]
    noise_pieces = gather_noise(noise, True)
    half_weight = lax.dynamic_slice(
        out_weight, (0, parity[0] * (width // 2)), (out_weight.shape[0], width // 2)
    )
    half_weight, latents, noise_pieces = lax.optimization_barrier(
        (half_weight, latents, noise_pieces)
    )
    mine = one_hop(half_weight, *mesh_sizes)

    def modulation(level):
        row = lax.dynamic_slice(mod_table, (level, 0), (1, 3 * width)).astype(F32)
        rate = lax.dynamic_slice(step_size, (level,), (1,))[:, None]
        return row[:, :width], 1.0 + row[:, width : 2 * width], rate * row[:, 2 * width :]

    shift, scale1, _ = modulation(worked_level)
    _, _, gate = modulation(levels[0])
    info = jnp.stack([is_last, tensor_index // 2, tensor_index % 2])
    info = info.astype(jnp.int32)
    gains = jnp.stack([q_gain * SCORE_SCALE, k_gain])

    frame = latents[0]
    for step_index in range(STEPS):
        final = step_index == STEPS - 1
        key, value, normed, state = project_keys_values(
            info, scale1, shift, gains, qkv_weight, frame, noise, noise_pieces
        )
        to_next = [q for q in range(queue_size) if q != queue_size - 2]
        earlier = [ring(block, to_next) for block in (key, value)]
        query, *own = own_attention(gains, normed, qkv_weight, key, value)
        if not final:
            query, mine = lax.optimization_barrier((query, mine))
            theirs = [sibling(block) for block in mine]
        attended = earlier_attention(
            info, query, *own, *earlier, CHUNKS if final else 1
        )
        if not final:
            mine_corners = [
                jnp.concatenate(parts, axis=0) for parts in two_hops(mine, *mesh_sizes)
            ]
        senders = range(queue_size) if final else to_next
        targets = range(queue_size if final else queue_size - 1)
        attended = [ring(block, senders) for block in attended]
        sent_state, attended = lax.optimization_barrier((state, attended))
        resid = ring(sent_state, senders)
        if not final:
            attended, mine_corners, theirs = lax.optimization_barrier(
                (attended, mine_corners, theirs)
            )
            theirs_corners = [sibling(block) for block in mine_corners]
        near = [one_hop(block, *mesh_sizes, targets) for block in attended]
        if not final:
            near, theirs_corners, noise = lax.optimization_barrier(
                (near, theirs_corners, fresh_noise[step_index + 1])
            )
            noise_pieces = gather_noise(noise, False)
        beyond = [two_hops(blocks, *mesh_sizes, targets) for blocks in near]
        direct = [attended] + [list(parts) for parts in zip(*near)]
        corners = [[half for parts in p for half in parts] for p in zip(*beyond)]
        begun = output_projection(parity, direct, [out_weight], mine, theirs)
        frame = output_projection(
            parity, corners, [], mine_corners, theirs_corners, (begun, resid, gate)
        )
    return frame[None]


def solution(mesh):
    return jax.shard_map(
        body,
        mesh=mesh,
        in_specs=(
            P("queue", None, None),
            P("queue"),
            P(),
            P(),
            P(None, None, "tensor"),
            P(),
            P(),
            P("tensor", None),
            P(None, "tensor", None),
        ),
        out_specs=P("queue", None, None),
        check_vma=False,
    )
```

```python
import functools
import math

import jax
import jax.numpy as jnp
from jax import lax
from jax.experimental import pallas as pl
from jax.experimental.pallas import tpu as pltpu
from jax.sharding import PartitionSpec as P

HD = 128
STEPS = 2
CHUNKS = 2
EPS = 1e-6
AXES = ("queue", "tensor")
F32 = jnp.float32
BF16 = jnp.bfloat16
SCORE_SCALE = math.log2(math.e) / math.sqrt(HD)
ANY = pl.BlockSpec(memory_space=pl.ANY)


def compiler_params(mib):
    return pltpu.CompilerParams(vmem_limit_bytes=mib * 2**20)


def in_hbm(array):
    return pltpu.with_memory_space_constraint(array, pltpu.HBM)


def cost(flops, nbytes, transcendentals=0, share=1000):
    return pl.CostEstimate(
        flops=int(flops) // share,
        bytes_accessed=int(nbytes) // share,
        transcendentals=int(transcendentals) // share,
    )


def head_normalized(values, gain):
    heads = []
    for h in range(values.shape[1] // HD):
        head = values[:, h * HD : (h + 1) * HD]
        mean = jnp.mean(head * head, axis=-1, keepdims=True)
        heads.append((head * lax.rsqrt(mean + EPS) * gain).astype(BF16))
    return heads[0] if len(heads) == 1 else jnp.concatenate(heads, axis=1)


def over_lanes(values, fold, reduce):
    parts = [values[:, i : i + HD] for i in range(0, values.shape[1], HD)]
    return reduce(functools.reduce(fold, parts), axis=-1, keepdims=True)


def tile_cols(head_cols):
    return 256 if head_cols % 256 == 0 else HD


def weight_copies(w_any, part, w_ref, w_sems):
    splits = w_sems.shape[0]
    split_rows = w_ref.shape[0] // splits
    for i in range(splits):
        at = pl.ds(i * split_rows, split_rows)
        yield pltpu.make_async_copy(w_any.at[part, at], w_ref.at[at], w_sems.at[i])


def key_value_kernel(*refs, half):
    info_ref, scale_ref, shift_ref, gain_ref, w_any, z_any, noise_any, near_any = refs[:8]
    pair_refs = refs[8 : 7 + half]
    key_ref, value_ref, normed_any, state_any = refs[7 + half : 11 + half]
    state_ref, normed_ref, inverse_ref, w_ref, sem, out_sems, w_sems = refs[11 + half :]
    step = pl.program_id(0)
    rows, width = state_ref.shape
    piece_rows = noise_any.shape[0]

    def weights_of(part):
        return weight_copies(w_any, part + 1, w_ref.at[part], w_sems.at[part])

    def start_weights():
        for part in range(2):
            for weight_copy in weights_of(part):
                weight_copy.start()

    def piece_at(j, f):
        if j > 0:
            return pair_refs[j - 1], f * piece_rows
        return (noise_any, near_any)[f], 0

    cols = key_ref.shape[1]
    blocks = pl.num_programs(0) // 2
    state_copy = pltpu.make_async_copy(state_ref, state_any, out_sems.at[0])
    normed_copy = pltpu.make_async_copy(normed_ref, normed_any, out_sems.at[1])

    @pl.when(step == 0)
    def _():
        @pl.when(info_ref[0] == 0)
        def _():
            copy = pltpu.make_async_copy(z_any, state_ref, sem.at[0])
            copy.start()
            copy.wait()
            start_weights()

        @pl.when(info_ref[0] != 0)
        def _():
            start_weights()
            for block in range(2 * half):
                high, low = block // 2, block % 2
                steps = lax.rem(high + half - info_ref[1], half)
                other = jnp.abs(low - info_ref[2])
                for j in range(half):
                    for f in range(2):
                        source, row = piece_at(j, f)

                        @pl.when(jnp.logical_and(steps == j, other == f))
                        def _():
                            copy = pltpu.make_async_copy(
                                source.at[pl.ds(row, piece_rows)],
                                state_ref.at[pl.ds(block * piece_rows, piece_rows)],
                                sem.at[0],
                            )
                            copy.start()
                            copy.wait()

        state_copy.start()

        block_rows = math.gcd(rows, 64)

        def measure(i, carry):
            at = pl.ds(pl.multiple_of(i * block_rows, block_rows), block_rows)
            squares = None
            for k in range(0, width, HD):
                part = state_ref[at, k : k + HD].astype(F32)
                squares = part * part if squares is None else squares + part * part
            mean = jnp.sum(squares, axis=-1, keepdims=True) * (1.0 / width)
            inverse_ref[at, :] = jnp.broadcast_to(lax.rsqrt(mean + EPS), (block_rows, HD))
            return carry

        def apply(k, carry):
            at = pl.ds(pl.multiple_of(k * HD, HD), HD)
            state = state_ref[:, at].astype(F32) * inverse_ref[...]
            normed_ref[:, at] = (state * scale_ref[:, at] + shift_ref[:, at]).astype(BF16)
            return carry

        lax.fori_loop(0, rows // block_rows, measure, 0)
        lax.fori_loop(0, width // HD, apply, 0)
        normed_copy.start()

    for part in range(2):

        @pl.when(step == part * blocks)
        def _():
            for copy in weights_of(part):
                copy.wait()

    at = pl.ds(pl.multiple_of(lax.rem(step, blocks) * cols, HD), cols)

    @pl.when(step < blocks)
    def _():
        product = jnp.dot(normed_ref[...], w_ref[0, :, at], preferred_element_type=F32)
        key_ref[...] = head_normalized(product, gain_ref[1:2])

    @pl.when(step >= blocks)
    def _():
        product = jnp.dot(normed_ref[...], w_ref[1, :, at], preferred_element_type=F32)
        value_ref[...] = product.astype(BF16)

    @pl.when(step == pl.num_programs(0) - 1)
    def _():
        state_copy.wait()
        normed_copy.wait()


def project_keys_values(info, scale1, shift, gains, qkv_weight, z, noise, noise_pieces):
    rows, width = z.shape
    head_cols = qkv_weight.shape[2]
    cols = tile_cols(head_cols)
    half = len(noise_pieces)
    blocks = head_cols // cols
    return pl.pallas_call(
        functools.partial(key_value_kernel, half=half),
        grid_spec=pltpu.PrefetchScalarGridSpec(
            num_scalar_prefetch=1,
            grid=(2 * blocks,),
            in_specs=[
                pl.BlockSpec((1, width), lambda j, i: (0, 0)),
                pl.BlockSpec((1, width), lambda j, i: (0, 0)),
                pl.BlockSpec((2, HD), lambda j, i: (0, 0)),
            ]
            + [ANY] * (3 + half),
            out_specs=[
                pl.BlockSpec((rows, cols), lambda j, i: (0, jnp.minimum(j, blocks - 1))),
                pl.BlockSpec((rows, cols), lambda j, i: (0, jnp.maximum(j - blocks, 0))),
                ANY,
                ANY,
            ],
            scratch_shapes=[
                pltpu.VMEM((rows, width), BF16),
                pltpu.VMEM((rows, width), BF16),
                pltpu.VMEM((rows, HD), F32),
                pltpu.VMEM((2, width, head_cols), BF16),
                pltpu.SemaphoreType.DMA((1,)),
                pltpu.SemaphoreType.DMA((2,)),
                pltpu.SemaphoreType.DMA((2, 4)),
            ],
        ),
        out_shape=[
            jax.ShapeDtypeStruct((rows, head_cols), BF16),
            jax.ShapeDtypeStruct((rows, head_cols), BF16),
            jax.ShapeDtypeStruct((rows, width), BF16),
            pltpu.HBM((rows, width), BF16),
        ],
        compiler_params=compiler_params(32),
        cost_estimate=cost(
            4 * rows * width * head_cols,
            6 * rows * width + 4 * rows * head_cols + 4 * width * head_cols,
        ),
        name="norm_keys_values",
    )(
        info,
        scale1,
        shift,
        gains,
        *[in_hbm(a) for a in (qkv_weight, z)],
        noise,
        *noise_pieces,
    )


def attend(query, key):
    return lax.dot_general(query, key, (((1,), (1,)), ((), ())), preferred_element_type=F32)


def weigh(scores, top, values):
    weights = jnp.exp2(scores - top).astype(BF16)
    extended = jnp.concatenate([values, jnp.ones_like(values)], axis=1)
    total = jnp.dot(weights, extended, preferred_element_type=F32)
    return total[:, :HD], total[:, HD:]


def attention_tiles(query, key, finish):
    rows, cols = query.shape
    tile = math.gcd(rows, 256)
    waiting = None
    for h in range(cols // HD):
        at = slice(h * HD, (h + 1) * HD)
        for r in range(rows // tile):
            row = slice(r * tile, (r + 1) * tile)
            scores = attend(query[row, at], key[:, at])
            if waiting is not None:
                finish(*waiting)
            waiting = (scores, row, at)
    finish(*waiting)


def own_kernel(
    gain_ref, normed_ref, key_ref, value_ref, w_any,
    query_ref, acc_ref, top_ref, total_ref, w_ref, w_sems,
):
    step = pl.program_id(0)
    cols = query_ref.shape[1]

    @pl.when(step == 0)
    def _():
        for copy in weight_copies(w_any, 0, w_ref, w_sems):
            copy.start()
        for copy in weight_copies(w_any, 0, w_ref, w_sems):
            copy.wait()

    inside = pl.ds(pl.multiple_of(step * cols, HD), cols)
    product = jnp.dot(normed_ref[...], w_ref[:, inside], preferred_element_type=F32)
    query = head_normalized(product, gain_ref[0:1])
    query_ref[...] = query

    def finish(scores, row, at):
        top = over_lanes(scores, jnp.maximum, jnp.max)
        acc, total = weigh(scores, top, value_ref[:, at])
        acc_ref[row, at] = acc
        total_ref[row, at] = total
        top_ref[row, at] = jnp.broadcast_to(top, acc.shape)

    attention_tiles(query, key_ref, finish)


def own_attention(gains, normed, qkv_weight, key, value):
    rows, width = normed.shape
    head_cols = qkv_weight.shape[2]
    cols = tile_cols(head_cols)
    by_heads = pl.BlockSpec((rows, cols), lambda j: (0, j))
    return pl.pallas_call(
        own_kernel,
        grid=(head_cols // cols,),
        in_specs=[
            pl.BlockSpec((2, HD), lambda j: (0, 0)),
            pl.BlockSpec((rows, width), lambda j: (0, 0)),
            by_heads,
            by_heads,
            ANY,
        ],
        out_specs=[by_heads] * 4,
        scratch_shapes=[
            pltpu.VMEM((width, head_cols), BF16),
            pltpu.SemaphoreType.DMA((4,)),
        ],
        out_shape=[jax.ShapeDtypeStruct((rows, head_cols), BF16)]
        + [jax.ShapeDtypeStruct((rows, head_cols), F32)] * 3,
        compiler_params=compiler_params(32),
        cost_estimate=cost(
            2 * rows * width * head_cols + 8 * rows * rows * head_cols,
            2 * rows * width + 18 * rows * head_cols + 2 * width * head_cols,
            rows * rows * head_cols // HD,
        ),
        name="queries_own_frame",
    )(gains, normed, key, value, in_hbm(qkv_weight))


def earlier_kernel(*refs, chunks):
    info_ref, query_ref, acc_ref, top_ref, total_ref, key_ref, value_ref = refs[:7]
    out_refs = refs[7:]
    rows = query_ref.shape[0] // chunks

    def store(row, at, result):
        for c, out_ref in enumerate(out_refs):
            first, end = max(row.start, c * rows), min(row.stop, (c + 1) * rows)
            if first < end:
                inside = slice(first - c * rows, end - c * rows)
                out_ref[inside, at] = result[first - row.start : end - row.start]

    @pl.when(info_ref[0] != 0)
    def _():
        every = slice(0, query_ref.shape[0])
        store(every, slice(None), (acc_ref[...] / total_ref[...]).astype(BF16))

    @pl.when(info_ref[0] == 0)
    def _():
        def finish(scores, row, at):
            old_top = top_ref[row, at][:, :1]
            top = jnp.maximum(over_lanes(scores, jnp.maximum, jnp.max), old_top)
            acc, total = weigh(scores, top, value_ref[:, at])
            kept = jnp.exp2(old_top - top)
            acc = acc + acc_ref[row, at] * kept
            total = total + total_ref[row, at] * kept
            store(row, at, (acc / total).astype(BF16))

        attention_tiles(query_ref[...], key_ref, finish)


def earlier_attention(info, query, acc, top, total, key, value, chunks):
    rows, head_cols = query.shape
    cols = tile_cols(head_cols)
    return pl.pallas_call(
        functools.partial(earlier_kernel, chunks=chunks),
        grid_spec=pltpu.PrefetchScalarGridSpec(
            num_scalar_prefetch=1,
            grid=(head_cols // cols,),
            in_specs=[pl.BlockSpec((rows, cols), lambda j, i: (0, j))] * 6,
            out_specs=[pl.BlockSpec((rows // chunks, cols), lambda j, i: (0, j))] * chunks,
        ),
        out_shape=[jax.ShapeDtypeStruct((rows // chunks, head_cols), BF16)] * chunks,
        compiler_params=compiler_params(24),
        cost_estimate=cost(
            8 * rows * rows * head_cols,
            22 * rows * head_cols,
            rows * rows * head_cols // HD,
        ),
        name="earlier_frame",
    )(info, query, acc, top, total, key, value)


def output_kernel(*refs, part_counts, whole_weights, half_blocks, last):
    parity_ref = refs[0]
    at = 1
    acc_in = resid_ref = gate_ref = None
    if last:
        acc_in, resid_ref, gate_ref = refs[1:4]
        at = 4
    pieces = []
    for count in part_counts:
        pieces.append(refs[at : at + count])
        at += count
    size = len(part_counts)
    wholes = refs[at : at + whole_weights]
    at += whole_weights
    halves = refs[at : at + 2 * (size - whole_weights)]
    at += 2 * (size - whole_weights)
    out_ref, held_ref, w_ref, held_sems, w_sems = refs[at:]
    step = pl.program_id(0)
    cols = out_ref.shape[1]
    half_width = w_ref.shape[3]

    def weight_copy(half, k):
        if k < whole_weights:
            column = (parity_ref[0] ^ half) * half_width
            source = wholes[k].at[:, pl.ds(pl.multiple_of(column, HD), half_width)]
        else:
            source = halves[half * (size - whole_weights) + k - whole_weights]
        return pltpu.make_async_copy(source, w_ref.at[half, k], w_sems.at[half, k])

    def held_copies(k):
        row = 0
        for number, part in enumerate(pieces[k]):
            count = part.shape[0]
            yield pltpu.make_async_copy(
                part, held_ref.at[k, pl.ds(row, count)], held_sems.at[k, number]
            )
            row += count

    @pl.when(step == 0)
    def _():
        for k in range(size):
            for copy in held_copies(k):
                copy.start()
        for half in range(2):
            for k in range(size):
                weight_copy(half, k).start()
        for k in range(size):
            for copy in held_copies(k):
                copy.wait()

    for half in range(2):

        @pl.when(step == half * half_blocks)
        def _():
            for k in range(size):
                weight_copy(half, k).wait()

    half = step // half_blocks
    tile = tile_cols(cols)
    for t in range(cols // tile):
        at = slice(t * tile, (t + 1) * tile)
        first = lax.rem(step, half_blocks) * cols + t * tile
        inside = pl.ds(pl.multiple_of(first, HD), tile)
        update = acc_in[:, at].astype(F32) if last else None
        for k in range(size):
            term = jnp.dot(held_ref[k], w_ref[half, k, :, inside], preferred_element_type=F32)
            update = term if update is None else update + term
        if last:
            update = resid_ref[:, at].astype(F32) + gate_ref[:, at] * update
        out_ref[:, at] = update.astype(BF16)


def output_projection(parity, pieces, wholes, mine, theirs, finish=None):
    head_cols, half_width = mine[0].shape
    rows = sum(part.shape[0] for part in pieces[0])
    width = 2 * half_width
    size = len(pieces)
    cols = half_width // 2 if half_width % 512 == 0 else half_width
    half_blocks = half_width // cols
    parts = max(len(p) for p in pieces)
    flat = [part for group in pieces for part in group]
    weights = [in_hbm(array) for array in [*wholes, *mine, *theirs]]
    last = finish is not None

    def column(j, parity):
        return 0, ((j // half_blocks) ^ parity[0]) * half_blocks + j % half_blocks

    block = pl.BlockSpec((rows, cols), column)
    return pl.pallas_call(
        functools.partial(
            output_kernel,
            part_counts=tuple(len(p) for p in pieces),
            whole_weights=len(wholes),
            half_blocks=half_blocks,
            last=last,
        ),
        grid_spec=pltpu.PrefetchScalarGridSpec(
            num_scalar_prefetch=1,
            grid=(2 * half_blocks,),
            in_specs=([block, block, pl.BlockSpec((1, cols), column)] if last else [])
            + [ANY] * (len(flat) + len(weights)),
            out_specs=block,
            scratch_shapes=[
                pltpu.VMEM((size, rows, head_cols), BF16),
                pltpu.VMEM((2, size, head_cols, half_width), BF16),
                pltpu.SemaphoreType.DMA((size, parts)),
                pltpu.SemaphoreType.DMA((2, size)),
            ],
        ),
        out_shape=(pltpu.HBM if last else jax.ShapeDtypeStruct)((rows, width), BF16),
        compiler_params=compiler_params(24 if last else 32),
        cost_estimate=cost(
            2 * rows * width * head_cols * size,
            (6 if last else 2) * rows * width + 2 * head_cols * width * size,
        ),
        name="projection_end" if last else "projection_start",
    )(parity, *(finish if last else ()), *flat, *weights)


def send(block, move, queue_size, tensor_size, frames=None):
    pairs = []
    for q in range(queue_size) if frames is None else frames:
        for t in range(tensor_size):
            to_q, to_t = move(q, t)
            pairs.append((q * tensor_size + t, to_q * tensor_size + to_t))
    return lax.ppermute(block, AXES, pairs)


def one_hop(block, queue_size, tensor_size, frames=None):
    half = tensor_size // 2
    args = (queue_size, tensor_size, frames)
    near = send(block, lambda q, t: (q, t ^ 1), *args)
    return [near] + [send(block, away(j, half), *args) for j in range(1, half)]


def two_hops(blocks, queue_size, tensor_size, frames=None):
    half = tensor_size // 2
    args = (queue_size, tensor_size, frames)
    near, far = blocks[0], blocks[1:]
    rows = near.shape[0] // 2
    corners = []
    for j in range(1, half):
        top = send(near[:rows], away(j, half), *args)
        bottom = send(far[j - 1][rows:], lambda q, t: (q, t ^ 1), *args)
        corners.append([top, bottom])
    return corners


def away(j, half):
    return lambda q, t: (q, (t // 2 - j) % half * 2 + t % 2)


def body(
    latents, levels, mod_table, step_size, qkv_weight, q_gain, k_gain, out_weight, fresh_noise
):
    queue_size = lax.axis_size("queue")
    tensor_size = lax.axis_size("tensor")
    rows, width = latents.shape[1:]
    mesh_sizes = (queue_size, tensor_size)
    queue_index = lax.axis_index("queue")
    tensor_index = lax.axis_index("tensor")
    parity = (queue_index % 2).astype(jnp.int32)[None]

    def ring(block, frames=None):
        return send(block, lambda q, t: ((q + 1) % queue_size, t), *mesh_sizes, frames)

    def sibling(block):
        return send(block, lambda q, t: (q ^ 1, t), *mesh_sizes)

    def gather_noise(noise):
        args = (*mesh_sizes, [0])
        half = tensor_size // 2
        near = send(noise, lambda q, t: (q, t ^ 1), *args)
        pair = jnp.concatenate([noise, near], axis=0)
        return [near, *[send(pair, away(j, half), *args) for j in range(1, half)]]

    to_next = range(queue_size - 1)
    frame = ring(latents[0], to_next)
    noise = fresh_noise[0]
    noise_pieces = gather_noise(noise)
    half_weight = lax.dynamic_slice(
        out_weight, (0, parity[0] * (width // 2)), (out_weight.shape[0], width // 2)
    )
    mine = one_hop(half_weight, *mesh_sizes)

    def modulation(level):
        row = lax.dynamic_slice(mod_table, (level, 0), (1, 3 * width)).astype(F32)
        rate = lax.dynamic_slice(step_size, (level,), (1,))[:, None]
        return row[:, :width], 1.0 + row[:, width : 2 * width], rate * row[:, 2 * width :]

    shift, scale1, own_gate = modulation(levels[0])
    arriving_gate = modulation(ring(levels, to_next)[0])[2]
    info = jnp.stack([queue_index == 0, tensor_index // 2, tensor_index % 2])
    info = info.astype(jnp.int32)
    gains = jnp.stack([q_gain * SCORE_SCALE, k_gain])

    for step_index in range(STEPS):
        final = step_index == STEPS - 1
        key, value, normed, state = project_keys_values(
            info, scale1, shift, gains, qkv_weight, frame, noise, noise_pieces
        )
        if not final:
            value, mine = lax.optimization_barrier((value, mine))
        earlier = [ring(block, to_next) for block in (key, value)]
        query, *own = own_attention(gains, normed, qkv_weight, key, value)
        if not final:
            mine_corners = two_hops(mine, *mesh_sizes)
            earlier, mine_corners = lax.optimization_barrier((earlier, mine_corners))
        attended = earlier_attention(
            info, query, *own, *earlier, CHUNKS if final else 1
        )
        targets = range(queue_size) if final else range(1, queue_size)
        resid, gate = state, own_gate
        if not final:
            attended, mine, mine_corners = lax.optimization_barrier(
                (attended, mine, mine_corners)
            )
            mine_corners = [jnp.concatenate(parts, axis=0) for parts in mine_corners]
            theirs = [sibling(block) for block in mine]
            theirs_corners = [sibling(block) for block in mine_corners]
            attended = [ring(block, to_next) for block in attended]
            sent_state, attended = lax.optimization_barrier((state, attended))
            resid, gate = ring(sent_state, to_next), arriving_gate
            attended, theirs, theirs_corners = lax.optimization_barrier(
                (attended, theirs, theirs_corners)
            )
        near = [one_hop(block, *mesh_sizes, targets) for block in attended]
        if not final:
            near, noise = lax.optimization_barrier((near, fresh_noise[step_index + 1]))
            noise_pieces = gather_noise(noise)
        beyond = [two_hops(blocks, *mesh_sizes, targets) for blocks in near]
        direct = [attended] + [list(parts) for parts in zip(*near)]
        corners = [[half for parts in p for half in parts] for p in zip(*beyond)]
        begun = output_projection(parity, direct, [out_weight], mine, theirs)
        frame = output_projection(
            parity, corners, [], mine_corners, theirs_corners, (begun, resid, gate)
        )
    return frame[None]


def solution(mesh):
    return jax.shard_map(
        body,
        mesh=mesh,
        in_specs=(
            P("queue", None, None),
            P("queue"),
            P(),
            P(),
            P(None, None, "tensor"),
            P(),
            P(),
            P("tensor", None),
            P(None, "tensor", None),
        ),
        out_specs=P("queue", None, None),
        check_vma=False,
    )
```

```python
import functools
import math

import jax
import jax.numpy as jnp
from jax import lax
from jax.experimental import pallas as pl
from jax.experimental.pallas import tpu as pltpu
from jax.sharding import PartitionSpec as P

HD = 128
STEPS = 2
EPS = 1e-6
AXES = ("queue", "tensor")
F32 = jnp.float32
BF16 = jnp.bfloat16
SCORE_SCALE = math.log2(math.e) / math.sqrt(HD)
ANY = pl.BlockSpec(memory_space=pl.ANY)


def compiler_params(mib):
    return pltpu.CompilerParams(vmem_limit_bytes=mib * 2**20)


def in_hbm(array):
    return pltpu.with_memory_space_constraint(array, pltpu.HBM)


def cost(flops, nbytes, transcendentals=0, share=1000):
    return pl.CostEstimate(
        flops=int(flops) // share,
        bytes_accessed=int(nbytes) // share,
        transcendentals=int(transcendentals) // share,
    )


def head_normalized(values, gain):
    heads = []
    for h in range(values.shape[1] // HD):
        head = values[:, h * HD : (h + 1) * HD]
        mean = jnp.mean(head * head, axis=-1, keepdims=True)
        heads.append((head * lax.rsqrt(mean + EPS) * gain).astype(BF16))
    return heads[0] if len(heads) == 1 else jnp.concatenate(heads, axis=1)


def over_lanes(values, fold, reduce):
    parts = [values[:, i : i + HD] for i in range(0, values.shape[1], HD)]
    return reduce(functools.reduce(fold, parts), axis=-1, keepdims=True)


def tile_cols(head_cols):
    return 256 if head_cols % 256 == 0 else HD


def weight_copies(w_any, part, w_ref, w_sems):
    splits = w_sems.shape[0]
    split_rows = w_ref.shape[0] // splits
    for i in range(splits):
        at = pl.ds(i * split_rows, split_rows)
        yield pltpu.make_async_copy(w_any.at[part, at], w_ref.at[at], w_sems.at[i])


def key_value_kernel(*refs, half):
    info_ref, scale_ref, shift_ref, gain_ref, w_any, z_any, noise_any, near_any = refs[:8]
    pair_refs = refs[8 : 7 + half]
    first_ref, second_ref, normed_any, state_any = refs[7 + half : 11 + half]
    state_ref, normed_ref, inverse_ref, w_ref, sem, out_sems, w_sems = refs[11 + half :]
    step = pl.program_id(0)
    rows, width = state_ref.shape
    piece_rows = noise_any.shape[0]

    def weights_of(part):
        return weight_copies(w_any, part + 1, w_ref.at[part], w_sems.at[part])

    def start_weights():
        for part in range(2):
            for weight_copy in weights_of(part):
                weight_copy.start()

    def piece_at(j, f):
        if j > 0:
            return pair_refs[j - 1], f * piece_rows
        return (noise_any, near_any)[f], 0

    cols = first_ref.shape[2]
    blocks = pl.num_programs(0) // 2
    state_copy = pltpu.make_async_copy(state_ref, state_any, out_sems.at[0])
    normed_copy = pltpu.make_async_copy(normed_ref, normed_any, out_sems.at[1])

    @pl.when(step == 0)
    def _():
        @pl.when(info_ref[0] == 0)
        def _():
            copy = pltpu.make_async_copy(z_any, state_ref, sem.at[0])
            copy.start()
            copy.wait()
            start_weights()

        @pl.when(info_ref[0] != 0)
        def _():
            start_weights()
            for block in range(2 * half):
                high, low = block // 2, block % 2
                steps = lax.rem(high + half - info_ref[1], half)
                other = jnp.abs(low - info_ref[2])
                for j in range(half):
                    for f in range(2):
                        source, row = piece_at(j, f)

                        @pl.when(jnp.logical_and(steps == j, other == f))
                        def _():
                            copy = pltpu.make_async_copy(
                                source.at[pl.ds(row, piece_rows)],
                                state_ref.at[pl.ds(block * piece_rows, piece_rows)],
                                sem.at[0],
                            )
                            copy.start()
                            copy.wait()

        state_copy.start()

        block_rows = math.gcd(rows, 64)

        def measure(i, carry):
            at = pl.ds(pl.multiple_of(i * block_rows, block_rows), block_rows)
            squares = None
            for k in range(0, width, HD):
                part = state_ref[at, k : k + HD].astype(F32)
                squares = part * part if squares is None else squares + part * part
            mean = jnp.sum(squares, axis=-1, keepdims=True) * (1.0 / width)
            inverse_ref[at, :] = jnp.broadcast_to(lax.rsqrt(mean + EPS), (block_rows, HD))
            return carry

        def apply(k, carry):
            at = pl.ds(pl.multiple_of(k * HD, HD), HD)
            state = state_ref[:, at].astype(F32) * inverse_ref[...]
            normed_ref[:, at] = (state * scale_ref[:, at] + shift_ref[:, at]).astype(BF16)
            return carry

        lax.fori_loop(0, rows // block_rows, measure, 0)
        lax.fori_loop(0, width // HD, apply, 0)
        normed_copy.start()

    for part in range(2):

        @pl.when(step == part)
        def _():
            for copy in weights_of(part):
                copy.wait()

    block = jnp.where(step < 2, 0, lax.rem(step - 2 + blocks - 1, blocks - 1) + 1)
    at = pl.ds(pl.multiple_of(block * cols, HD), cols)

    def keys():
        product = jnp.dot(normed_ref[...], w_ref[0, :, at], preferred_element_type=F32)
        return head_normalized(product, gain_ref[1:2])

    def values():
        product = jnp.dot(normed_ref[...], w_ref[1, :, at], preferred_element_type=F32)
        return product.astype(BF16)

    @pl.when(step == 0)
    def _():
        first_ref[0] = keys()

    @pl.when(step == 1)
    def _():
        first_ref[0] = values()

    @pl.when(jnp.logical_and(step > 1, step < 1 + blocks))
    def _():
        second_ref[0] = keys()

    @pl.when(step >= 1 + blocks)
    def _():
        second_ref[0] = values()

    @pl.when(step == pl.num_programs(0) - 1)
    def _():
        state_copy.wait()
        normed_copy.wait()


def project_keys_values(info, scale1, shift, gains, qkv_weight, z, noise, noise_pieces):
    rows, width = z.shape
    head_cols = qkv_weight.shape[2]
    cols = tile_cols(head_cols)
    half = len(noise_pieces)
    blocks = head_cols // cols

    def second_block(j, i):
        j = jnp.maximum(j - 2, 0)
        return j // (blocks - 1), 0, j % (blocks - 1)

    return pl.pallas_call(
        functools.partial(key_value_kernel, half=half),
        grid_spec=pltpu.PrefetchScalarGridSpec(
            num_scalar_prefetch=1,
            grid=(2 * blocks,),
            in_specs=[
                pl.BlockSpec((1, width), lambda j, i: (0, 0)),
                pl.BlockSpec((1, width), lambda j, i: (0, 0)),
                pl.BlockSpec((2, HD), lambda j, i: (0, 0)),
            ]
            + [ANY] * (3 + half),
            out_specs=[
                pl.BlockSpec((1, rows, cols), lambda j, i: (jnp.minimum(j, 1), 0, 0)),
                pl.BlockSpec((1, rows, cols), second_block),
                ANY,
                ANY,
            ],
            scratch_shapes=[
                pltpu.VMEM((rows, width), BF16),
                pltpu.VMEM((rows, width), BF16),
                pltpu.VMEM((rows, HD), F32),
                pltpu.VMEM((2, width, head_cols), BF16),
                pltpu.SemaphoreType.DMA((1,)),
                pltpu.SemaphoreType.DMA((2,)),
                pltpu.SemaphoreType.DMA((2, 4)),
            ],
        ),
        out_shape=[
            jax.ShapeDtypeStruct((2, rows, cols), BF16),
            jax.ShapeDtypeStruct((2, rows, head_cols - cols), BF16),
            jax.ShapeDtypeStruct((rows, width), BF16),
            pltpu.HBM((rows, width), BF16),
        ],
        compiler_params=compiler_params(32),
        cost_estimate=cost(
            4 * rows * width * head_cols,
            6 * rows * width + 4 * rows * head_cols + 4 * width * head_cols,
        ),
        name="norm_keys_values",
    )(
        info,
        scale1,
        shift,
        gains,
        *[in_hbm(a) for a in (qkv_weight, z)],
        noise,
        *noise_pieces,
    )


def attend(query, key):
    return lax.dot_general(query, key, (((1,), (1,)), ((), ())), preferred_element_type=F32)


def weigh(scores, top, values):
    weights = jnp.exp2(scores - top).astype(BF16)
    extended = jnp.concatenate([values, jnp.ones_like(values)], axis=1)
    total = jnp.dot(weights, extended, preferred_element_type=F32)
    return total[:, :HD], total[:, HD:]


def attention_tiles(query, key, finish):
    rows, cols = query.shape
    tile = math.gcd(rows, 256)
    waiting = None
    for h in range(cols // HD):
        at = slice(h * HD, (h + 1) * HD)
        for r in range(rows // tile):
            row = slice(r * tile, (r + 1) * tile)
            scores = attend(query[row, at], key[:, at])
            if waiting is not None:
                finish(*waiting)
            waiting = (scores, row, at)
    finish(*waiting)


def own_kernel(
    gain_ref, normed_ref, first_ref, second_ref, w_any,
    query_ref, acc_ref, top_ref, total_ref, w_ref, w_sems,
):
    step = pl.program_id(0)
    cols = query_ref.shape[1]

    @pl.when(step == 0)
    def _():
        for copy in weight_copies(w_any, 0, w_ref, w_sems):
            copy.start()
        for copy in weight_copies(w_any, 0, w_ref, w_sems):
            copy.wait()

    inside = pl.ds(pl.multiple_of(step * cols, HD), cols)
    product = jnp.dot(normed_ref[...], w_ref[:, inside], preferred_element_type=F32)
    query = head_normalized(product, gain_ref[0:1])
    query_ref[...] = query
    keys = jnp.where(step == 0, first_ref[0], second_ref[0])
    values = jnp.where(step == 0, first_ref[1], second_ref[1])

    def finish(scores, row, at):
        top = over_lanes(scores, jnp.maximum, jnp.max)
        acc, total = weigh(scores, top, values[:, at])
        acc_ref[row, at] = acc
        total_ref[row, at] = total
        top_ref[row, at] = jnp.broadcast_to(top, acc.shape)

    attention_tiles(query, keys, finish)


def own_attention(gains, normed, qkv_weight, first, second):
    rows, width = normed.shape
    head_cols = qkv_weight.shape[2]
    cols = tile_cols(head_cols)
    by_heads = pl.BlockSpec((rows, cols), lambda j: (0, j))
    return pl.pallas_call(
        own_kernel,
        grid=(head_cols // cols,),
        in_specs=[
            pl.BlockSpec((2, HD), lambda j: (0, 0)),
            pl.BlockSpec((rows, width), lambda j: (0, 0)),
            pl.BlockSpec((2, rows, cols), lambda j: (0, 0, 0)),
            pl.BlockSpec((2, rows, cols), lambda j: (0, 0, jnp.maximum(j - 1, 0))),
            ANY,
        ],
        out_specs=[by_heads] * 4,
        scratch_shapes=[
            pltpu.VMEM((width, head_cols), BF16),
            pltpu.SemaphoreType.DMA((4,)),
        ],
        out_shape=[jax.ShapeDtypeStruct((rows, head_cols), BF16)]
        + [jax.ShapeDtypeStruct((rows, head_cols), F32)] * 3,
        compiler_params=compiler_params(32),
        cost_estimate=cost(
            2 * rows * width * head_cols + 8 * rows * rows * head_cols,
            2 * rows * width + 18 * rows * head_cols + 2 * width * head_cols,
            rows * rows * head_cols // HD,
        ),
        name="queries_own_frame",
    )(gains, normed, first, second, in_hbm(qkv_weight))


def earlier_kernel(info_ref, query_ref, acc_ref, top_ref, total_ref, kv_ref, out_ref):
    @pl.when(info_ref[0] != 0)
    def _():
        out_ref[...] = (acc_ref[...] / total_ref[...]).astype(BF16)

    @pl.when(info_ref[0] == 0)
    def _():
        def finish(scores, row, at):
            old_top = top_ref[row, at][:, :1]
            top = jnp.maximum(over_lanes(scores, jnp.maximum, jnp.max), old_top)
            acc, total = weigh(scores, top, kv_ref[1, :, at])
            kept = jnp.exp2(old_top - top)
            acc = acc + acc_ref[row, at] * kept
            total = total + total_ref[row, at] * kept
            out_ref[row, at] = (acc / total).astype(BF16)

        attention_tiles(query_ref[...], kv_ref[0], finish)


def earlier_attention(info, query, acc, top, total, kv, first_block):
    rows = query.shape[0]
    group = kv.shape[2]
    cols = tile_cols(query.shape[1])
    by_heads = pl.BlockSpec((rows, cols), lambda j, i: (0, first_block + j))
    return pl.pallas_call(
        earlier_kernel,
        grid_spec=pltpu.PrefetchScalarGridSpec(
            num_scalar_prefetch=1,
            grid=(group // cols,),
            in_specs=[by_heads] * 4 + [pl.BlockSpec((2, rows, cols), lambda j, i: (0, 0, j))],
            out_specs=pl.BlockSpec((rows, cols), lambda j, i: (0, j)),
        ),
        out_shape=jax.ShapeDtypeStruct((rows, group), BF16),
        compiler_params=compiler_params(24),
        cost_estimate=cost(8 * rows * rows * group, 20 * rows * group, rows * rows * group // HD),
        name="earlier_frame",
    )(info, query, acc, top, total, kv)


def output_kernel(*refs, part_places, whole_weights, half_blocks, last):
    parity_ref = refs[0]
    at = 1
    acc_in = resid_ref = gate_ref = None
    if last:
        acc_in, resid_ref, gate_ref = refs[1:4]
        at = 4
    pieces = []
    for places in part_places:
        pieces.append(refs[at : at + len(places)])
        at += len(places)
    size = len(part_places)
    wholes = refs[at : at + whole_weights]
    at += whole_weights
    halves = refs[at : at + 2 * (size - whole_weights)]
    at += 2 * (size - whole_weights)
    out_ref, held_ref, w_ref, held_sems, w_sems = refs[at:]
    step = pl.program_id(0)
    cols = out_ref.shape[1]
    half_width = w_ref.shape[3]

    def weight_copy(half, k):
        if k < whole_weights:
            column = (parity_ref[0] ^ half) * half_width
            source = wholes[k].at[:, pl.ds(pl.multiple_of(column, HD), half_width)]
        else:
            source = halves[half * (size - whole_weights) + k - whole_weights]
        return pltpu.make_async_copy(source, w_ref.at[half, k], w_sems.at[half, k])

    def held_copies(k):
        for number, (part, place) in enumerate(zip(pieces[k], part_places[k])):
            rows, cols = (pl.ds(first, count) for first, count in zip(place, part.shape))
            yield pltpu.make_async_copy(
                part, held_ref.at[k, rows, cols], held_sems.at[k, number]
            )

    @pl.when(step == 0)
    def _():
        for k in range(size):
            for copy in held_copies(k):
                copy.start()
        for half in range(2):
            for k in range(size):
                weight_copy(half, k).start()
        for k in range(size):
            for copy in held_copies(k):
                copy.wait()

    for half in range(2):

        @pl.when(step == half * half_blocks)
        def _():
            for k in range(size):
                weight_copy(half, k).wait()

    half = step // half_blocks
    tile = tile_cols(cols)
    for t in range(cols // tile):
        at = slice(t * tile, (t + 1) * tile)
        first = lax.rem(step, half_blocks) * cols + t * tile
        inside = pl.ds(pl.multiple_of(first, HD), tile)
        update = acc_in[:, at].astype(F32) if last else None
        for k in range(size):
            term = jnp.dot(held_ref[k], w_ref[half, k, :, inside], preferred_element_type=F32)
            update = term if update is None else update + term
        if last:
            update = resid_ref[:, at].astype(F32) + gate_ref[:, at] * update
        out_ref[:, at] = update.astype(BF16)


def output_projection(parity, pieces, wholes, mine, theirs, finish=None):
    head_cols, half_width = mine[0].shape
    width = 2 * half_width
    rows = max(row + part.shape[0] for part, row, _ in pieces[0])
    size = len(pieces)
    cols = half_width // 2 if half_width % 512 == 0 else half_width
    half_blocks = half_width // cols
    parts = max(len(p) for p in pieces)
    flat = [part for group in pieces for part, _, _ in group]
    weights = [in_hbm(array) for array in [*wholes, *mine, *theirs]]
    last = finish is not None

    def column(j, parity):
        return 0, ((j // half_blocks) ^ parity[0]) * half_blocks + j % half_blocks

    block = pl.BlockSpec((rows, cols), column)
    return pl.pallas_call(
        functools.partial(
            output_kernel,
            part_places=tuple(tuple((row, col) for _, row, col in p) for p in pieces),
            whole_weights=len(wholes),
            half_blocks=half_blocks,
            last=last,
        ),
        grid_spec=pltpu.PrefetchScalarGridSpec(
            num_scalar_prefetch=1,
            grid=(2 * half_blocks,),
            in_specs=([block, block, pl.BlockSpec((1, cols), column)] if last else [])
            + [ANY] * (len(flat) + len(weights)),
            out_specs=block,
            scratch_shapes=[
                pltpu.VMEM((size, rows, head_cols), BF16),
                pltpu.VMEM((2, size, head_cols, half_width), BF16),
                pltpu.SemaphoreType.DMA((size, parts)),
                pltpu.SemaphoreType.DMA((2, size)),
            ],
        ),
        out_shape=(pltpu.HBM if last else jax.ShapeDtypeStruct)((rows, width), BF16),
        compiler_params=compiler_params(24 if last else 32),
        cost_estimate=cost(
            2 * rows * width * head_cols * size,
            (6 if last else 2) * rows * width + 2 * head_cols * width * size,
        ),
        name="projection_end" if last else "projection_start",
    )(parity, *(finish if last else ()), *flat, *weights)


def send(block, move, queue_size, tensor_size, frames=None):
    pairs = []
    for q in range(queue_size) if frames is None else frames:
        for t in range(tensor_size):
            to_q, to_t = move(q, t)
            pairs.append((q * tensor_size + t, to_q * tensor_size + to_t))
    return lax.ppermute(block, AXES, pairs)


def one_hop(block, queue_size, tensor_size, frames=None):
    half = tensor_size // 2
    args = (queue_size, tensor_size, frames)
    near = send(block, lambda q, t: (q, t ^ 1), *args)
    return [near] + [send(block, away(j, half), *args) for j in range(1, half)]


def two_hops(blocks, queue_size, tensor_size, frames=None):
    half = tensor_size // 2
    args = (queue_size, tensor_size, frames)
    near, far = blocks[0], blocks[1:]
    rows = near.shape[0] // 2
    corners = []
    for j in range(1, half):
        top = send(near[:rows], away(j, half), *args)
        bottom = send(far[j - 1][rows:], lambda q, t: (q, t ^ 1), *args)
        corners.append([top, bottom])
    return corners


def away(j, half):
    return lambda q, t: (q, (t // 2 - j) % half * 2 + t % 2)


def body(
    latents, levels, mod_table, step_size, qkv_weight, q_gain, k_gain, out_weight, fresh_noise
):
    queue_size = lax.axis_size("queue")
    tensor_size = lax.axis_size("tensor")
    rows, width = latents.shape[1:]
    mesh_sizes = (queue_size, tensor_size)
    queue_index = lax.axis_index("queue")
    tensor_index = lax.axis_index("tensor")
    parity = (queue_index % 2).astype(jnp.int32)[None]

    def ring(block, frames=None):
        return send(block, lambda q, t: ((q + 1) % queue_size, t), *mesh_sizes, frames)

    def sibling(block):
        return send(block, lambda q, t: (q ^ 1, t), *mesh_sizes)

    def gather_noise(noise):
        args = (*mesh_sizes, [0])
        half = tensor_size // 2
        near = send(noise, lambda q, t: (q, t ^ 1), *args)
        pair = jnp.concatenate([noise, near], axis=0)
        return [near, *[send(pair, away(j, half), *args) for j in range(1, half)]]

    to_next = range(queue_size - 1)
    frame = ring(latents[0], to_next)
    noise = fresh_noise[0]
    noise_pieces = gather_noise(noise)
    half_weight = lax.dynamic_slice(
        out_weight, (0, parity[0] * (width // 2)), (out_weight.shape[0], width // 2)
    )
    mine = one_hop(half_weight, *mesh_sizes)

    def modulation(level):
        row = lax.dynamic_slice(mod_table, (level, 0), (1, 3 * width)).astype(F32)
        rate = lax.dynamic_slice(step_size, (level,), (1,))[:, None]
        return row[:, :width], 1.0 + row[:, width : 2 * width], rate * row[:, 2 * width :]

    shift, scale1, own_gate = modulation(levels[0])
    info = jnp.stack([queue_index == 0, tensor_index // 2, tensor_index % 2])
    info = info.astype(jnp.int32)
    gains = jnp.stack([q_gain * SCORE_SCALE, k_gain])

    for step_index in range(STEPS):
        final = step_index == STEPS - 1
        *made, normed, state = project_keys_values(
            info, scale1, shift, gains, qkv_weight, frame, noise, noise_pieces
        )
        if not final:
            made[1], mine, sent_levels = lax.optimization_barrier((made[1], mine, levels))
            arriving_level = ring(sent_levels, to_next)
        earlier = [ring(group, to_next) for group in made]
        query, *own = own_attention(gains, normed, qkv_weight, *made)
        if not final:
            mine_corners = two_hops(mine, *mesh_sizes)
            earlier, mine_corners = lax.optimization_barrier((earlier, mine_corners))
        attended, columns, block = [], [], 0
        for group in earlier:
            attended.append(earlier_attention(info, query, *own, group, block))
            columns.append(block * made[0].shape[2])
            block += group.shape[2] // made[0].shape[2]
        targets = range(queue_size) if final else range(1, queue_size)
        resid, gate = state, own_gate
        if not final:
            attended, mine, mine_corners, arriving_level = lax.optimization_barrier(
                (attended, mine, mine_corners, arriving_level)
            )
            mine_corners = [jnp.concatenate(parts, axis=0) for parts in mine_corners]
            theirs = [sibling(block) for block in mine]
            theirs_corners = [sibling(block) for block in mine_corners]
            attended = [ring(block, to_next) for block in attended]
            sent_state, attended = lax.optimization_barrier((state, attended))
            resid = ring(sent_state, to_next)
            gate = modulation(arriving_level[0])[2]
            attended, theirs, theirs_corners = lax.optimization_barrier(
                (attended, theirs, theirs_corners)
            )
        near = [one_hop(block, *mesh_sizes, targets) for block in attended]
        if not final:
            near, noise = lax.optimization_barrier((near, fresh_noise[step_index + 1]))
            noise_pieces = gather_noise(noise)
        beyond = [two_hops(blocks, *mesh_sizes, targets) for blocks in near]
        direct = [[(block, 0, col) for block, col in zip(attended, columns)]]
        direct += [[(block, 0, col) for block, col in zip(p, columns)] for p in zip(*near)]
        corners = [
            [(half, h * (rows // 2), col) for parts, col in zip(p, columns)
             for h, half in enumerate(parts)]
            for p in zip(*beyond)
        ]
        begun = output_projection(parity, direct, [out_weight], mine, theirs)
        frame = output_projection(
            parity, corners, [], mine_corners, theirs_corners, (begun, resid, gate)
        )
    return frame[None]


def solution(mesh):
    return jax.shard_map(
        body,
        mesh=mesh,
        in_specs=(
            P("queue", None, None),
            P("queue"),
            P(),
            P(),
            P(None, None, "tensor"),
            P(),
            P(),
            P("tensor", None),
            P(None, "tensor", None),
        ),
        out_specs=P("queue", None, None),
        check_vma=False,
    )
```

```python
import functools
import math

import jax
import jax.numpy as jnp
from jax import lax
from jax.experimental import pallas as pl
from jax.experimental.pallas import tpu as pltpu
from jax.sharding import PartitionSpec as P

HD = 128
STEPS = 2
EPS = 1e-6
AXES = ("queue", "tensor")
F32 = jnp.float32
BF16 = jnp.bfloat16
SCORE_SCALE = math.log2(math.e) / math.sqrt(HD)
ANY = pl.BlockSpec(memory_space=pl.ANY)


def compiler_params(mib):
    return pltpu.CompilerParams(vmem_limit_bytes=mib * 2**20)


def in_hbm(array):
    return pltpu.with_memory_space_constraint(array, pltpu.HBM)


def cost(flops, nbytes, transcendentals=0, share=1000):
    return pl.CostEstimate(
        flops=int(flops) // share,
        bytes_accessed=int(nbytes) // share,
        transcendentals=int(transcendentals) // share,
    )


def head_normalized(values, gain):
    heads = []
    for h in range(values.shape[1] // HD):
        head = values[:, h * HD : (h + 1) * HD]
        mean = jnp.mean(head * head, axis=-1, keepdims=True)
        heads.append((head * lax.rsqrt(mean + EPS) * gain).astype(BF16))
    return heads[0] if len(heads) == 1 else jnp.concatenate(heads, axis=1)


def over_lanes(values, fold, reduce):
    parts = [values[:, i : i + HD] for i in range(0, values.shape[1], HD)]
    return reduce(functools.reduce(fold, parts), axis=-1, keepdims=True)


def tile_cols(head_cols):
    return 256 if head_cols % 256 == 0 else HD


def weight_copies(w_any, part, w_ref, w_sems):
    splits = w_sems.shape[0]
    split_rows = w_ref.shape[0] // splits
    for i in range(splits):
        at = pl.ds(i * split_rows, split_rows)
        yield pltpu.make_async_copy(w_any.at[part, at], w_ref.at[at], w_sems.at[i])


def key_value_kernel(*refs, half):
    info_ref, scale_ref, shift_ref, gain_ref, w_any, z_any, noise_any, near_any = refs[:8]
    pair_refs = refs[8 : 7 + half]
    first_ref, second_ref, normed_any, state_any = refs[7 + half : 11 + half]
    state_ref, normed_ref, inverse_ref, w_ref, sem, out_sems, w_sems = refs[11 + half :]
    step = pl.program_id(0)
    rows, width = state_ref.shape
    piece_rows = noise_any.shape[0]

    def weights_of(part):
        return weight_copies(w_any, part + 1, w_ref.at[part], w_sems.at[part])

    def start_weights():
        for part in range(2):
            for weight_copy in weights_of(part):
                weight_copy.start()

    def piece_at(j, f):
        if j > 0:
            return pair_refs[j - 1], f * piece_rows
        return (noise_any, near_any)[f], 0

    cols = first_ref.shape[2]
    blocks = pl.num_programs(0) // 2
    state_copy = pltpu.make_async_copy(state_ref, state_any, out_sems.at[0])
    normed_copy = pltpu.make_async_copy(normed_ref, normed_any, out_sems.at[1])

    @pl.when(step == 0)
    def _():
        @pl.when(info_ref[0] == 0)
        def _():
            copy = pltpu.make_async_copy(z_any, state_ref, sem.at[0])
            copy.start()
            copy.wait()
            start_weights()

        @pl.when(info_ref[0] != 0)
        def _():
            start_weights()
            for block in range(2 * half):
                high, low = block // 2, block % 2
                steps = lax.rem(high + half - info_ref[1], half)
                other = jnp.abs(low - info_ref[2])
                for j in range(half):
                    for f in range(2):
                        source, row = piece_at(j, f)

                        @pl.when(jnp.logical_and(steps == j, other == f))
                        def _():
                            copy = pltpu.make_async_copy(
                                source.at[pl.ds(row, piece_rows)],
                                state_ref.at[pl.ds(block * piece_rows, piece_rows)],
                                sem.at[0],
                            )
                            copy.start()
                            copy.wait()

        state_copy.start()

        block_rows = math.gcd(rows, 64)

        def measure(i, carry):
            at = pl.ds(pl.multiple_of(i * block_rows, block_rows), block_rows)
            squares = None
            for k in range(0, width, HD):
                part = state_ref[at, k : k + HD].astype(F32)
                squares = part * part if squares is None else squares + part * part
            mean = jnp.sum(squares, axis=-1, keepdims=True) * (1.0 / width)
            inverse_ref[at, :] = jnp.broadcast_to(lax.rsqrt(mean + EPS), (block_rows, HD))
            return carry

        def apply(k, carry):
            at = pl.ds(pl.multiple_of(k * HD, HD), HD)
            state = state_ref[:, at].astype(F32) * inverse_ref[...]
            normed_ref[:, at] = (state * scale_ref[:, at] + shift_ref[:, at]).astype(BF16)
            return carry

        lax.fori_loop(0, rows // block_rows, measure, 0)
        lax.fori_loop(0, width // HD, apply, 0)
        normed_copy.start()

    for part in range(2):

        @pl.when(step == part)
        def _():
            for copy in weights_of(part):
                copy.wait()

    block = jnp.where(step < 2, 0, lax.rem(step - 2 + blocks - 1, blocks - 1) + 1)
    at = pl.ds(pl.multiple_of(block * cols, HD), cols)

    def keys():
        product = jnp.dot(normed_ref[...], w_ref[0, :, at], preferred_element_type=F32)
        return head_normalized(product, gain_ref[1:2])

    def values():
        product = jnp.dot(normed_ref[...], w_ref[1, :, at], preferred_element_type=F32)
        return product.astype(BF16)

    @pl.when(step == 0)
    def _():
        first_ref[0] = keys()

    @pl.when(step == 1)
    def _():
        first_ref[0] = values()

    @pl.when(jnp.logical_and(step > 1, step < 1 + blocks))
    def _():
        second_ref[0] = keys()

    @pl.when(step >= 1 + blocks)
    def _():
        second_ref[0] = values()

    @pl.when(step == pl.num_programs(0) - 1)
    def _():
        state_copy.wait()
        normed_copy.wait()


def project_keys_values(info, scale1, shift, gains, qkv_weight, z, noise, noise_pieces):
    rows, width = z.shape
    head_cols = qkv_weight.shape[2]
    cols = tile_cols(head_cols)
    half = len(noise_pieces)
    blocks = head_cols // cols

    def second_block(j, i):
        j = jnp.maximum(j - 2, 0)
        return j // (blocks - 1), 0, j % (blocks - 1)

    return pl.pallas_call(
        functools.partial(key_value_kernel, half=half),
        grid_spec=pltpu.PrefetchScalarGridSpec(
            num_scalar_prefetch=1,
            grid=(2 * blocks,),
            in_specs=[
                pl.BlockSpec((1, width), lambda j, i: (0, 0)),
                pl.BlockSpec((1, width), lambda j, i: (0, 0)),
                pl.BlockSpec((2, HD), lambda j, i: (0, 0)),
            ]
            + [ANY] * (3 + half),
            out_specs=[
                pl.BlockSpec((1, rows, cols), lambda j, i: (jnp.minimum(j, 1), 0, 0)),
                pl.BlockSpec((1, rows, cols), second_block),
                ANY,
                ANY,
            ],
            scratch_shapes=[
                pltpu.VMEM((rows, width), BF16),
                pltpu.VMEM((rows, width), BF16),
                pltpu.VMEM((rows, HD), F32),
                pltpu.VMEM((2, width, head_cols), BF16),
                pltpu.SemaphoreType.DMA((1,)),
                pltpu.SemaphoreType.DMA((2,)),
                pltpu.SemaphoreType.DMA((2, 4)),
            ],
        ),
        out_shape=[
            jax.ShapeDtypeStruct((2, rows, cols), BF16),
            jax.ShapeDtypeStruct((2, rows, head_cols - cols), BF16),
            jax.ShapeDtypeStruct((rows, width), BF16),
            pltpu.HBM((rows, width), BF16),
        ],
        compiler_params=compiler_params(32),
        cost_estimate=cost(
            4 * rows * width * head_cols,
            6 * rows * width + 4 * rows * head_cols + 4 * width * head_cols,
        ),
        name="norm_keys_values",
    )(
        info,
        scale1,
        shift,
        gains,
        *[in_hbm(a) for a in (qkv_weight, z)],
        noise,
        *noise_pieces,
    )


def attend(query, key):
    return lax.dot_general(query, key, (((1,), (1,)), ((), ())), preferred_element_type=F32)


def weigh(scores, top, values):
    weights = jnp.exp2(scores - top).astype(BF16)
    extended = jnp.concatenate([values, jnp.ones_like(values)], axis=1)
    total = jnp.dot(weights, extended, preferred_element_type=F32)
    return total[:, :HD], total[:, HD:]


def attention_tiles(query, key, finish):
    rows, cols = query.shape
    tile = math.gcd(rows, 256)
    waiting = None
    for h in range(cols // HD):
        at = slice(h * HD, (h + 1) * HD)
        for r in range(rows // tile):
            row = slice(r * tile, (r + 1) * tile)
            scores = attend(query[row, at], key[:, at])
            if waiting is not None:
                finish(*waiting)
            waiting = (scores, row, at)
    finish(*waiting)


def own_kernel(
    gain_ref, normed_ref, first_ref, second_ref, w_any,
    query_ref, acc_ref, top_ref, total_ref, w_ref, w_sems,
):
    step = pl.program_id(0)
    cols = query_ref.shape[1]

    @pl.when(step == 0)
    def _():
        for copy in weight_copies(w_any, 0, w_ref, w_sems):
            copy.start()
        for copy in weight_copies(w_any, 0, w_ref, w_sems):
            copy.wait()

    inside = pl.ds(pl.multiple_of(step * cols, HD), cols)
    product = jnp.dot(normed_ref[...], w_ref[:, inside], preferred_element_type=F32)
    query = head_normalized(product, gain_ref[0:1])
    query_ref[...] = query
    keys = jnp.where(step == 0, first_ref[0], second_ref[0])
    values = jnp.where(step == 0, first_ref[1], second_ref[1])

    def finish(scores, row, at):
        top = over_lanes(scores, jnp.maximum, jnp.max)
        acc, total = weigh(scores, top, values[:, at])
        acc_ref[row, at] = acc
        total_ref[row, at] = total
        top_ref[row, at] = jnp.broadcast_to(top, acc.shape)

    attention_tiles(query, keys, finish)


def own_attention(gains, normed, qkv_weight, first, second):
    rows, width = normed.shape
    head_cols = qkv_weight.shape[2]
    cols = tile_cols(head_cols)
    by_heads = pl.BlockSpec((rows, cols), lambda j: (0, j))
    return pl.pallas_call(
        own_kernel,
        grid=(head_cols // cols,),
        in_specs=[
            pl.BlockSpec((2, HD), lambda j: (0, 0)),
            pl.BlockSpec((rows, width), lambda j: (0, 0)),
            pl.BlockSpec((2, rows, cols), lambda j: (0, 0, 0)),
            pl.BlockSpec((2, rows, cols), lambda j: (0, 0, jnp.maximum(j - 1, 0))),
            ANY,
        ],
        out_specs=[by_heads] * 4,
        scratch_shapes=[
            pltpu.VMEM((width, head_cols), BF16),
            pltpu.SemaphoreType.DMA((4,)),
        ],
        out_shape=[jax.ShapeDtypeStruct((rows, head_cols), BF16)]
        + [jax.ShapeDtypeStruct((rows, head_cols), F32)] * 3,
        compiler_params=compiler_params(32),
        cost_estimate=cost(
            2 * rows * width * head_cols + 8 * rows * rows * head_cols,
            2 * rows * width + 18 * rows * head_cols + 2 * width * head_cols,
            rows * rows * head_cols // HD,
        ),
        name="queries_own_frame",
    )(gains, normed, first, second, in_hbm(qkv_weight))


def earlier_kernel(info_ref, query_ref, acc_ref, top_ref, total_ref, kv_ref, out_ref):
    @pl.when(info_ref[0] != 0)
    def _():
        out_ref[...] = (acc_ref[...] / total_ref[...]).astype(BF16)

    @pl.when(info_ref[0] == 0)
    def _():
        def finish(scores, row, at):
            old_top = top_ref[row, at][:, :1]
            top = jnp.maximum(over_lanes(scores, jnp.maximum, jnp.max), old_top)
            acc, total = weigh(scores, top, kv_ref[1, :, at])
            kept = jnp.exp2(old_top - top)
            acc = acc + acc_ref[row, at] * kept
            total = total + total_ref[row, at] * kept
            out_ref[row, at] = (acc / total).astype(BF16)

        attention_tiles(query_ref[...], kv_ref[0], finish)


def earlier_attention(info, query, acc, top, total, kv, first_block):
    rows = query.shape[0]
    group = kv.shape[2]
    cols = tile_cols(query.shape[1])
    by_heads = pl.BlockSpec((rows, cols), lambda j, i: (0, first_block + j))
    return pl.pallas_call(
        earlier_kernel,
        grid_spec=pltpu.PrefetchScalarGridSpec(
            num_scalar_prefetch=1,
            grid=(group // cols,),
            in_specs=[by_heads] * 4 + [pl.BlockSpec((2, rows, cols), lambda j, i: (0, 0, j))],
            out_specs=pl.BlockSpec((rows, cols), lambda j, i: (0, j)),
        ),
        out_shape=jax.ShapeDtypeStruct((rows, group), BF16),
        compiler_params=compiler_params(24),
        cost_estimate=cost(8 * rows * rows * group, 20 * rows * group, rows * rows * group // HD),
        name="earlier_frame",
    )(info, query, acc, top, total, kv)


def output_kernel(*refs, part_places, whole_weights, half_blocks, last):
    parity_ref = refs[0]
    at = 1
    acc_in = resid_ref = gate_ref = None
    if last:
        acc_in, resid_ref, gate_ref = refs[1:4]
        at = 4
    pieces = []
    for places in part_places:
        pieces.append(refs[at : at + len(places)])
        at += len(places)
    size = len(part_places)
    wholes = refs[at : at + whole_weights]
    at += whole_weights
    halves = refs[at : at + 2 * (size - whole_weights)]
    at += 2 * (size - whole_weights)
    out_ref, held_ref, w_ref, held_sems, w_sems = refs[at:]
    step = pl.program_id(0)
    cols = out_ref.shape[1]
    half_width = w_ref.shape[3]

    def weight_copy(half, k):
        if k < whole_weights:
            column = (parity_ref[0] ^ half) * half_width
            source = wholes[k].at[:, pl.ds(pl.multiple_of(column, HD), half_width)]
        else:
            source = halves[half * (size - whole_weights) + k - whole_weights]
        return pltpu.make_async_copy(source, w_ref.at[half, k], w_sems.at[half, k])

    def held_copies(k):
        for number, (part, place) in enumerate(zip(pieces[k], part_places[k])):
            rows, cols = (pl.ds(first, count) for first, count in zip(place, part.shape))
            yield pltpu.make_async_copy(
                part, held_ref.at[k, rows, cols], held_sems.at[k, number]
            )

    @pl.when(step == 0)
    def _():
        for k in range(size):
            for copy in held_copies(k):
                copy.start()
        for half in range(2):
            for k in range(size):
                weight_copy(half, k).start()
        for k in range(size):
            for copy in held_copies(k):
                copy.wait()

    for half in range(2):

        @pl.when(step == half * half_blocks)
        def _():
            for k in range(size):
                weight_copy(half, k).wait()

    half = step // half_blocks
    tile = tile_cols(cols)
    for t in range(cols // tile):
        at = slice(t * tile, (t + 1) * tile)
        first = lax.rem(step, half_blocks) * cols + t * tile
        inside = pl.ds(pl.multiple_of(first, HD), tile)
        update = acc_in[:, at].astype(F32) if last else None
        for k in range(size):
            term = jnp.dot(held_ref[k], w_ref[half, k, :, inside], preferred_element_type=F32)
            update = term if update is None else update + term
        if last:
            update = resid_ref[:, at].astype(F32) + gate_ref[:, at] * update
        out_ref[:, at] = update.astype(BF16)


def output_projection(parity, pieces, wholes, mine, theirs, finish=None):
    head_cols, half_width = mine[0].shape
    width = 2 * half_width
    rows = max(row + part.shape[0] for part, row, _ in pieces[0])
    size = len(pieces)
    cols = half_width // 2 if half_width % 512 == 0 else half_width
    half_blocks = half_width // cols
    parts = max(len(p) for p in pieces)
    flat = [part for group in pieces for part, _, _ in group]
    weights = [in_hbm(array) for array in [*wholes, *mine, *theirs]]
    last = finish is not None

    def column(j, parity):
        return 0, ((j // half_blocks) ^ parity[0]) * half_blocks + j % half_blocks

    block = pl.BlockSpec((rows, cols), column)
    return pl.pallas_call(
        functools.partial(
            output_kernel,
            part_places=tuple(tuple((row, col) for _, row, col in p) for p in pieces),
            whole_weights=len(wholes),
            half_blocks=half_blocks,
            last=last,
        ),
        grid_spec=pltpu.PrefetchScalarGridSpec(
            num_scalar_prefetch=1,
            grid=(2 * half_blocks,),
            in_specs=([block, block, pl.BlockSpec((1, cols), column)] if last else [])
            + [ANY] * (len(flat) + len(weights)),
            out_specs=block,
            scratch_shapes=[
                pltpu.VMEM((size, rows, head_cols), BF16),
                pltpu.VMEM((2, size, head_cols, half_width), BF16),
                pltpu.SemaphoreType.DMA((size, parts)),
                pltpu.SemaphoreType.DMA((2, size)),
            ],
        ),
        out_shape=(pltpu.HBM if last else jax.ShapeDtypeStruct)((rows, width), BF16),
        compiler_params=compiler_params(24 if last else 32),
        cost_estimate=cost(
            2 * rows * width * head_cols * size,
            (6 if last else 2) * rows * width + 2 * head_cols * width * size,
        ),
        name="projection_end" if last else "projection_start",
    )(parity, *(finish if last else ()), *flat, *weights)


def send(block, move, queue_size, tensor_size, frames=None):
    pairs = []
    for q in range(queue_size) if frames is None else frames:
        for t in range(tensor_size):
            to_q, to_t = move(q, t)
            pairs.append((q * tensor_size + t, to_q * tensor_size + to_t))
    return lax.ppermute(block, AXES, pairs)


def one_hop(block, queue_size, tensor_size, frames=None):
    half = tensor_size // 2
    args = (queue_size, tensor_size, frames)
    near = send(block, lambda q, t: (q, t ^ 1), *args)
    return [near] + [send(block, away(j, half), *args) for j in range(1, half)]


def two_hops(blocks, queue_size, tensor_size, frames=None):
    half = tensor_size // 2
    args = (queue_size, tensor_size, frames)
    near, far = blocks[0], blocks[1:]
    rows = near.shape[0] // 2
    corners = []
    for j in range(1, half):
        top = send(near[:rows], away(j, half), *args)
        bottom = send(far[j - 1][rows:], lambda q, t: (q, t ^ 1), *args)
        corners.append([top, bottom])
    return corners


def away(j, half):
    return lambda q, t: (q, (t // 2 - j) % half * 2 + t % 2)


def body(
    latents, levels, mod_table, step_size, qkv_weight, q_gain, k_gain, out_weight, fresh_noise
):
    queue_size = lax.axis_size("queue")
    tensor_size = lax.axis_size("tensor")
    rows, width = latents.shape[1:]
    mesh_sizes = (queue_size, tensor_size)
    queue_index = lax.axis_index("queue")
    tensor_index = lax.axis_index("tensor")
    parity = (queue_index % 2).astype(jnp.int32)[None]

    def ring(block, frames=None):
        return send(block, lambda q, t: ((q + 1) % queue_size, t), *mesh_sizes, frames)

    def sibling(block):
        return send(block, lambda q, t: (q ^ 1, t), *mesh_sizes)

    def gather_noise(noise, at_once):
        args = (*mesh_sizes, [0])
        half = tensor_size // 2
        near = send(noise, lambda q, t: (q, t ^ 1), *args)
        pairs = []
        for j in range(1, half):
            if at_once:
                straight = send(noise, away(j, half), *args)
                across = send(noise, lambda q, t: away(j, half)(q, t ^ 1), *args)
                pairs.append(jnp.concatenate([straight, across], axis=0))
            else:
                pair = jnp.concatenate([noise, near], axis=0)
                pairs.append(send(pair, away(j, half), *args))
        return [near, *pairs]

    to_next = range(queue_size - 1)
    frame = ring(latents[0], to_next)
    noise = fresh_noise[0]
    noise_pieces = gather_noise(noise, True)
    half_weight = lax.dynamic_slice(
        out_weight, (0, parity[0] * (width // 2)), (out_weight.shape[0], width // 2)
    )
    mine = one_hop(half_weight, *mesh_sizes)

    def modulation(level):
        row = lax.dynamic_slice(mod_table, (level, 0), (1, 3 * width)).astype(F32)
        rate = lax.dynamic_slice(step_size, (level,), (1,))[:, None]
        return row[:, :width], 1.0 + row[:, width : 2 * width], rate * row[:, 2 * width :]

    shift, scale1, own_gate = modulation(levels[0])
    info = jnp.stack([queue_index == 0, tensor_index // 2, tensor_index % 2])
    info = info.astype(jnp.int32)
    gains = jnp.stack([q_gain * SCORE_SCALE, k_gain])

    for step_index in range(STEPS):
        final = step_index == STEPS - 1
        *made, normed, state = project_keys_values(
            info, scale1, shift, gains, qkv_weight, frame, noise, noise_pieces
        )
        if not final:
            state, mine, sent_levels = lax.optimization_barrier((state, mine, levels))
            arriving_level = ring(sent_levels, to_next)
        earlier = [ring(group, to_next) for group in made]
        query, *own = own_attention(gains, normed, qkv_weight, *made)
        if not final:
            mine_corners = two_hops(mine, *mesh_sizes)
            earlier, mine_corners = lax.optimization_barrier((earlier, mine_corners))
        attended, columns, block = [], [], 0
        for group in earlier:
            attended.append(earlier_attention(info, query, *own, group, block))
            columns.append(block * made[0].shape[2])
            block += group.shape[2] // made[0].shape[2]
        targets = range(queue_size) if final else range(1, queue_size)
        resid, gate = state, own_gate
        if not final:
            attended, mine, mine_corners, arriving_level = lax.optimization_barrier(
                (attended, mine, mine_corners, arriving_level)
            )
            mine_corners = [jnp.concatenate(parts, axis=0) for parts in mine_corners]
            theirs = [sibling(block) for block in mine]
            theirs_corners = [sibling(block) for block in mine_corners]
            attended = [ring(block, to_next) for block in attended]
            sent_state, attended = lax.optimization_barrier((state, attended))
            resid = ring(sent_state, to_next)
            gate = modulation(arriving_level[0])[2]
            attended, theirs, theirs_corners = lax.optimization_barrier(
                (attended, theirs, theirs_corners)
            )
        near = [one_hop(block, *mesh_sizes, targets) for block in attended]
        if not final:
            near, noise = lax.optimization_barrier((near, fresh_noise[step_index + 1]))
            noise_pieces = gather_noise(noise, False)
        beyond = [two_hops(blocks, *mesh_sizes, targets) for blocks in near]
        direct = [[(block, 0, col) for block, col in zip(attended, columns)]]
        direct += [[(block, 0, col) for block, col in zip(p, columns)] for p in zip(*near)]
        corners = [
            [(half, h * (rows // 2), col) for parts, col in zip(p, columns)
             for h, half in enumerate(parts)]
            for p in zip(*beyond)
        ]
        begun = output_projection(parity, direct, [out_weight], mine, theirs)
        frame = output_projection(
            parity, corners, [], mine_corners, theirs_corners, (begun, resid, gate)
        )
    return frame[None]


def solution(mesh):
    return jax.shard_map(
        body,
        mesh=mesh,
        in_specs=(
            P("queue", None, None),
            P("queue"),
            P(),
            P(),
            P(None, None, "tensor"),
            P(),
            P(),
            P("tensor", None),
            P(None, "tensor", None),
        ),
        out_specs=P("queue", None, None),
        check_vma=False,
    )
```

```python
import functools
import math

import jax
import jax.numpy as jnp
from jax import lax
from jax.experimental import pallas as pl
from jax.experimental.pallas import tpu as pltpu
from jax.sharding import PartitionSpec as P

HD = 128
STEPS = 2
CHUNKS = 2
EPS = 1e-6
AXES = ("queue", "tensor")
F32 = jnp.float32
BF16 = jnp.bfloat16
SCORE_SCALE = math.log2(math.e) / math.sqrt(HD)
ANY = pl.BlockSpec(memory_space=pl.ANY)


def compiler_params(mib):
    return pltpu.CompilerParams(vmem_limit_bytes=mib * 2**20)


def in_hbm(array):
    return pltpu.with_memory_space_constraint(array, pltpu.HBM)


def cost(flops, nbytes, transcendentals=0, share=1000):
    return pl.CostEstimate(
        flops=int(flops) // share,
        bytes_accessed=int(nbytes) // share,
        transcendentals=int(transcendentals) // share,
    )


def head_normalized(values, gain):
    heads = []
    for h in range(values.shape[1] // HD):
        head = values[:, h * HD : (h + 1) * HD]
        mean = jnp.mean(head * head, axis=-1, keepdims=True)
        heads.append((head * lax.rsqrt(mean + EPS) * gain).astype(BF16))
    return heads[0] if len(heads) == 1 else jnp.concatenate(heads, axis=1)


def over_lanes(values, fold, reduce):
    parts = [values[:, i : i + HD] for i in range(0, values.shape[1], HD)]
    return reduce(functools.reduce(fold, parts), axis=-1, keepdims=True)


def tile_cols(head_cols):
    return 256 if head_cols % 256 == 0 else HD


def weight_copies(w_any, part, w_ref, w_sems):
    splits = w_sems.shape[0]
    split_rows = w_ref.shape[0] // splits
    for i in range(splits):
        at = pl.ds(i * split_rows, split_rows)
        yield pltpu.make_async_copy(w_any.at[part, at], w_ref.at[at], w_sems.at[i])


def key_value_kernel(*refs, half):
    info_ref, scale_ref, shift_ref, gain_ref, w_any, z_any, noise_any, near_any = refs[:8]
    pair_refs = refs[8 : 7 + half]
    key_ref, value_ref, normed_any, state_any = refs[7 + half : 11 + half]
    state_ref, normed_ref, inverse_ref, w_ref, sem, out_sems, w_sems = refs[11 + half :]
    step = pl.program_id(0)
    rows, width = state_ref.shape
    piece_rows = noise_any.shape[0]

    def weights_of(part):
        return weight_copies(w_any, part + 1, w_ref.at[part], w_sems.at[part])

    def start_weights():
        for part in range(2):
            for weight_copy in weights_of(part):
                weight_copy.start()

    def piece_at(j, f):
        if j > 0:
            return pair_refs[j - 1], f * piece_rows
        return (noise_any, near_any)[f], 0

    cols = key_ref.shape[1]
    blocks = pl.num_programs(0) // 2
    state_copy = pltpu.make_async_copy(state_ref, state_any, out_sems.at[0])
    normed_copy = pltpu.make_async_copy(normed_ref, normed_any, out_sems.at[1])

    @pl.when(step == 0)
    def _():
        @pl.when(info_ref[0] == 0)
        def _():
            copy = pltpu.make_async_copy(z_any, state_ref, sem.at[0])
            copy.start()
            copy.wait()
            start_weights()

        @pl.when(info_ref[0] != 0)
        def _():
            start_weights()
            for block in range(2 * half):
                high, low = block // 2, block % 2
                steps = lax.rem(high + half - info_ref[1], half)
                other = jnp.abs(low - info_ref[2])
                for j in range(half):
                    for f in range(2):
                        source, row = piece_at(j, f)

                        @pl.when(jnp.logical_and(steps == j, other == f))
                        def _():
                            copy = pltpu.make_async_copy(
                                source.at[pl.ds(row, piece_rows)],
                                state_ref.at[pl.ds(block * piece_rows, piece_rows)],
                                sem.at[0],
                            )
                            copy.start()
                            copy.wait()

        state_copy.start()

        block_rows = math.gcd(rows, 64)

        def measure(i, carry):
            at = pl.ds(pl.multiple_of(i * block_rows, block_rows), block_rows)
            squares = None
            for k in range(0, width, HD):
                part = state_ref[at, k : k + HD].astype(F32)
                squares = part * part if squares is None else squares + part * part
            mean = jnp.sum(squares, axis=-1, keepdims=True) * (1.0 / width)
            inverse_ref[at, :] = jnp.broadcast_to(lax.rsqrt(mean + EPS), (block_rows, HD))
            return carry

        def apply(k, carry):
            at = pl.ds(pl.multiple_of(k * HD, HD), HD)
            state = state_ref[:, at].astype(F32) * inverse_ref[...]
            normed_ref[:, at] = (state * scale_ref[:, at] + shift_ref[:, at]).astype(BF16)
            return carry

        lax.fori_loop(0, rows // block_rows, measure, 0)
        lax.fori_loop(0, width // HD, apply, 0)
        normed_copy.start()

    for part in range(2):

        @pl.when(step == part * blocks)
        def _():
            for copy in weights_of(part):
                copy.wait()

    at = pl.ds(pl.multiple_of(lax.rem(step, blocks) * cols, HD), cols)

    @pl.when(step < blocks)
    def _():
        product = jnp.dot(normed_ref[...], w_ref[0, :, at], preferred_element_type=F32)
        key_ref[...] = head_normalized(product, gain_ref[1:2])

    @pl.when(step >= blocks)
    def _():
        product = jnp.dot(normed_ref[...], w_ref[1, :, at], preferred_element_type=F32)
        value_ref[...] = product.astype(BF16)

    @pl.when(step == pl.num_programs(0) - 1)
    def _():
        state_copy.wait()
        normed_copy.wait()


def project_keys_values(info, scale1, shift, gains, qkv_weight, z, noise, noise_pieces):
    rows, width = z.shape
    head_cols = qkv_weight.shape[2]
    cols = tile_cols(head_cols)
    half = len(noise_pieces)
    blocks = head_cols // cols
    return pl.pallas_call(
        functools.partial(key_value_kernel, half=half),
        grid_spec=pltpu.PrefetchScalarGridSpec(
            num_scalar_prefetch=1,
            grid=(2 * blocks,),
            in_specs=[
                pl.BlockSpec((1, width), lambda j, i: (0, 0)),
                pl.BlockSpec((1, width), lambda j, i: (0, 0)),
                pl.BlockSpec((2, HD), lambda j, i: (0, 0)),
            ]
            + [ANY] * (3 + half),
            out_specs=[
                pl.BlockSpec((rows, cols), lambda j, i: (0, jnp.minimum(j, blocks - 1))),
                pl.BlockSpec((rows, cols), lambda j, i: (0, jnp.maximum(j - blocks, 0))),
                ANY,
                ANY,
            ],
            scratch_shapes=[
                pltpu.VMEM((rows, width), BF16),
                pltpu.VMEM((rows, width), BF16),
                pltpu.VMEM((rows, HD), F32),
                pltpu.VMEM((2, width, head_cols), BF16),
                pltpu.SemaphoreType.DMA((1,)),
                pltpu.SemaphoreType.DMA((2,)),
                pltpu.SemaphoreType.DMA((2, 4)),
            ],
        ),
        out_shape=[
            jax.ShapeDtypeStruct((rows, head_cols), BF16),
            jax.ShapeDtypeStruct((rows, head_cols), BF16),
            jax.ShapeDtypeStruct((rows, width), BF16),
            pltpu.HBM((rows, width), BF16),
        ],
        compiler_params=compiler_params(32),
        cost_estimate=cost(
            4 * rows * width * head_cols,
            6 * rows * width + 4 * rows * head_cols + 4 * width * head_cols,
        ),
        name="norm_keys_values",
    )(
        info,
        scale1,
        shift,
        gains,
        *[in_hbm(a) for a in (qkv_weight, z)],
        noise,
        *noise_pieces,
    )


def attend(query, key):
    return lax.dot_general(query, key, (((1,), (1,)), ((), ())), preferred_element_type=F32)


def weigh(scores, top, values):
    weights = jnp.exp2(scores - top).astype(BF16)
    extended = jnp.concatenate([values, jnp.ones_like(values)], axis=1)
    total = jnp.dot(weights, extended, preferred_element_type=F32)
    return total[:, :HD], total[:, HD:]


def attention_tiles(query, key, finish):
    rows, cols = query.shape
    tile = math.gcd(rows, 256)
    waiting = None
    for h in range(cols // HD):
        at = slice(h * HD, (h + 1) * HD)
        for r in range(rows // tile):
            row = slice(r * tile, (r + 1) * tile)
            scores = attend(query[row, at], key[:, at])
            if waiting is not None:
                finish(*waiting)
            waiting = (scores, row, at)
    finish(*waiting)


def own_kernel(
    gain_ref, normed_ref, key_ref, value_ref, w_any,
    query_ref, acc_ref, top_ref, total_ref, w_ref, w_sems,
):
    step = pl.program_id(0)
    cols = query_ref.shape[1]

    @pl.when(step == 0)
    def _():
        for copy in weight_copies(w_any, 0, w_ref, w_sems):
            copy.start()
        for copy in weight_copies(w_any, 0, w_ref, w_sems):
            copy.wait()

    inside = pl.ds(pl.multiple_of(step * cols, HD), cols)
    product = jnp.dot(normed_ref[...], w_ref[:, inside], preferred_element_type=F32)
    query = head_normalized(product, gain_ref[0:1])
    query_ref[...] = query

    def finish(scores, row, at):
        top = over_lanes(scores, jnp.maximum, jnp.max)
        acc, total = weigh(scores, top, value_ref[:, at])
        acc_ref[row, at] = acc
        total_ref[row, at] = total
        top_ref[row, at] = jnp.broadcast_to(top, acc.shape)

    attention_tiles(query, key_ref, finish)


def own_attention(gains, normed, qkv_weight, key, value):
    rows, width = normed.shape
    head_cols = qkv_weight.shape[2]
    cols = tile_cols(head_cols)
    by_heads = pl.BlockSpec((rows, cols), lambda j: (0, j))
    return pl.pallas_call(
        own_kernel,
        grid=(head_cols // cols,),
        in_specs=[
            pl.BlockSpec((2, HD), lambda j: (0, 0)),
            pl.BlockSpec((rows, width), lambda j: (0, 0)),
            by_heads,
            by_heads,
            ANY,
        ],
        out_specs=[by_heads] * 4,
        scratch_shapes=[
            pltpu.VMEM((width, head_cols), BF16),
            pltpu.SemaphoreType.DMA((4,)),
        ],
        out_shape=[jax.ShapeDtypeStruct((rows, head_cols), BF16)]
        + [jax.ShapeDtypeStruct((rows, head_cols), F32)] * 3,
        compiler_params=compiler_params(32),
        cost_estimate=cost(
            2 * rows * width * head_cols + 8 * rows * rows * head_cols,
            2 * rows * width + 18 * rows * head_cols + 2 * width * head_cols,
            rows * rows * head_cols // HD,
        ),
        name="queries_own_frame",
    )(gains, normed, key, value, in_hbm(qkv_weight))


def earlier_kernel(*refs, chunks):
    info_ref, query_ref, acc_ref, top_ref, total_ref, key_ref, value_ref = refs[:7]
    out_refs = refs[7:]
    rows = query_ref.shape[0] // chunks

    def store(row, at, result):
        for c, out_ref in enumerate(out_refs):
            first, end = max(row.start, c * rows), min(row.stop, (c + 1) * rows)
            if first < end:
                inside = slice(first - c * rows, end - c * rows)
                out_ref[inside, at] = result[first - row.start : end - row.start]

    @pl.when(info_ref[0] != 0)
    def _():
        every = slice(0, query_ref.shape[0])
        store(every, slice(None), (acc_ref[...] / total_ref[...]).astype(BF16))

    @pl.when(info_ref[0] == 0)
    def _():
        def finish(scores, row, at):
            old_top = top_ref[row, at][:, :1]
            top = jnp.maximum(over_lanes(scores, jnp.maximum, jnp.max), old_top)
            acc, total = weigh(scores, top, value_ref[:, at])
            kept = jnp.exp2(old_top - top)
            acc = acc + acc_ref[row, at] * kept
            total = total + total_ref[row, at] * kept
            store(row, at, (acc / total).astype(BF16))

        attention_tiles(query_ref[...], key_ref, finish)


def earlier_attention(info, query, acc, top, total, key, value, chunks):
    rows, head_cols = query.shape
    cols = tile_cols(head_cols)
    return pl.pallas_call(
        functools.partial(earlier_kernel, chunks=chunks),
        grid_spec=pltpu.PrefetchScalarGridSpec(
            num_scalar_prefetch=1,
            grid=(head_cols // cols,),
            in_specs=[pl.BlockSpec((rows, cols), lambda j, i: (0, j))] * 6,
            out_specs=[pl.BlockSpec((rows // chunks, cols), lambda j, i: (0, j))] * chunks,
        ),
        out_shape=[jax.ShapeDtypeStruct((rows // chunks, head_cols), BF16)] * chunks,
        compiler_params=compiler_params(24),
        cost_estimate=cost(
            8 * rows * rows * head_cols,
            22 * rows * head_cols,
            rows * rows * head_cols // HD,
        ),
        name="earlier_frame",
    )(info, query, acc, top, total, key, value)


def output_kernel(*refs, part_counts, whole_weights, half_blocks, last):
    parity_ref = refs[0]
    at = 1
    acc_in = resid_ref = gate_ref = None
    if last:
        acc_in, resid_ref, gate_ref = refs[1:4]
        at = 4
    pieces = []
    for count in part_counts:
        pieces.append(refs[at : at + count])
        at += count
    size = len(part_counts)
    wholes = refs[at : at + whole_weights]
    at += whole_weights
    halves = refs[at : at + 2 * (size - whole_weights)]
    at += 2 * (size - whole_weights)
    out_ref, held_ref, w_ref, held_sems, w_sems = refs[at:]
    step = pl.program_id(0)
    cols = out_ref.shape[1]
    half_width = w_ref.shape[3]

    def weight_copy(half, k):
        if k < whole_weights:
            column = (parity_ref[0] ^ half) * half_width
            source = wholes[k].at[:, pl.ds(pl.multiple_of(column, HD), half_width)]
        else:
            source = halves[half * (size - whole_weights) + k - whole_weights]
        return pltpu.make_async_copy(source, w_ref.at[half, k], w_sems.at[half, k])

    def held_copies(k):
        row = 0
        for number, part in enumerate(pieces[k]):
            count = part.shape[0]
            yield pltpu.make_async_copy(
                part, held_ref.at[k, pl.ds(row, count)], held_sems.at[k, number]
            )
            row += count

    @pl.when(step == 0)
    def _():
        for k in range(size):
            for copy in held_copies(k):
                copy.start()
        for half in range(2):
            for k in range(size):
                weight_copy(half, k).start()
        for k in range(size):
            for copy in held_copies(k):
                copy.wait()

    for half in range(2):

        @pl.when(step == half * half_blocks)
        def _():
            for k in range(size):
                weight_copy(half, k).wait()

    half = step // half_blocks
    tile = tile_cols(cols)
    for t in range(cols // tile):
        at = slice(t * tile, (t + 1) * tile)
        first = lax.rem(step, half_blocks) * cols + t * tile
        inside = pl.ds(pl.multiple_of(first, HD), tile)
        update = acc_in[:, at].astype(F32) if last else None
        for k in range(size):
            term = jnp.dot(held_ref[k], w_ref[half, k, :, inside], preferred_element_type=F32)
            update = term if update is None else update + term
        if last:
            update = resid_ref[:, at].astype(F32) + gate_ref[:, at] * update
        out_ref[:, at] = update.astype(BF16)


def output_projection(parity, pieces, wholes, mine, theirs, finish=None):
    head_cols, half_width = mine[0].shape
    rows = sum(part.shape[0] for part in pieces[0])
    width = 2 * half_width
    size = len(pieces)
    cols = half_width // 2 if half_width % 512 == 0 else half_width
    half_blocks = half_width // cols
    parts = max(len(p) for p in pieces)
    flat = [part for group in pieces for part in group]
    weights = [in_hbm(array) for array in [*wholes, *mine, *theirs]]
    last = finish is not None

    def column(j, parity):
        return 0, ((j // half_blocks) ^ parity[0]) * half_blocks + j % half_blocks

    block = pl.BlockSpec((rows, cols), column)
    return pl.pallas_call(
        functools.partial(
            output_kernel,
            part_counts=tuple(len(p) for p in pieces),
            whole_weights=len(wholes),
            half_blocks=half_blocks,
            last=last,
        ),
        grid_spec=pltpu.PrefetchScalarGridSpec(
            num_scalar_prefetch=1,
            grid=(2 * half_blocks,),
            in_specs=([block, block, pl.BlockSpec((1, cols), column)] if last else [])
            + [ANY] * (len(flat) + len(weights)),
            out_specs=block,
            scratch_shapes=[
                pltpu.VMEM((size, rows, head_cols), BF16),
                pltpu.VMEM((2, size, head_cols, half_width), BF16),
                pltpu.SemaphoreType.DMA((size, parts)),
                pltpu.SemaphoreType.DMA((2, size)),
            ],
        ),
        out_shape=(pltpu.HBM if last else jax.ShapeDtypeStruct)((rows, width), BF16),
        compiler_params=compiler_params(24 if last else 32),
        cost_estimate=cost(
            2 * rows * width * head_cols * size,
            (6 if last else 2) * rows * width + 2 * head_cols * width * size,
        ),
        name="projection_end" if last else "projection_start",
    )(parity, *(finish if last else ()), *flat, *weights)


def send(block, move, queue_size, tensor_size, frames=None):
    pairs = []
    for q in range(queue_size) if frames is None else frames:
        for t in range(tensor_size):
            to_q, to_t = move(q, t)
            pairs.append((q * tensor_size + t, to_q * tensor_size + to_t))
    return lax.ppermute(block, AXES, pairs)


def one_hop(block, queue_size, tensor_size, frames=None):
    half = tensor_size // 2
    args = (queue_size, tensor_size, frames)
    near = send(block, lambda q, t: (q, t ^ 1), *args)
    return [near] + [send(block, away(j, half), *args) for j in range(1, half)]


def two_hops(blocks, queue_size, tensor_size, frames=None):
    half = tensor_size // 2
    args = (queue_size, tensor_size, frames)
    near, far = blocks[0], blocks[1:]
    rows = near.shape[0] // 2
    corners = []
    for j in range(1, half):
        top = send(near[:rows], away(j, half), *args)
        bottom = send(far[j - 1][rows:], lambda q, t: (q, t ^ 1), *args)
        corners.append([top, bottom])
    return corners


def away(j, half):
    return lambda q, t: (q, (t // 2 - j) % half * 2 + t % 2)


def body(
    latents, levels, mod_table, step_size, qkv_weight, q_gain, k_gain, out_weight, fresh_noise
):
    queue_size = lax.axis_size("queue")
    tensor_size = lax.axis_size("tensor")
    rows, width = latents.shape[1:]
    mesh_sizes = (queue_size, tensor_size)
    queue_index = lax.axis_index("queue")
    tensor_index = lax.axis_index("tensor")
    parity = (queue_index % 2).astype(jnp.int32)[None]

    def ring(block, frames=None):
        return send(block, lambda q, t: ((q + 1) % queue_size, t), *mesh_sizes, frames)

    def sibling(block):
        return send(block, lambda q, t: (q ^ 1, t), *mesh_sizes)

    def gather_noise(noise):
        args = (*mesh_sizes, [0])
        half = tensor_size // 2
        near = send(noise, lambda q, t: (q, t ^ 1), *args)
        pair = jnp.concatenate([noise, near], axis=0)
        return [near, *[send(pair, away(j, half), *args) for j in range(1, half)]]

    to_next = range(queue_size - 1)
    frame = ring(latents[0], to_next)
    noise = fresh_noise[0]
    noise_pieces = gather_noise(noise)
    half_weight = lax.dynamic_slice(
        out_weight, (0, parity[0] * (width // 2)), (out_weight.shape[0], width // 2)
    )
    mine = one_hop(half_weight, *mesh_sizes)

    def modulation(level):
        row = lax.dynamic_slice(mod_table, (level, 0), (1, 3 * width)).astype(F32)
        rate = lax.dynamic_slice(step_size, (level,), (1,))[:, None]
        return row[:, :width], 1.0 + row[:, width : 2 * width], rate * row[:, 2 * width :]

    shift, scale1, own_gate = modulation(levels[0])
    info = jnp.stack([queue_index == 0, tensor_index // 2, tensor_index % 2])
    info = info.astype(jnp.int32)
    gains = jnp.stack([q_gain * SCORE_SCALE, k_gain])

    for step_index in range(STEPS):
        final = step_index == STEPS - 1
        key, value, normed, state = project_keys_values(
            info, scale1, shift, gains, qkv_weight, frame, noise, noise_pieces
        )
        if not final:
            value, mine, sent_levels = lax.optimization_barrier((value, mine, levels))
            arriving_level = ring(sent_levels, to_next)
        earlier = [ring(block, to_next) for block in (key, value)]
        query, *own = own_attention(gains, normed, qkv_weight, key, value)
        if not final:
            mine_corners = two_hops(mine, *mesh_sizes)
            earlier, mine_corners = lax.optimization_barrier((earlier, mine_corners))
        attended = earlier_attention(
            info, query, *own, *earlier, CHUNKS if final else 1
        )
        targets = range(queue_size) if final else range(1, queue_size)
        resid, gate = state, own_gate
        if not final:
            attended, mine, mine_corners, arriving_level = lax.optimization_barrier(
                (attended, mine, mine_corners, arriving_level)
            )
            mine_corners = [jnp.concatenate(parts, axis=0) for parts in mine_corners]
            theirs = [sibling(block) for block in mine]
            theirs_corners = [sibling(block) for block in mine_corners]
            attended = [ring(block, to_next) for block in attended]
            sent_state, attended = lax.optimization_barrier((state, attended))
            resid, gate = ring(sent_state, to_next), modulation(arriving_level[0])[2]
            attended, theirs, theirs_corners = lax.optimization_barrier(
                (attended, theirs, theirs_corners)
            )
        near = [one_hop(block, *mesh_sizes, targets) for block in attended]
        if not final:
            near, noise = lax.optimization_barrier((near, fresh_noise[step_index + 1]))
            noise_pieces = gather_noise(noise)
        beyond = [two_hops(blocks, *mesh_sizes, targets) for blocks in near]
        direct = [attended] + [list(parts) for parts in zip(*near)]
        corners = [[half for parts in p for half in parts] for p in zip(*beyond)]
        begun = output_projection(parity, direct, [out_weight], mine, theirs)
        frame = output_projection(
            parity, corners, [], mine_corners, theirs_corners, (begun, resid, gate)
        )
    return frame[None]


def solution(mesh):
    return jax.shard_map(
        body,
        mesh=mesh,
        in_specs=(
            P("queue", None, None),
            P("queue"),
            P(),
            P(),
            P(None, None, "tensor"),
            P(),
            P(),
            P("tensor", None),
            P(None, "tensor", None),
        ),
        out_specs=P("queue", None, None),
        check_vma=False,
    )
```
